128 devices in a mesh: curve: 8 (over x, core), seg: 16 (over y, z).
Axes of the slice: x: 4, y: 4, z: 4, core: 2. Of those that a mesh axis runs over, the one named last changes fastest.
Arguments:
- adjoint: float32 [9, 8192, 512], P(None, ('curve', 'seg')), may hold values from -6 to 6
- material: float32 [3, 8192], P(None, ('curve', 'seg')), may hold values from 0.5 to 2
- face_partner: int32 [8192, 6], P(('curve', 'seg')), may hold values from 0 to 447, as said below
- send_faces: int32 [128, 4, 16], P(('curve', 'seg')), may hold values from 0 to 383, as said below
- migration: int32 [3, 8192], P(None, ('curve', 'seg')), may hold values from 0 to 15, as said below
- children: int32 [2, 1024], P(None, ('curve', 'seg')), may hold values from -1 to 15, as said below
Outputs:
- adjoint_next: float32 [9, 8192, 512], P(None, ('curve', 'seg'))
- parent_adjoint: float32 [9, 1024, 512], P(None, ('curve', 'seg'))
The draws below stay inside these ranges and needn't reach their ends.
Inputs may be any that keep to these rules, and one draw needn't show every extreme that they name: `face_partner`: entries below 384 name a face of the same partition; the others name a slot of a side's received faces as in the reference program. Each face is the partner of exactly one face. `send_faces`: slot t of side -x or +x is the face at position (t // 4, t % 4) in (y, z), of side -y or +y at (x, z); entries are 6 l + f of this partition's elements. `migration`: the eight children of each parent lie on one partition of the owner's segment group, one per octant. Each partition keeps all children of 4 of its own parents (row 1 is then the parent) and holds the children of 4 foreign parents (row 1 is then the slot, below 2, unique per owner). At most 2 foreign parents of one owner lie on one partition, and some partition holds exactly 2 for some owner. Row 0 is the owner itself with row 1 equal to -1 for the 4 parents whose children stayed; otherwise the holder and the slot of the matching migration entry.
All inputs are finite; a program needn't handle non-finite values.
Results may differ from the reference program's by a relative error of at most 0.000052.
Values sent between devices are 32-bit elements; how exact they have to be, the bound alone decides.
No kernel may reach another device: no remote copies, remote signals or barrier semaphores. Data moves between devices by JAX's collectives and lax.ppermute only.
A program may use at most 128 MiB of HBM per device.

```python
import math
import jax
import jax.numpy as jnp
import numpy as np
from jax import lax

NP = 8
NODES = 512
FACE = 64
BXY = 4
BZ = 4
E_DEV = 64
CAP = 16
P_DEV = 8
MIG_CAP = 2
ELEMENTS = 8192
PARENTS = 1024
N_CURVE = 8
N_SEG = 16


def brick_orders(key):
    devices = ELEMENTS // E_DEV
    base_key = jax.random.fold_in(key, 11)

    def device_order(device):
        return jax.random.permutation(jax.random.fold_in(base_key, device), E_DEV).astype(jnp.int32)
    return jax.vmap(device_order)(jnp.arange(devices))


def cell_number(along_x, along_y, along_z):
    return (along_x * BXY + along_y) * BZ + along_z


def device_faces(cell_order):
    cell_ids = jnp.arange(E_DEV)
    along_x = cell_ids // (BXY * BZ)
    along_y = cell_ids // BZ % BXY
    along_z = cell_ids % BZ
    remote = 6 * E_DEV
    across_x = along_y * BZ + along_z
    across_y = along_x * BZ + along_z
    lower_x = jnp.where(along_x > 0, cell_order[cell_number(jnp.maximum(along_x - 1, 0), along_y, along_z)] * 6 + 1, remote + across_x)
    upper_x = jnp.where(along_x < BXY - 1, cell_order[cell_number(jnp.minimum(along_x + 1, BXY - 1), along_y, along_z)] * 6 + 0, remote + CAP + across_x)
    lower_y = jnp.where(along_y > 0, cell_order[cell_number(along_x, jnp.maximum(along_y - 1, 0), along_z)] * 6 + 3, remote + 2 * CAP + across_y)
    upper_y = jnp.where(along_y < BXY - 1, cell_order[cell_number(along_x, jnp.minimum(along_y + 1, BXY - 1), along_z)] * 6 + 2, remote + 3 * CAP + across_y)
    lower_z = cell_order[cell_number(along_x, along_y, (along_z - 1) % BZ)] * 6 + 5
    upper_z = cell_order[cell_number(along_x, along_y, (along_z + 1) % BZ)] * 6 + 4
    by_cell = jnp.stack([lower_x, upper_x, lower_y, upper_y, lower_z, upper_z], axis=1).astype(jnp.int32)
    partner = jnp.zeros((E_DEV, 6), jnp.int32).at[cell_order].set(by_cell)
    slot_ids = jnp.arange(CAP)
    outer_pos = slot_ids // BZ
    inner_pos = slot_ids % BZ
    send_lists = jnp.stack([cell_order[cell_number(0, outer_pos, inner_pos)] * 6 + 0, cell_order[cell_number(BXY - 1, outer_pos, inner_pos)] * 6 + 1, cell_order[cell_number(outer_pos, 0, inner_pos)] * 6 + 2, cell_order[cell_number(outer_pos, BXY - 1, inner_pos)] * 6 + 3]).astype(jnp.int32)
    return (partner, send_lists)


def draw_face_partner(key, part):
    partner, send_lists = jax.vmap(device_faces)(brick_orders(key))
    return partner.reshape(ELEMENTS, 6).astype(jnp.int32)


def draw_send_faces(key, part):
    partner, send_lists = jax.vmap(device_faces)(brick_orders(key))
    return send_lists.astype(jnp.int32)


def migration_tables(key):
    base_key = jax.random.fold_in(key, 23)
    half_count = P_DEV // 2

    def group_tables(group):
        group_keys = jax.random.split(jax.random.fold_in(base_key, group), 4)
        arrangement = jax.random.permutation(group_keys[0], N_SEG).astype(jnp.int32)
        full_offset = jax.random.randint(group_keys[1], (), 0, N_SEG - 1)
        weights = jnp.zeros((N_SEG - 1,), jnp.int32).at[full_offset].set(MIG_CAP)
        random_picks = jax.random.randint(group_keys[2], (half_count - MIG_CAP,), 0, N_SEG - 1)
        offsets = jnp.arange(N_SEG - 1)

        def assign_unit(current, pick_value):
            distance = (offsets - pick_value) % (N_SEG - 1)
            priority = jnp.where(current < MIG_CAP, distance, 4 * N_SEG)
            return (current.at[jnp.argmin(priority)].add(1), None)
        weights, unused = lax.scan(assign_unit, weights, random_picks)
        upper_sum = jnp.cumsum(weights)
        lower_sum = upper_sum - weights
        moving = jnp.arange(half_count)
        offset_rank = jnp.sum(moving[:, None] >= upper_sum[None, :], axis=1)
        slot_index = (moving - lower_sum[offset_rank]).astype(jnp.int32)
        offset_step = offset_rank + 1

        def member(position):
            member_keys = jax.random.split(jax.random.fold_in(group_keys[3], position), 2)
            element_order = jax.random.permutation(member_keys[0], E_DEV)
            parent_order = jax.random.permutation(member_keys[1], P_DEV).astype(jnp.int32)
            holder = arrangement[position]
            owners = arrangement[(position + offset_step) % N_SEG]
            sources = arrangement[(position - offset_step) % N_SEG]
            group_owner = jnp.concatenate([jnp.full((half_count,), holder, jnp.int32), owners])
            group_slot = jnp.concatenate([parent_order[:half_count], slot_index])
            local_ids = jnp.arange(E_DEV)
            values = jnp.stack([group_owner[local_ids // 8], group_slot[local_ids // 8], (local_ids % 8).astype(jnp.int32)])
            moved = jnp.zeros((3, E_DEV), jnp.int32).at[:, element_order].set(values)
            parent_values = jnp.stack([jnp.concatenate([jnp.full((half_count,), holder, jnp.int32), sources]), jnp.concatenate([jnp.full((half_count,), -1, jnp.int32), slot_index])])
            owned = jnp.zeros((2, P_DEV), jnp.int32).at[:, parent_order].set(parent_values)
            return (moved, owned)
        moved, owned = jax.vmap(member)(jnp.arange(N_SEG))
        inverse = jnp.argsort(arrangement)
        return (moved[inverse], owned[inverse])
    moved, owned = jax.vmap(group_tables)(jnp.arange(N_CURVE))
    moved = jnp.transpose(moved, (2, 0, 1, 3)).reshape(3, ELEMENTS)
    owned = jnp.transpose(owned, (2, 0, 1, 3)).reshape(2, PARENTS)
    return (moved.astype(jnp.int32), owned.astype(jnp.int32))


def draw_migration(key, part):
    moved, owned = migration_tables(key)
    return moved


def draw_children(key, part):
    moved, owned = migration_tables(key)
    return owned


def block_levels(key, dims, shards, low, largest):
    factor_of = 1.0
    for axis_at, blocks in shards:
        heights = jax.random.uniform(jax.random.fold_in(jax.random.fold_in(key, 6), axis_at), (blocks,), jnp.float32, low / len(shards), largest / len(shards))
        factor_of = factor_of * jnp.repeat(jnp.exp(heights), dims[axis_at] // blocks).reshape((-1,) + (1,) * (len(dims) - 1 - axis_at))
    return factor_of


def bell_draw(rng, dims, deviation, most, pieces=(), kind=jnp.bfloat16):
    level = block_levels(rng, dims, pieces, -0.22, 0.18) if pieces else 1.0
    values = jax.random.normal(rng, dims, jnp.float32) * deviation * level
    return jnp.minimum(jnp.maximum(values, -most), most).astype(kind)


def setup_inputs(seed: int = 0) -> dict:
    keys = jax.random.split(jax.random.key(seed), 7)
    adjoint = bell_draw(keys[0], (9, ELEMENTS, NODES), 1.0, 6.0, ((1, 128),), jnp.float32)
    material = jnp.clip(jnp.exp(math.log(2.0) - 1.3862944 * jax.random.uniform(keys[1], (3, ELEMENTS), jnp.float32) ** block_levels(keys[1], (3, ELEMENTS), ((1, 128),), -0.2, 0.2)), 0.5, 2.0)
    face_partner = draw_face_partner(jax.random.fold_in(keys[6], 71), 0)
    send_faces = draw_send_faces(jax.random.fold_in(keys[6], 71), 0)
    migration = draw_migration(jax.random.fold_in(keys[6], 71), 0)
    children = draw_children(jax.random.fold_in(keys[6], 71), 0)
    return {"adjoint": adjoint, "material": material, "face_partner": face_partner, "send_faces": send_faces, "migration": migration, "children": children}


voigt_index = ((3, 8, 7), (8, 4, 6), (7, 6, 5))
courant = 0.8


def lobatto_nodes(edge_nodes):
    return -np.cos(np.pi * np.arange(edge_nodes) / (edge_nodes - 1))


def derivative_line(edge_nodes):
    points = lobatto_nodes(edge_nodes)
    node_ids = np.arange(edge_nodes)
    weight = np.where((node_ids == 0) | (node_ids == edge_nodes - 1), 2.0, 1.0)
    row_ids = node_ids[:, None]
    column_ids = node_ids[None, :]
    differ = points[:, None] - points[None, :]
    safe_gap = np.where(row_ids == column_ids, 1.0, differ)
    matrix = (weight[:, None] / weight[None, :]) * (-1.0) ** (row_ids + column_ids) / safe_gap
    matrix = np.where(row_ids == column_ids, 0.0, matrix)
    return matrix - np.eye(edge_nodes) * matrix.sum(axis=1)[:, None]


def derivative_stack(edge_nodes):
    line_matrix = derivative_line(edge_nodes)
    identity = np.eye(edge_nodes)
    blocks = [np.kron(np.kron(line_matrix, identity), identity), np.kron(np.kron(identity, line_matrix), identity), np.kron(np.kron(identity, identity), line_matrix)]
    return jnp.asarray(np.concatenate(blocks, axis=0), dtype=jnp.float32)


def refine_line(edge_nodes, upper):
    points = lobatto_nodes(edge_nodes)
    targets = (points + (2.0 * upper - 1.0)) / 2.0
    columns = []
    for column in range(edge_nodes):
        factor = np.ones(edge_nodes)
        for other_node in range(edge_nodes):
            if other_node != column:
                factor = factor * (targets - points[other_node]) / (points[column] - points[other_node])
        columns.append(factor)
    return np.stack(columns, axis=1)


def refine_stack(edge_nodes):
    blocks = []
    for octant in range(8):
        blocks.append(np.kron(np.kron(refine_line(edge_nodes, (octant // 4) % 2), refine_line(edge_nodes, (octant // 2) % 2)), refine_line(edge_nodes, octant % 2)))
    return jnp.asarray(np.concatenate(blocks, axis=0), dtype=jnp.float32)


def material_image(field_state, inv_density, lame_first, shear_modulus, direction):
    trace_sum = field_state[3] + field_state[4] + field_state[5]
    velocity = []
    for component in range(3):
        velocity_term = shear_modulus * field_state[voigt_index[direction][component]]
        if component == direction:
            velocity_term = 2.0 * velocity_term + lame_first * trace_sum
        velocity.append(velocity_term)
    stress = [inv_density * field_state[component] for component in range(3)]
    return jnp.stack(velocity), jnp.stack(stress)


def place_rows(velocity, stress, direction):
    zero_row = jnp.zeros_like(velocity[0])
    row_list = [velocity[0], velocity[1], velocity[2]] + [zero_row] * 6
    for component in range(3):
        row_list[voigt_index[component][direction]] = stress[component]
    return jnp.stack(row_list)


def face_selector(face_id, edge_nodes):
    plane_index = 0 if face_id % 2 == 0 else edge_nodes - 1
    selector = [slice(None)] * 5
    selector[2 + face_id // 2] = plane_index
    return tuple(selector)


def volume_term(field_state, materials, derivative):
    elements = field_state.shape[1]
    columns = []
    for direction in range(3):
        velocity, stress = material_image(field_state, materials[0][:, None], materials[1][:, None], materials[2][:, None], direction)
        columns.append(place_rows(velocity, stress, direction))
    stacked = jnp.concatenate(columns, axis=2).reshape(9 * elements, 3 * field_state.shape[2])
    product = jnp.dot(stacked, derivative, precision=lax.Precision.HIGHEST, preferred_element_type=jnp.float32)
    return product.reshape(9, elements, field_state.shape[2])


def image_of_faces(traces, inv_density, lame_first, shear_modulus):
    parts = []
    for direction in range(3):
        face_part = traces[:, :, 2 * direction:2 * direction + 2]
        velocity, stress = material_image(face_part, inv_density[:, None, None], lame_first[:, None, None], shear_modulus[:, None, None], direction)
        parts.append(jnp.concatenate([velocity, stress], axis=0))
    return jnp.concatenate(parts, axis=2)


def add_faces(result, face_total, edge_nodes):
    elements = face_total.shape[1]
    lift = 0.5 * edge_nodes * (edge_nodes - 1)
    for face_id in range(6):
        lift_factor = 0.5 * lift if face_id % 2 == 0 else -0.5 * lift
        piece = lift_factor * face_total[:, :, face_id]
        row_block = place_rows(piece[0:3], piece[3:6], face_id // 2)
        result = result.at[face_selector(face_id, edge_nodes)].add(row_block.reshape(9, elements, edge_nodes, edge_nodes))
    return result


def runge_step(field_state, operator, time_step):
    section_one = operator(field_state)
    section_two = operator(field_state + 0.5 * time_step * section_one)
    section_three = operator(field_state + 0.5 * time_step * section_two)
    section_four = operator(field_state + time_step * section_three)
    return field_state + (time_step / 6.0) * (section_one + 2.0 * section_two + 2.0 * section_three + section_four)


def reference(adjoint, material, face_partner, send_faces, migration, children):
    elements = adjoint.shape[1]
    devices = elements // E_DEV
    derivative = derivative_stack(NP)
    inv_density = 1.0 / material[0]
    lame_first = material[1]
    shear_modulus = material[2]
    materials = jnp.moveaxis(jnp.stack([inv_density, lame_first, shear_modulus]).reshape(3, devices, E_DEV), 1, 0)

    def block_volume(block_pair):
        return volume_term(block_pair[0], block_pair[1], derivative)

    def operator(field_state):
        blocks = jnp.moveaxis(field_state.reshape(9, devices, E_DEV, NODES), 1, 0)
        volume = lax.map(block_volume, (blocks, materials))
        result = jnp.moveaxis(volume, 0, 1).reshape(9, elements, NP, NP, NP)
        node_cube = field_state.reshape(9, elements, NP, NP, NP)
        traces = jnp.stack([node_cube[face_selector(face_id, NP)].reshape(9, elements, FACE) for face_id in range(6)], axis=2)
        face_image = image_of_faces(traces, inv_density, lame_first, shear_modulus)
        local_table = face_image.reshape(6, devices, E_DEV * 6, FACE)
        sent_rows = jnp.take_along_axis(local_table, send_faces.reshape(1, devices, 4 * CAP, 1), axis=2).reshape(6, N_CURVE, N_SEG, 4, CAP, FACE)
        received = jnp.stack([jnp.roll(sent_rows[:, :, :, 1], 1, axis=1), jnp.roll(sent_rows[:, :, :, 0], -1, axis=1), jnp.roll(sent_rows[:, :, :, 3], 1, axis=2), jnp.roll(sent_rows[:, :, :, 2], -1, axis=2)], axis=3).reshape(6, devices, 4 * CAP, FACE)
        image_table = jnp.concatenate([local_table, received], axis=2)
        partner_image = jnp.take_along_axis(image_table, face_partner.reshape(1, devices, E_DEV * 6, 1), axis=2).reshape(6, elements, 6, FACE)
        return add_faces(result, face_image + partner_image, NP).reshape(9, elements, NODES)

    adjoint_next = runge_step(adjoint, operator, courant / (NP * NP))

    element_ids = jnp.arange(elements, dtype=jnp.int32)
    device_ids = element_ids // E_DEV
    own_seg = device_ids % N_SEG
    owner_device = (device_ids // N_SEG) * N_SEG + migration[0]
    parent_ids = jnp.arange(PARENTS, dtype=jnp.int32)
    parent_device = parent_ids // P_DEV
    migrated = children[1] >= 0
    table_size = devices * N_SEG * MIG_CAP
    lookup_key = jnp.where(migrated, (parent_device * N_SEG + children[0]) * MIG_CAP + jnp.maximum(children[1], 0), table_size).astype(jnp.int32)
    lookup = jnp.zeros((table_size,), jnp.int32).at[lookup_key].set((parent_ids % P_DEV).astype(jnp.int32), mode="drop")
    stays_home = migration[0] == own_seg
    remote_key = ((owner_device * N_SEG + own_seg) * MIG_CAP + jnp.clip(migration[1], 0, MIG_CAP - 1)).astype(jnp.int32)
    local_parent = jnp.where(stays_home, migration[1], lookup[remote_key])
    position = ((owner_device * P_DEV + local_parent) * 8 + migration[2]).astype(jnp.int32)
    placed = jnp.zeros((9, PARENTS * 8, NODES), jnp.float32).at[:, position].set(adjoint_next)
    parent_adjoint = jnp.dot(placed.reshape(9 * PARENTS, 8 * NODES), refine_stack(NP), precision=lax.Precision.HIGHEST, preferred_element_type=jnp.float32).reshape(9, PARENTS, NODES)
    return adjoint_next, parent_adjoint
```

```python
import functools

import jax
import jax.numpy as jnp
import numpy as np
from jax import lax
from jax.experimental import pallas as pl
from jax.experimental.pallas import tpu as pltpu
from jax.sharding import PartitionSpec as P

NP = 8
NODES = 512
E_DEV = 64
CAP = 16
P_DEV = 8
N_CURVE = 8
N_SEG = 16
LOCAL = 6 * E_DEV

voigt_index = ((3, 8, 7), (8, 4, 6), (7, 6, 5))
time_step = 0.8 / (NP * NP)
lift_half = 0.25 * NP * (NP - 1)
BF = jnp.bfloat16
F32 = jnp.float32


def lobatto_nodes(edge_nodes):
    return -np.cos(np.pi * np.arange(edge_nodes) / (edge_nodes - 1))


def derivative_line(edge_nodes):
    points = lobatto_nodes(edge_nodes)
    node_ids = np.arange(edge_nodes)
    weight = np.where((node_ids == 0) | (node_ids == edge_nodes - 1), 2.0, 1.0)
    row_ids = node_ids[:, None]
    column_ids = node_ids[None, :]
    differ = points[:, None] - points[None, :]
    safe_gap = np.where(row_ids == column_ids, 1.0, differ)
    matrix = weight[:, None] / weight[None, :] * (-1.0) ** (row_ids + column_ids) / safe_gap
    matrix = np.where(row_ids == column_ids, 0.0, matrix)
    return matrix - np.eye(edge_nodes) * matrix.sum(axis=1)[:, None]


def refine_line(edge_nodes, upper):
    points = lobatto_nodes(edge_nodes)
    targets = (points + (2.0 * upper - 1.0)) / 2.0
    columns = []
    for column in range(edge_nodes):
        factor = np.ones(edge_nodes)
        for other_node in range(edge_nodes):
            if other_node != column:
                factor = (
                    factor * (targets - points[other_node]) / (points[column] - points[other_node])
                )
        columns.append(factor)
    return np.stack(columns, axis=1)


def refine_parts():
    blocks = []
    for octant in range(8):
        lines = [refine_line(NP, octant // 4 % 2), refine_line(NP, octant // 2 % 2), refine_line(NP, octant % 2)]
        blocks.append(np.kron(np.kron(lines[0], lines[1]), lines[2]))
    whole = np.stack(blocks).astype(np.float32)
    high = whole.astype(BF)
    low = (whole - high.astype(np.float32)).astype(BF)
    return high, low


_line = derivative_line(NP)
_line[0, 0] += lift_half
_line[7, 7] -= lift_half
ODD = 0.5 * (_line[:4, :4] - _line[:3:-1, :4])
EVEN = 0.5 * (_line[:4, :4] + _line[:3:-1, :4])


def line_product(x):
    odd = [x[a] - x[7 - a] for a in range(4)]
    even = [x[a] + x[7 - a] for a in range(4)]
    out = [None] * 8
    for m in range(4):
        p = sum(odd[a] * float(ODD[a, m]) for a in range(4))
        q = sum(even[a] * float(EVEN[a, m]) for a in range(4))
        out[m] = p + q
        out[7 - m] = p - q
    return out


def low_half():
    return lax.broadcasted_iota(jnp.int32, (8, 128), 1) < 64


def swap_halves(x):
    return pltpu.roll(x, 64, 1)


def lane_patterns():
    low = low_half()
    out = []
    for matrix in (ODD, EVEN):
        straight = [[None] * 2 for _ in range(2)]
        crossed = [[None] * 2 for _ in range(2)]
        for j in range(2):
            for m in range(2):
                straight[j][m] = jnp.where(low, float(matrix[2 * j, 2 * m]), float(matrix[2 * j + 1, 2 * m + 1]))
                crossed[j][m] = jnp.where(low, float(matrix[2 * j + 1, 2 * m]), float(matrix[2 * j, 2 * m + 1]))
        out.append((straight, crossed))
    return out


def lane_product(x, patterns):
    back = [swap_halves(x[3]), swap_halves(x[2])]
    sums = []
    for parts, (straight, crossed) in zip(
        ([x[0] - back[0], x[1] - back[1]], [x[0] + back[0], x[1] + back[1]]), patterns
    ):
        turned = [swap_halves(part) for part in parts]
        sums.append(
            [
                parts[0] * straight[0][m] + turned[0] * crossed[0][m] + parts[1] * straight[1][m] + turned[1] * crossed[1][m]
                for m in range(2)
            ]
        )
    p, q = sums
    return [p[0] + q[0], p[1] + q[1], swap_halves(p[1] - q[1]), swap_halves(p[0] - q[0])]


def split(x):
    high = x.astype(BF)
    return high, (x - high.astype(F32)).astype(BF)


def along(k, start=None):
    return pl.ds(k, 8, stride=8)


def image_rows(get, mat, direction):
    inv_density, lame, shear = mat
    trace = get(3) + get(4) + get(5)
    out = []
    for k in range(3):
        term = shear * get(voigt_index[direction][k])
        if k == direction:
            term = 2.0 * term + lame * trace
        out.append(term)
    return out + [inv_density * get(i) for i in range(3)]


def target_row(value, direction):
    return value if value < 3 else voigt_index[value - 3][direction]


def build_table(v_ref, mat, t_ref):
    low = low_half()

    def put(value, block, direction, x0, x1):
        pair = jnp.concatenate([x0, x1], axis=0)
        high, rest = split(pair)
        rows = pl.ds(value * 64 + block * 16, 16)
        t_ref[rows, pl.ds(direction * 128, 128)] = high
        t_ref[rows, pl.ds(LOCAL + direction * 128, 128)] = rest

    for direction in range(2):
        for j in range(4):
            if direction == 0:
                ends = [image_rows(lambda i, r=r: v_ref[i, j, pl.ds(r, 8), :], mat, 0) for r in (0, 56)]
            else:
                ends = [image_rows(lambda i, r=r: v_ref[i, j, along(r), :], mat, 1) for r in (0, 7)]
            for value in range(6):
                a0, a1 = ends[0][value], ends[1][value]
                put(
                    value,
                    j,
                    direction,
                    jnp.where(low, a0, swap_halves(a1)),
                    jnp.where(low, swap_halves(a0), a1),
                )
    for pair in range(4):
        blocks = []
        for b in (2 * pair, 2 * pair + 1):
            blocks.append(
                image_rows(
                    lambda i, b=b: jnp.where(
                        low, v_ref[i, 0, along(b), :], v_ref[i, 3, along(b), :]
                    ),
                    mat,
                    2,
                )
            )
        for value in range(6):
            put(value, pair, 2, blocks[0][value], blocks[1][value])


def materials(mat_ref):
    return mat_ref[0], mat_ref[1], mat_ref[2]


def send_values(send_ref, t_ref, out_refs):
    rows = lax.dot_general(
        send_ref[...], t_ref[...], (((1,), (1,)), ((), ())), preferred_element_type=F32
    )
    for k in range(4):
        out_refs[k][...] = rows[16 * k : 16 * k + 16]


def begin_kernel(
    adjoint_ref, mat_ref, partner_ref, sent_ref,
    v_ref, t_ref, local_ref, remote_ref, send_ref, p0, p1, p2, p3, turn_ref,
):
    low = lax.broadcasted_iota(jnp.int32, (64, 128), 1) < 64

    def body(i, carry):
        x = adjoint_ref[i]
        turn_ref[...] = jnp.concatenate([x, x], axis=0).T
        for j in range(4):
            v_ref[i, j] = jnp.where(
                low, turn_ref[pl.ds(2 * j, 64, stride=8), :], turn_ref[pl.ds(2 * j + 1, 64, stride=8), :]
            )
        return carry

    lax.fori_loop(0, 9, body, 0)
    partner = partner_ref[...]
    face = lax.broadcasted_iota(jnp.int32, (1, LOCAL), 1) // 64
    weight = jnp.where(face % 2 == 0, lift_half, -lift_half)
    for start in range(0, LOCAL, 64):
        source = lax.broadcasted_iota(jnp.int32, (64, LOCAL), 0) + start
        block = jnp.where(source == partner, weight, 0.0).astype(BF)
        local_ref[pl.ds(start, 64), :] = block
        local_ref[pl.ds(LOCAL + start, 64), :] = block
    source = lax.broadcasted_iota(jnp.int32, (64, LOCAL), 0) + LOCAL
    block = jnp.where(source == partner, weight, 0.0).astype(BF)
    remote_ref[pl.ds(0, 64), :] = block
    remote_ref[pl.ds(64, 64), :] = block
    chosen = jnp.where(
        lax.broadcasted_iota(jnp.int32, (64, LOCAL), 1) == sent_ref[...], 1.0, 0.0
    ).astype(BF)
    send_ref[:, pl.ds(0, LOCAL)] = chosen
    send_ref[:, pl.ds(LOCAL, LOCAL)] = chosen
    build_table(v_ref, materials(mat_ref), t_ref)
    send_values(send_ref, t_ref, (p0, p1, p2, p3))


def first_volume_kernel(v_ref, t_ref, local_ref, mat_ref, vol_ref, part_ref):
    volume_kernel(v_ref, t_ref, local_ref, mat_ref, None, vol_ref, part_ref, None)


def volume_kernel(v_ref, t_ref, local_ref, mat_ref, acc_ref, vol_ref, part_ref, sum_ref):
    mat = materials(mat_ref)
    inv_density, lame, shear = mat

    def scaled(get, direction):
        out = []
        for k in range(3):
            if k == direction:
                out.append(
                    (k, [2.0 * shear * d + lame * (s0 + s1 + s2) for d, s0, s1, s2 in zip(get(3 + k), get(3), get(4), get(5))])
                )
            else:
                out.append((k, [shear * x for x in get(voigt_index[direction][k])]))
        for i in range(3):
            out.append((voigt_index[i][direction], [inv_density * x for x in get(i)]))
        return out

    def tiles(j, carry):
        for row, x in scaled(lambda i: [v_ref[i, j, along(b), :] for b in range(8)], 1):
            for b, y in enumerate(line_product(x)):
                vol_ref[row, j, along(b), :] = y
        for row, x in scaled(lambda i: [v_ref[i, j, pl.ds(8 * a, 8), :] for a in range(8)], 0):
            for a, y in enumerate(line_product(x)):
                if row not in (3, 7):
                    y = y + vol_ref[row, j, pl.ds(8 * a, 8), :]
                vol_ref[row, j, pl.ds(8 * a, 8), :] = y
        return carry

    lax.fori_loop(0, 4, tiles, 0)
    patterns = lane_patterns()

    def groups(a, carry):
        rows = pl.ds(pl.multiple_of(a * 8, 8), 8)
        for row, x in scaled(lambda i: [v_ref[i, j, rows, :] for j in range(4)], 2):
            for j, y in enumerate(lane_product(x, patterns)):
                if row != 5:
                    y = y + vol_ref[row, j, rows, :]
                vol_ref[row, j, rows, :] = y
        if sum_ref is not None:
            for i in range(9):
                for j in range(4):
                    sum_ref[i, j, rows, :] = acc_ref[i, j, rows, :] + v_ref[i, j, rows, :]
        return carry

    lax.fori_loop(0, 8, groups, 0)
    for k in range(6):
        part_ref[pl.ds(64 * k, 64), :] = jnp.dot(
            t_ref[pl.ds(64 * k, 64), :], local_ref[...], preferred_element_type=F32
        )


def add_faces(vol_ref, part_ref, r_refs, remote_ref, factor, out_ref, face_ref):
    for i in range(9):
        out_ref[i] = vol_ref[i] * factor
    arrived = jnp.concatenate([r[...] for r in r_refs], axis=0).T
    both = jnp.concatenate(split(arrived), axis=1)
    face_ref[...] = (part_ref[...] + jnp.dot(both, remote_ref[...], preferred_element_type=F32)) * factor
    low = low_half()
    for direction in range(3):
        for value in range(6):
            row = target_row(value, direction)
            for j in range(4):
                x0 = face_ref[pl.ds(value * 64 + 16 * j, 8), pl.ds(direction * 128, 128)]
                x1 = face_ref[pl.ds(value * 64 + 16 * j + 8, 8), pl.ds(direction * 128, 128)]
                if direction < 2:
                    y0 = jnp.where(low, x0, swap_halves(x1))
                    y1 = jnp.where(low, swap_halves(x0), x1)
                    rows = (pl.ds(0, 8), pl.ds(56, 8)) if direction == 0 else (along(0), along(7))
                    out_ref[row, j, rows[0], :] += y0
                    out_ref[row, j, rows[1], :] += y1
                else:
                    for b, x in ((2 * j, x0), (2 * j + 1, x1)):
                        out_ref[row, 0, along(b), :] += jnp.where(low, x, 0.0)
                        out_ref[row, 3, along(b), :] += jnp.where(low, 0.0, x)


def finish_kernel(
    factor, vol_ref, part_ref, r0, r1, r2, r3, remote_ref, mat_ref, send_ref,
    v_ref, t_ref, p0, p1, p2, p3, face_ref,
):
    add_faces(vol_ref, part_ref, (r0, r1, r2, r3), remote_ref, factor, v_ref, face_ref)
    build_table(v_ref, materials(mat_ref), t_ref)
    send_values(send_ref, t_ref, (p0, p1, p2, p3))


def end_kernel(
    factor, keys_ref, vol_ref, part_ref, r0, r1, r2, r3, remote_ref, acc_ref, place_ref, high_ref, low_ref,
    next_ref, home_ref, away_ref, v_ref, face_ref, turn_ref, sorted_ref, parent_ref,
):
    add_faces(vol_ref, part_ref, (r0, r1, r2, r3), remote_ref, factor, v_ref, face_ref)
    place = jnp.where(
        lax.broadcasted_iota(jnp.int32, (64, 64), 0) == place_ref[...], 1.0, 0.0
    ).astype(BF)

    def body(i, carry):
        for j in range(4):
            tile = acc_ref[i, j] + v_ref[i, j]
            turn_ref[pl.ds(2 * j, 64, stride=8), :] = tile
            turn_ref[pl.ds(2 * j + 1, 64, stride=8), :] = pltpu.roll(tile, 64, 1)
        x = turn_ref[...].T[:64]
        next_ref[i] = x
        high, rest = split(x)
        sorted_ref[i] = (
            jnp.dot(place, high, preferred_element_type=F32)
            + jnp.dot(place, rest, preferred_element_type=F32)
        )
        return carry

    lax.fori_loop(0, 9, body, 0)
    parent_ref[...] = jnp.zeros_like(parent_ref)

    def octants(c, carry):
        x = jnp.concatenate(
            [sorted_ref[i, pl.ds(pl.multiple_of(c * 8, 8), 8), :] for i in range(9)]
            + [jnp.zeros((8, NODES), F32)],
            axis=0,
        )
        high, rest = split(x)
        parent_ref[...] += (
            jnp.dot(high, high_ref[c], preferred_element_type=F32)
            + jnp.dot(rest, high_ref[c], preferred_element_type=F32)
            + jnp.dot(high, low_ref[c], preferred_element_type=F32)
        )
        return carry

    lax.fori_loop(0, 8, octants, 0)
    away_ref[...] = jnp.zeros_like(away_ref)
    home_ref[...] = jnp.zeros_like(home_ref)
    for g in range(P_DEV):
        key = keys_ref[g]

        @pl.when(key < P_DEV)
        def _():
            for i in range(9):
                home_ref[i, pl.ds(key, 1), :] = parent_ref[pl.ds(8 * i + g, 1), :]

        @pl.when(key >= P_DEV)
        def _():
            owner = (key - P_DEV) // 2
            slot = (key - P_DEV) % 2
            for i in range(9):
                for j in range(4):
                    away_ref[owner, i, pl.ds(slot * 4 + j, 1), :] = parent_ref[
                        pl.ds(8 * i + g, 1), pl.ds(128 * j, 128)
                    ]


def parent_kernel(table_ref, home_ref, arrived_ref, out_ref):
    out_ref[...] = home_ref[...]
    for p in range(P_DEV):
        holder = table_ref[0, p]
        slot = table_ref[1, p]

        @pl.when(slot >= 0)
        def _():
            for i in range(9):
                for j in range(4):
                    out_ref[i, pl.ds(p, 1), pl.ds(128 * j, 128)] = arrived_ref[
                        holder, i, pl.ds(slot * 4 + j, 1), :
                    ]


def shape(*dims, dtype=F32):
    return jax.ShapeDtypeStruct(dims, dtype)


VMEM = pl.BlockSpec(memory_space=pltpu.VMEM)
SMEM = pl.BlockSpec(memory_space=pltpu.SMEM)


def call(kernel, outs, scratch=(), smem=(), count=0, flops=10**8, traffic=6 * 10**6):
    return pl.pallas_call(
        kernel,
        out_shape=outs,
        in_specs=[SMEM if k in smem else VMEM for k in range(count)],
        out_specs=jax.tree.map(lambda _: VMEM, outs),
        scratch_shapes=list(scratch),
        compiler_params=pltpu.CompilerParams(vmem_limit_bytes=32 * 2**20),
        cost_estimate=pl.CostEstimate(flops=flops, bytes_accessed=traffic, transcendentals=0),
    )


def exchange_pairs():
    along_x = [[(k, (k + 1) % N_CURVE) for k in range(start, N_CURVE, 2)] for start in (0, 1)]
    along_y = [[(k, (k + 1) % N_SEG) for k in range(start, N_SEG, 2)] for start in (0, 1)]
    both = lambda pairs: pairs + [(b, a) for a, b in pairs]
    return [("curve", both(p)) for p in along_x] + [("seg", both(p)) for p in along_y]


def shards(adjoint, material, face_partner, send_faces, migration, children):
    own_curve = lax.axis_index("curve")
    own_seg = lax.axis_index("seg")
    double = lambda x: jnp.broadcast_to(jnp.concatenate([x, x])[None, :], (8, 128))
    mat = jnp.stack([double(1.0 / material[0]), double(material[1]), double(material[2])])
    even_x = (own_curve % 2 == 0).astype(jnp.int32)
    even_y = (own_seg % 2 == 0).astype(jnp.int32)
    remote = face_partner - LOCAL
    side = remote // CAP
    block = side ^ jnp.where(side < 2, even_x, even_y)
    lane = lambda q: (q % 6) * E_DEV + q // 6
    partner = jnp.where(remote < 0, lane(face_partner), LOCAL + block * CAP + remote % CAP)
    partner = partner.T.reshape(1, LOCAL)
    sides = lane(send_faces[0])
    flipped = sides.reshape(2, 2, CAP)[:, ::-1]
    even = jnp.stack([even_x, even_y])[:, None, None]
    sent = jnp.where(even == 1, flipped, sides.reshape(2, 2, CAP)).reshape(4 * CAP, 1)

    owner, slot, octant = migration[0], migration[1], migration[2]
    key = jnp.where(owner == own_seg, slot, P_DEV + 2 * owner + slot)
    first = octant == 0
    rank = jnp.sum((first[:, None] & (key[:, None] < key[None, :])).astype(jnp.int32), axis=0)
    place = (octant * P_DEV + rank).reshape(1, E_DEV)
    keys = jnp.sum(
        jnp.where(first[:, None] & (rank[:, None] == jnp.arange(P_DEV)[None, :]), key[:, None], 0), axis=0
    )
    source = jnp.stack([children[0], jnp.where(children[0] == own_seg, -1, children[1])])

    state = shape(9, 4, 64, 128)
    table = shape(LOCAL, 2 * LOCAL, dtype=BF)
    face_part = shape(LOCAL, LOCAL)
    payload = [shape(CAP, LOCAL)] * 4
    face_scratch = pltpu.VMEM((LOCAL, LOCAL), F32)
    turn = pltpu.VMEM((NODES, 128), F32)

    outs = call(
        begin_kernel,
        [state, table, shape(2 * LOCAL, LOCAL, dtype=BF), shape(128, LOCAL, dtype=BF), shape(64, 2 * LOCAL, dtype=BF)]
        + payload,
        [turn],
        count=4,
    )(adjoint, mat, partner, sent)
    v, t, local_hot, remote_hot, send_hot = outs[:5]
    out_going = outs[5:]
    pairs = exchange_pairs()
    for step in range(1, 5):
        arrived = [lax.ppermute(x, axis, p) for x, (axis, p) in zip(out_going, pairs)]
        if step == 1:
            vol, part = call(first_volume_kernel, [state, face_part], count=4)(v, t, local_hot, mat)
            acc = v
        else:
            vol, part, acc = call(volume_kernel, [state, face_part, state], count=5)(v, t, local_hot, mat, acc)
        factor = time_step / step
        if step < 4:
            outs = call(
                functools.partial(finish_kernel, factor), [state, table] + payload, [face_scratch], count=9
            )(vol, part, *arrived, remote_hot, mat, send_hot)
            v, t, out_going = outs[0], outs[1], outs[2:]
    high, low = refine_parts()
    updated, home, away = call(
        functools.partial(end_kernel, factor),
        [shape(9, E_DEV, NODES), shape(9, P_DEV, NODES), shape(N_SEG, 9, 8, 128)],
        [
            pltpu.VMEM((9, 4, 64, 128), F32),
            face_scratch,
            turn,
            pltpu.VMEM((9, E_DEV, NODES), F32),
            pltpu.VMEM((80, NODES), F32),
        ],
        smem=(0,),
        count=12,
    )(keys, vol, part, *arrived, remote_hot, acc, place, jnp.asarray(high), jnp.asarray(low))
    fetched = lax.all_to_all(away, "seg", split_axis=0, concat_axis=0, tiled=True)
    parents = call(parent_kernel, [shape(9, P_DEV, NODES)], smem=(0,), count=3)(source, home, fetched)[0]
    return (updated, parents)


def solution(mesh):
    in_specs = (
        P(None, ("curve", "seg"), None),
        P(None, ("curve", "seg")),
        P(("curve", "seg"), None),
        P(("curve", "seg"), None, None),
        P(None, ("curve", "seg")),
        P(None, ("curve", "seg")),
    )
    out_specs = (P(None, ("curve", "seg"), None), P(None, ("curve", "seg"), None))
    return jax.shard_map(shards, mesh=mesh, in_specs=in_specs, out_specs=out_specs, check_vma=False)
```

```python
import functools

import jax
import jax.numpy as jnp
import numpy as np
from jax import lax
from jax.experimental import pallas as pl
from jax.experimental.pallas import tpu as pltpu
from jax.sharding import PartitionSpec as P

NP = 8
NODES = 512
E_DEV = 64
CAP = 16
P_DEV = 8
N_CURVE = 8
N_SEG = 16
LOCAL = 6 * E_DEV

voigt_index = ((3, 8, 7), (8, 4, 6), (7, 6, 5))
time_step = 0.8 / (NP * NP)
lift_half = 0.25 * NP * (NP - 1)
BF = jnp.bfloat16
F32 = jnp.float32


def lobatto_nodes(edge_nodes):
    return -np.cos(np.pi * np.arange(edge_nodes) / (edge_nodes - 1))


def derivative_line(edge_nodes):
    points = lobatto_nodes(edge_nodes)
    node_ids = np.arange(edge_nodes)
    weight = np.where((node_ids == 0) | (node_ids == edge_nodes - 1), 2.0, 1.0)
    row_ids = node_ids[:, None]
    column_ids = node_ids[None, :]
    differ = points[:, None] - points[None, :]
    safe_gap = np.where(row_ids == column_ids, 1.0, differ)
    matrix = weight[:, None] / weight[None, :] * (-1.0) ** (row_ids + column_ids) / safe_gap
    matrix = np.where(row_ids == column_ids, 0.0, matrix)
    return matrix - np.eye(edge_nodes) * matrix.sum(axis=1)[:, None]


def refine_line(edge_nodes, upper):
    points = lobatto_nodes(edge_nodes)
    targets = (points + (2.0 * upper - 1.0)) / 2.0
    columns = []
    for column in range(edge_nodes):
        factor = np.ones(edge_nodes)
        for other_node in range(edge_nodes):
            if other_node != column:
                factor = (
                    factor * (targets - points[other_node]) / (points[column] - points[other_node])
                )
        columns.append(factor)
    return np.stack(columns, axis=1)


def refine_parts():
    lines = [refine_line(NP, upper) for upper in range(2)]
    plane = np.concatenate([np.kron(lines[k // 2], lines[k % 2]) for k in range(4)], axis=0).astype(np.float32)
    high = plane.astype(BF)
    low = (plane - high.astype(np.float32)).astype(BF)
    columns = [
        np.repeat(lines[upper][a, 2 * t : 2 * t + 2], 64) for upper in range(2) for a in range(8) for t in range(4)
    ]
    patterns = np.broadcast_to(np.stack(columns)[:, None, :], (64, 8, 128)).astype(np.float32)
    return np.concatenate([high, low], axis=1), np.concatenate([high, high], axis=1), patterns


_line = derivative_line(NP)
_line[0, 0] += lift_half
_line[7, 7] -= lift_half
ODD = 0.5 * (_line[:4, :4] - _line[:3:-1, :4])
EVEN = 0.5 * (_line[:4, :4] + _line[:3:-1, :4])


def line_product(x):
    odd = [x[a] - x[7 - a] for a in range(4)]
    even = [x[a] + x[7 - a] for a in range(4)]
    out = [None] * 8
    for m in range(4):
        p = sum(odd[a] * float(ODD[a, m]) for a in range(4))
        q = sum(even[a] * float(EVEN[a, m]) for a in range(4))
        out[m] = p + q
        out[7 - m] = p - q
    return out


def low_half():
    return lax.broadcasted_iota(jnp.int32, (8, 128), 1) < 64


def swap_halves(x):
    return pltpu.roll(x, 64, 1)


def lane_patterns():
    low = low_half()
    out = []
    for matrix in (ODD, EVEN):
        straight = [[None] * 2 for _ in range(2)]
        crossed = [[None] * 2 for _ in range(2)]
        for j in range(2):
            for m in range(2):
                straight[j][m] = jnp.where(low, float(matrix[2 * j, 2 * m]), float(matrix[2 * j + 1, 2 * m + 1]))
                crossed[j][m] = jnp.where(low, float(matrix[2 * j + 1, 2 * m]), float(matrix[2 * j, 2 * m + 1]))
        out.append((straight, crossed))
    return out


def lane_product(x, patterns):
    back = [swap_halves(x[3]), swap_halves(x[2])]
    sums = []
    for parts, (straight, crossed) in zip(
        ([x[0] - back[0], x[1] - back[1]], [x[0] + back[0], x[1] + back[1]]), patterns
    ):
        turned = [swap_halves(part) for part in parts]
        sums.append(
            [
                parts[0] * straight[0][m] + turned[0] * crossed[0][m] + parts[1] * straight[1][m] + turned[1] * crossed[1][m]
                for m in range(2)
            ]
        )
    p, q = sums
    return [p[0] + q[0], p[1] + q[1], swap_halves(p[1] - q[1]), swap_halves(p[0] - q[0])]


def split(x):
    high = x.astype(BF)
    return high, (x - high.astype(F32)).astype(BF)


def along(k, start=None):
    return pl.ds(k, 8, stride=8)


def image_rows(get, mat, direction):
    inv_density, lame, shear = mat
    trace = get(3) + get(4) + get(5)
    out = []
    for k in range(3):
        term = shear * get(voigt_index[direction][k])
        if k == direction:
            term = 2.0 * term + lame * trace
        out.append(term)
    return out + [inv_density * get(i) for i in range(3)]


def target_row(value, direction):
    return value if value < 3 else voigt_index[value - 3][direction]


def build_table(v_ref, mat, t_ref):
    low = low_half()

    def put(value, block, direction, x0, x1):
        pair = jnp.concatenate([x0, x1], axis=0)
        high, rest = split(pair)
        rows = pl.ds(value * 64 + block * 16, 16)
        t_ref[rows, pl.ds(direction * 128, 128)] = high
        t_ref[rows, pl.ds(LOCAL + direction * 128, 128)] = rest

    for direction in range(2):
        for j in range(4):
            if direction == 0:
                ends = [image_rows(lambda i, r=r: v_ref[i, j, pl.ds(r, 8), :], mat, 0) for r in (0, 56)]
            else:
                ends = [image_rows(lambda i, r=r: v_ref[i, j, along(r), :], mat, 1) for r in (0, 7)]
            for value in range(6):
                a0, a1 = ends[0][value], ends[1][value]
                put(
                    value,
                    j,
                    direction,
                    jnp.where(low, a0, swap_halves(a1)),
                    jnp.where(low, swap_halves(a0), a1),
                )
    for pair in range(4):
        blocks = []
        for b in (2 * pair, 2 * pair + 1):
            blocks.append(
                image_rows(
                    lambda i, b=b: jnp.where(
                        low, v_ref[i, 0, along(b), :], v_ref[i, 3, along(b), :]
                    ),
                    mat,
                    2,
                )
            )
        for value in range(6):
            put(value, pair, 2, blocks[0][value], blocks[1][value])


def materials(mat_ref):
    return mat_ref[0], mat_ref[1], mat_ref[2]


def send_values(send_ref, t_ref, out_refs):
    rows = lax.dot_general(
        send_ref[...], t_ref[...], (((1,), (1,)), ((), ())), preferred_element_type=F32
    )
    for k in range(4):
        out_refs[k][...] = rows[16 * k : 16 * k + 16]


def begin_kernel(
    adjoint_ref, material_ref, faces_ref, sides_ref,
    v_ref, mat_ref, t_ref, local_ref, remote_ref, send_ref, p0, p1, p2, p3,
    staged_ref, sem, turn_ref, small_ref,
):
    def fetch(i):
        return pltpu.make_async_copy(adjoint_ref.at[i], staged_ref.at[i], sem.at[i])

    for i in range(9):
        fetch(i).start()
    even_x = 1 - lax.axis_index("curve") % 2
    even_y = 1 - lax.axis_index("seg") % 2

    def lane(q):
        element = (q * 10923) >> 16
        return (q - 6 * element) * E_DEV + element

    for i in range(3):
        row = material_ref[pl.ds(i, 1), :]
        if i == 0:
            row = 1.0 / row
        mat_ref[i] = jnp.broadcast_to(jnp.concatenate([row, row], axis=1), (8, 128))
    small_ref[...] = jnp.zeros_like(small_ref)
    faces = faces_ref[...].astype(F32)
    small_ref[pl.ds(0, 64), pl.ds(0, 6)] = faces
    small_ref[pl.ds(64, 64), pl.ds(0, 6)] = faces
    turned = small_ref[...].T
    low_row = lax.broadcasted_iota(jnp.int32, (1, 128), 1) < 64
    weight = jnp.where(low_row, lift_half, -lift_half)
    for direction in range(3):
        q = jnp.where(
            low_row, turned[2 * direction : 2 * direction + 1], turned[2 * direction + 1 : 2 * direction + 2]
        ).astype(jnp.int32)
        remote = q - LOCAL
        side = remote >> 4
        block = side ^ jnp.where(side < 2, even_x, even_y)
        partner = jnp.where(remote < 0, lane(q), LOCAL + block * CAP + (remote & 15))
        lanes = pl.ds(direction * 128, 128)
        for start in range(0, LOCAL + 64, 64):
            source = lax.broadcasted_iota(jnp.int32, (64, 128), 0) + start
            hot = jnp.where(source == partner, weight, 0.0).astype(BF)
            for part in range(2):
                if start < LOCAL:
                    local_ref[pl.ds(part * LOCAL + start, 64), lanes] = hot
                else:
                    remote_ref[pl.ds(part * 64, 64), lanes] = hot
    small_ref[pl.ds(0, 4), pl.ds(0, CAP)] = sides_ref[0].astype(F32)
    turned = small_ref[...].T
    columns = [lane(turned[0:CAP, r : r + 1].astype(jnp.int32)) for r in range(4)]
    for axis, even in ((0, even_x), (1, even_y)):
        first, second = columns[2 * axis], columns[2 * axis + 1]
        for k, column in enumerate((first + even * (second - first), second + even * (first - second))):
            hot = jnp.where(
                lax.broadcasted_iota(jnp.int32, (CAP, LOCAL), 1) == column, 1.0, 0.0
            ).astype(BF)
            rows = pl.ds((2 * axis + k) * CAP, CAP)
            send_ref[rows, pl.ds(0, LOCAL)] = hot
            send_ref[rows, pl.ds(LOCAL, LOCAL)] = hot
    low = lax.broadcasted_iota(jnp.int32, (64, 128), 1) < 64

    def body(i, carry):
        fetch(i).wait()
        x = staged_ref[i]
        turn_ref[...] = jnp.concatenate([x, x], axis=0).T
        for j in range(4):
            v_ref[i, j] = jnp.where(
                low, turn_ref[pl.ds(2 * j, 64, stride=8), :], turn_ref[pl.ds(2 * j + 1, 64, stride=8), :]
            )
        return carry

    lax.fori_loop(0, 9, body, 0)
    build_table(v_ref, materials(mat_ref), t_ref)
    send_values(send_ref, t_ref, (p0, p1, p2, p3))


def first_volume_kernel(v_ref, t_ref, local_ref, mat_ref, vol_ref, part_ref):
    volume_kernel(v_ref, t_ref, local_ref, mat_ref, None, vol_ref, part_ref, None)


def volume_kernel(v_ref, t_ref, local_ref, mat_ref, acc_ref, vol_ref, part_ref, sum_ref):
    mat = materials(mat_ref)
    inv_density, lame, shear = mat

    def scaled(get, direction):
        out = []
        for k in range(3):
            if k == direction:
                out.append(
                    (k, [2.0 * shear * d + lame * (s0 + s1 + s2) for d, s0, s1, s2 in zip(get(3 + k), get(3), get(4), get(5))])
                )
            else:
                out.append((k, [shear * x for x in get(voigt_index[direction][k])]))
        for i in range(3):
            out.append((voigt_index[i][direction], [inv_density * x for x in get(i)]))
        return out

    def tiles(j, carry):
        for row, x in scaled(lambda i: [v_ref[i, j, along(b), :] for b in range(8)], 1):
            for b, y in enumerate(line_product(x)):
                vol_ref[row, j, along(b), :] = y
        for row, x in scaled(lambda i: [v_ref[i, j, pl.ds(8 * a, 8), :] for a in range(8)], 0):
            for a, y in enumerate(line_product(x)):
                if row not in (3, 7):
                    y = y + vol_ref[row, j, pl.ds(8 * a, 8), :]
                vol_ref[row, j, pl.ds(8 * a, 8), :] = y
        return carry

    lax.fori_loop(0, 4, tiles, 0)
    patterns = lane_patterns()

    def groups(a, carry):
        rows = pl.ds(pl.multiple_of(a * 8, 8), 8)
        for row, x in scaled(lambda i: [v_ref[i, j, rows, :] for j in range(4)], 2):
            for j, y in enumerate(lane_product(x, patterns)):
                if row != 5:
                    y = y + vol_ref[row, j, rows, :]
                vol_ref[row, j, rows, :] = y
        chunk = pl.ds(pl.multiple_of(a * 48, 16), 48)
        part_ref[chunk, :] = jnp.dot(t_ref[chunk, :], local_ref[...], preferred_element_type=F32)
        if sum_ref is not None:
            for i in range(9):
                for j in range(4):
                    sum_ref[i, j, rows, :] = acc_ref[i, j, rows, :] + v_ref[i, j, rows, :]
        return carry

    lax.fori_loop(0, 8, groups, 0, unroll=4)


def add_faces(vol_ref, part_ref, r_refs, remote_ref, factor, out_ref, face_ref):
    for i in range(9):
        out_ref[i] = vol_ref[i] * factor
    arrived = jnp.concatenate([r[...] for r in r_refs], axis=0).T
    both = jnp.concatenate(split(arrived), axis=1)
    face_ref[...] = (part_ref[...] + jnp.dot(both, remote_ref[...], preferred_element_type=F32)) * factor
    low = low_half()
    for direction in range(3):
        for value in range(6):
            row = target_row(value, direction)
            for j in range(4):
                x0 = face_ref[pl.ds(value * 64 + 16 * j, 8), pl.ds(direction * 128, 128)]
                x1 = face_ref[pl.ds(value * 64 + 16 * j + 8, 8), pl.ds(direction * 128, 128)]
                if direction < 2:
                    y0 = jnp.where(low, x0, swap_halves(x1))
                    y1 = jnp.where(low, swap_halves(x0), x1)
                    rows = (pl.ds(0, 8), pl.ds(56, 8)) if direction == 0 else (along(0), along(7))
                    out_ref[row, j, rows[0], :] += y0
                    out_ref[row, j, rows[1], :] += y1
                else:
                    for b, x in ((2 * j, x0), (2 * j + 1, x1)):
                        out_ref[row, 0, along(b), :] += jnp.where(low, x, 0.0)
                        out_ref[row, 3, along(b), :] += jnp.where(low, 0.0, x)


def finish_kernel(
    factor, vol_ref, part_ref, r0, r1, r2, r3, remote_ref, mat_ref, send_ref,
    v_ref, t_ref, p0, p1, p2, p3, face_ref,
):
    add_faces(vol_ref, part_ref, (r0, r1, r2, r3), remote_ref, factor, v_ref, face_ref)
    build_table(v_ref, materials(mat_ref), t_ref)
    send_values(send_ref, t_ref, (p0, p1, p2, p3))


def end_kernel(
    factor, keys_ref, vol_ref, part_ref, r0, r1, r2, r3, remote_ref, acc_ref, place_ref, wa_ref, wb_ref, lines_ref,
    total_ref, home_ref, away_ref, v_ref, face_ref, turn_ref, rows_ref, parent_ref,
):
    add_faces(vol_ref, part_ref, (r0, r1, r2, r3), remote_ref, factor, v_ref, face_ref)
    place = jnp.where(
        lax.broadcasted_iota(jnp.int32, (64, 128), 0) == place_ref[...], 1.0, 0.0
    ).astype(BF)
    wide = lax.broadcasted_iota(jnp.int32, (64, 128), 1) < 64
    low = low_half()

    def body(i, carry):
        for j in range(4):
            tile = acc_ref[i, j] + v_ref[i, j]
            total_ref[i, j] = tile
            high = tile.astype(BF).astype(F32)
            rest = tile - high
            turn_ref[pl.ds(2 * j, 64, stride=8), :] = jnp.where(wide, high, pltpu.roll(rest, 64, 1))
            turn_ref[pl.ds(2 * j + 1, 64, stride=8), :] = jnp.where(wide, pltpu.roll(high, 64, 1), rest)
        ranked = lax.dot_general(
            place, turn_ref[...].astype(BF), (((1,), (1,)), ((), ())), preferred_element_type=F32
        )
        for upper in range(2):
            for t in range(4):
                x = [ranked[8 * (4 * upper + k) : 8 * (4 * upper + k) + 8, 128 * t : 128 * t + 128] for k in range(4)]
                for pair in range(2):
                    x0, x1 = x[2 * pair], x[2 * pair + 1]
                    lanes = pl.ds(128 * pair, 128)
                    rows_ref[pl.ds(64 * upper + 16 * t, 8), lanes] = jnp.where(low, x0, swap_halves(x1))
                    rows_ref[pl.ds(64 * upper + 16 * t + 8, 8), lanes] = jnp.where(low, swap_halves(x0), x1)
        high, rest = split(rows_ref[...])
        plane = jnp.dot(high, wa_ref[...], preferred_element_type=F32)
        plane = plane + pltpu.roll(plane, 64, 1) + jnp.dot(rest, wb_ref[...], preferred_element_type=F32)
        for t in range(4):
            parent_ref[i, t] = sum(
                plane[8 * k : 8 * k + 8] * lines_ref[4 * k + t] for k in range(16)
            )
        return carry

    lax.fori_loop(0, 9, body, 0)
    home_ref[...] = jnp.zeros_like(home_ref)
    for g in range(P_DEV):
        key = keys_ref[g]

        @pl.when(key < P_DEV)
        def _():
            for i in range(9):
                for t in range(4):
                    home_ref[i, t, pl.ds(key, 1), :] = parent_ref[i, t, pl.ds(g, 1), :]

        @pl.when(key >= P_DEV)
        def _():
            owner = (key - P_DEV) // 2
            slot = (key - P_DEV) % 2
            for i in range(9):
                for t in range(4):
                    away_ref[owner, i, pl.ds(slot * 4 + t, 1), :] = parent_ref[i, t, pl.ds(g, 1), :]


def next_kernel(total_ref, next_ref, turn_ref):
    def body(i, carry):
        for j in range(4):
            tile = total_ref[i, j]
            turn_ref[pl.ds(2 * j, 64, stride=8), :] = tile
            turn_ref[pl.ds(2 * j + 1, 64, stride=8), :] = pltpu.roll(tile, 64, 1)
        next_ref[i] = turn_ref[...].T[:64]
        return carry

    lax.fori_loop(0, 9, body, 0)


def parent_kernel(table_ref, home_ref, arrived_ref, out_ref, block_ref, sem):
    def fetch(p):
        return pltpu.make_async_copy(arrived_ref.at[table_ref[0, p]], block_ref.at[p], sem.at[p])

    for p in range(P_DEV):

        @pl.when(table_ref[1, p] >= 0)
        def _():
            fetch(p).start()

    for i in range(9):
        for t in range(4):
            out_ref[i, :, pl.ds(128 * t, 128)] = home_ref[i, t]
    for p in range(P_DEV):
        slot = table_ref[1, p]

        @pl.when(slot >= 0)
        def _():
            fetch(p).wait()
            for i in range(9):
                for t in range(4):
                    out_ref[i, pl.ds(p, 1), pl.ds(128 * t, 128)] = block_ref[p, i, pl.ds(slot * 4 + t, 1), :]


def shape(*dims, dtype=F32):
    return jax.ShapeDtypeStruct(dims, dtype)


VMEM = pl.BlockSpec(memory_space=pltpu.VMEM)
SMEM = pl.BlockSpec(memory_space=pltpu.SMEM)
ANYWHERE = pl.BlockSpec(memory_space=pl.ANY)
HBM = pl.BlockSpec(memory_space=pltpu.HBM)


def call(kernel, outs, scratch=(), smem=(), hbm=(), anywhere=(), count=0, flops=10**8, traffic=6 * 10**6):
    return pl.pallas_call(
        kernel,
        out_shape=outs,
        in_specs=[
            SMEM if k in smem else HBM if k in hbm else ANYWHERE if k in anywhere else VMEM for k in range(count)
        ],
        out_specs=jax.tree.map(lambda _: VMEM, outs),
        scratch_shapes=list(scratch),
        compiler_params=pltpu.CompilerParams(vmem_limit_bytes=32 * 2**20),
        cost_estimate=pl.CostEstimate(flops=flops, bytes_accessed=traffic, transcendentals=0),
    )


def exchange_pairs():
    along_x = [[(k, (k + 1) % N_CURVE) for k in range(start, N_CURVE, 2)] for start in (0, 1)]
    along_y = [[(k, (k + 1) % N_SEG) for k in range(start, N_SEG, 2)] for start in (0, 1)]
    both = lambda pairs: pairs + [(b, a) for a, b in pairs]
    return [("curve", both(p)) for p in along_x] + [("seg", both(p)) for p in along_y]


def shards(adjoint, material, face_partner, send_faces, migration, children):
    own_seg = lax.axis_index("seg")
    owner, slot, octant = migration[0], migration[1], migration[2]
    key = jnp.where(owner == own_seg, slot, P_DEV + 2 * owner + slot)
    first = octant == 0
    rank = jnp.sum((first[:, None] & (key[:, None] < key[None, :])).astype(jnp.int32), axis=0)
    place = octant * P_DEV + rank
    place = jnp.concatenate([place, place]).reshape(1, 128)
    keys = jnp.sum(
        jnp.where(first[:, None] & (rank[:, None] == jnp.arange(P_DEV)[None, :]), key[:, None], 0), axis=0
    )
    source = jnp.stack([children[0], jnp.where(children[0] == own_seg, -1, children[1])])

    state = shape(9, 4, 64, 128)
    table = shape(LOCAL, 2 * LOCAL, dtype=BF)
    face_part = shape(LOCAL, LOCAL)
    payload = [shape(CAP, LOCAL)] * 4
    face_scratch = pltpu.VMEM((LOCAL, LOCAL), F32)
    turn = pltpu.VMEM((NODES, 128), F32)

    outs = call(
        begin_kernel,
        [state, shape(3, 8, 128), table]
        + [shape(2 * LOCAL, LOCAL, dtype=BF), shape(128, LOCAL, dtype=BF), shape(64, 2 * LOCAL, dtype=BF)]
        + payload,
        [pltpu.VMEM((9, E_DEV, NODES), F32), pltpu.SemaphoreType.DMA((9,)), turn, pltpu.VMEM((128, 128), F32)],
        hbm=(0,),
        count=4,
    )(adjoint, material, face_partner, send_faces)
    v, mat, t, local_hot, remote_hot, send_hot = outs[:6]
    out_going = outs[6:]
    pairs = exchange_pairs()
    for step in range(1, 5):
        arrived = [lax.ppermute(x, axis, p) for x, (axis, p) in zip(out_going, pairs)]
        if step == 1:
            vol, part = call(first_volume_kernel, [state, face_part], count=4)(v, t, local_hot, mat)
            acc = v
        else:
            vol, part, acc = call(volume_kernel, [state, face_part, state], count=5)(v, t, local_hot, mat, acc)
        factor = time_step / step
        if step < 4:
            outs = call(
                functools.partial(finish_kernel, factor), [state, table] + payload, [face_scratch], count=9
            )(vol, part, *arrived, remote_hot, mat, send_hot)
            v, t, out_going = outs[0], outs[1], outs[2:]
    wa, wb, lines = (jnp.asarray(x) for x in refine_parts())
    total, home, away = call(
        functools.partial(end_kernel, factor),
        [state, shape(9, 4, P_DEV, 128), shape(N_SEG, 9, 8, 128)],
        [
            pltpu.VMEM((9, 4, 64, 128), F32),
            face_scratch,
            turn,
            pltpu.VMEM((128, 256), F32),
            pltpu.VMEM((9, 4, 8, 128), F32),
        ],
        smem=(0,),
        count=13,
    )(keys, vol, part, *arrived, remote_hot, acc, place, wa, wb, lines)
    fetched = lax.all_to_all(away, "seg", split_axis=0, concat_axis=0, tiled=True)
    updated = call(next_kernel, [shape(9, E_DEV, NODES)], [turn], count=1)(total)[0]
    parents = call(
        parent_kernel,
        [shape(9, P_DEV, NODES)],
        [pltpu.VMEM((P_DEV, 9, 8, 128), F32), pltpu.SemaphoreType.DMA((P_DEV,))],
        smem=(0,),
        anywhere=(2,),
        count=3,
    )(source, home, fetched)[0]
    return (updated, parents)


def solution(mesh):
    in_specs = (
        P(None, ("curve", "seg"), None),
        P(None, ("curve", "seg")),
        P(("curve", "seg"), None),
        P(("curve", "seg"), None, None),
        P(None, ("curve", "seg")),
        P(None, ("curve", "seg")),
    )
    out_specs = (P(None, ("curve", "seg"), None), P(None, ("curve", "seg"), None))
    return jax.shard_map(shards, mesh=mesh, in_specs=in_specs, out_specs=out_specs, check_vma=False)
```

```python
import functools

import jax
import jax.numpy as jnp
import numpy as np
from jax import lax
from jax.experimental import pallas as pl
from jax.experimental.pallas import tpu as pltpu
from jax.sharding import PartitionSpec as P

NP = 8
NODES = 512
E_DEV = 64
CAP = 16
P_DEV = 8
N_CURVE = 8
N_SEG = 16
LOCAL = 6 * E_DEV

voigt_index = ((3, 8, 7), (8, 4, 6), (7, 6, 5))
time_step = 0.8 / (NP * NP)
lift_half = 0.25 * NP * (NP - 1)
BF = jnp.bfloat16
F32 = jnp.float32


def lobatto_nodes(edge_nodes):
    return -np.cos(np.pi * np.arange(edge_nodes) / (edge_nodes - 1))


def derivative_line(edge_nodes):
    points = lobatto_nodes(edge_nodes)
    node_ids = np.arange(edge_nodes)
    weight = np.where((node_ids == 0) | (node_ids == edge_nodes - 1), 2.0, 1.0)
    row_ids = node_ids[:, None]
    column_ids = node_ids[None, :]
    differ = points[:, None] - points[None, :]
    safe_gap = np.where(row_ids == column_ids, 1.0, differ)
    matrix = weight[:, None] / weight[None, :] * (-1.0) ** (row_ids + column_ids) / safe_gap
    matrix = np.where(row_ids == column_ids, 0.0, matrix)
    return matrix - np.eye(edge_nodes) * matrix.sum(axis=1)[:, None]


def refine_line(edge_nodes, upper):
    points = lobatto_nodes(edge_nodes)
    targets = (points + (2.0 * upper - 1.0)) / 2.0
    columns = []
    for column in range(edge_nodes):
        factor = np.ones(edge_nodes)
        for other_node in range(edge_nodes):
            if other_node != column:
                factor = (
                    factor * (targets - points[other_node]) / (points[column] - points[other_node])
                )
        columns.append(factor)
    return np.stack(columns, axis=1)


def refine_parts():
    lines = [refine_line(NP, upper) for upper in range(2)]
    plane = np.concatenate([np.kron(lines[k // 2], lines[k % 2]) for k in range(4)], axis=0).astype(np.float32)
    high = plane.astype(BF)
    low = (plane - high.astype(np.float32)).astype(BF)
    columns = [
        np.repeat(lines[upper][a, 2 * t : 2 * t + 2], 64) for upper in range(2) for a in range(8) for t in range(4)
    ]
    patterns = np.broadcast_to(np.stack(columns)[:, None, :], (64, 8, 128)).astype(np.float32)
    return np.concatenate([high, low], axis=1), np.concatenate([high, high], axis=1), patterns


_line = derivative_line(NP)
_line[0, 0] += lift_half
_line[7, 7] -= lift_half
ODD = 0.5 * (_line[:4, :4] - _line[:3:-1, :4])
EVEN = 0.5 * (_line[:4, :4] + _line[:3:-1, :4])


def line_product(x):
    odd = [x[a] - x[7 - a] for a in range(4)]
    even = [x[a] + x[7 - a] for a in range(4)]
    out = [None] * 8
    for m in range(4):
        p = sum(odd[a] * float(ODD[a, m]) for a in range(4))
        q = sum(even[a] * float(EVEN[a, m]) for a in range(4))
        out[m] = p + q
        out[7 - m] = p - q
    return out


def low_half():
    return lax.broadcasted_iota(jnp.int32, (8, 128), 1) < 64


def swap_halves(x):
    return pltpu.roll(x, 64, 1)


def lane_patterns():
    low = low_half()
    out = []
    for matrix in (ODD, EVEN):
        straight = [[None] * 2 for _ in range(2)]
        crossed = [[None] * 2 for _ in range(2)]
        for j in range(2):
            for m in range(2):
                straight[j][m] = jnp.where(low, float(matrix[2 * j, 2 * m]), float(matrix[2 * j + 1, 2 * m + 1]))
                crossed[j][m] = jnp.where(low, float(matrix[2 * j + 1, 2 * m]), float(matrix[2 * j, 2 * m + 1]))
        out.append((straight, crossed))
    return out


def lane_product(x, patterns):
    back = [swap_halves(x[3]), swap_halves(x[2])]
    sums = []
    for parts, (straight, crossed) in zip(
        ([x[0] - back[0], x[1] - back[1]], [x[0] + back[0], x[1] + back[1]]), patterns
    ):
        turned = [swap_halves(part) for part in parts]
        sums.append(
            [
                parts[0] * straight[0][m] + turned[0] * crossed[0][m] + parts[1] * straight[1][m] + turned[1] * crossed[1][m]
                for m in range(2)
            ]
        )
    p, q = sums
    return [p[0] + q[0], p[1] + q[1], swap_halves(p[1] - q[1]), swap_halves(p[0] - q[0])]


def split(x):
    high = x.astype(BF)
    return high, (x - high.astype(F32)).astype(BF)


def along(k, start=None):
    return pl.ds(k, 8, stride=8)


def image_rows(get, mat, direction):
    inv_density, lame, shear = mat
    trace = get(3) + get(4) + get(5)
    out = []
    for k in range(3):
        term = shear * get(voigt_index[direction][k])
        if k == direction:
            term = 2.0 * term + lame * trace
        out.append(term)
    return out + [inv_density * get(i) for i in range(3)]


def target_row(value, direction):
    return value if value < 3 else voigt_index[value - 3][direction]


def build_table(v_ref, mat, t_ref):
    low = low_half()

    def put(value, block, direction, x0, x1):
        pair = jnp.concatenate([x0, x1], axis=0)
        high, rest = split(pair)
        rows = pl.ds(value * 64 + block * 16, 16)
        t_ref[rows, pl.ds(direction * 128, 128)] = high
        t_ref[rows, pl.ds(LOCAL + direction * 128, 128)] = rest

    for direction in range(2):
        for j in range(4):
            if direction == 0:
                ends = [image_rows(lambda i, r=r: v_ref[i, j, pl.ds(r, 8), :], mat, 0) for r in (0, 56)]
            else:
                ends = [image_rows(lambda i, r=r: v_ref[i, j, along(r), :], mat, 1) for r in (0, 7)]
            for value in range(6):
                a0, a1 = ends[0][value], ends[1][value]
                put(
                    value,
                    j,
                    direction,
                    jnp.where(low, a0, swap_halves(a1)),
                    jnp.where(low, swap_halves(a0), a1),
                )
    for pair in range(4):
        blocks = []
        for b in (2 * pair, 2 * pair + 1):
            blocks.append(
                image_rows(
                    lambda i, b=b: jnp.where(
                        low, v_ref[i, 0, along(b), :], v_ref[i, 3, along(b), :]
                    ),
                    mat,
                    2,
                )
            )
        for value in range(6):
            put(value, pair, 2, blocks[0][value], blocks[1][value])


def materials(mat_ref):
    return mat_ref[0], mat_ref[1], mat_ref[2]


def send_values(send_ref, t_ref, out_refs):
    rows = lax.dot_general(
        send_ref[...], t_ref[...], (((1,), (1,)), ((), ())), preferred_element_type=F32
    )
    for k in range(4):
        out_refs[k][...] = rows[16 * k : 16 * k + 16]


def index_kernel(pack_ref, mat_ref, local_ref, remote_ref, send_ref, small_ref):
    even_x = 1 - lax.axis_index("curve") % 2
    even_y = 1 - lax.axis_index("seg") % 2

    def lane(q):
        element = (q * 10923) >> 16
        return (q - 6 * element) * E_DEV + element

    for i in range(3):
        row = pack_ref[pl.ds(i, 1), :]
        if i == 0:
            row = 1.0 / row
        mat_ref[i] = jnp.broadcast_to(row, (8, 128))
    low_row = lax.broadcasted_iota(jnp.int32, (1, 128), 1) < 64
    weight = jnp.where(low_row, lift_half, -lift_half)
    for direction in range(3):
        q = jnp.where(
            low_row, pack_ref[pl.ds(3 + 2 * direction, 1), :], pack_ref[pl.ds(4 + 2 * direction, 1), :]
        ).astype(jnp.int32)
        remote = q - LOCAL
        side = remote >> 4
        block = side ^ jnp.where(side < 2, even_x, even_y)
        partner = jnp.where(remote < 0, lane(q), LOCAL + block * CAP + (remote & 15))
        lanes = pl.ds(direction * 128, 128)
        for start in range(0, LOCAL + 64, 64):
            source = lax.broadcasted_iota(jnp.int32, (64, 128), 0) + start
            hot = jnp.where(source == partner, weight, 0.0).astype(BF)
            for part in range(2):
                if start < LOCAL:
                    local_ref[pl.ds(part * LOCAL + start, 64), lanes] = hot
                else:
                    remote_ref[pl.ds(part * 64, 64), lanes] = hot
    small_ref[pl.ds(0, 16), :] = pack_ref[...]
    small_ref[pl.ds(16, 112), :] = jnp.zeros((112, 128), F32)
    turned = small_ref[...].T
    columns = [lane(turned[0:CAP, 9 + r : 10 + r].astype(jnp.int32)) for r in range(4)]
    for axis, even in ((0, even_x), (1, even_y)):
        first, second = columns[2 * axis], columns[2 * axis + 1]
        for k, column in enumerate((first + even * (second - first), second + even * (first - second))):
            hot = jnp.where(
                lax.broadcasted_iota(jnp.int32, (CAP, LOCAL), 1) == column, 1.0, 0.0
            ).astype(BF)
            rows = pl.ds((2 * axis + k) * CAP, CAP)
            send_ref[rows, pl.ds(0, LOCAL)] = hot
            send_ref[rows, pl.ds(LOCAL, LOCAL)] = hot


def begin_kernel(adjoint_ref, mat_ref, send_ref, v_ref, t_ref, p0, p1, p2, p3, turn_ref):
    low = lax.broadcasted_iota(jnp.int32, (64, 128), 1) < 64
    for i in range(9):
        x = adjoint_ref[i]
        turn = turn_ref.at[i % 3]
        turn[...] = jnp.concatenate([x, x], axis=0).T
        for j in range(4):
            v_ref[i, j] = jnp.where(
                low, turn[pl.ds(2 * j, 64, stride=8), :], turn[pl.ds(2 * j + 1, 64, stride=8), :]
            )
    build_table(v_ref, materials(mat_ref), t_ref)
    send_values(send_ref, t_ref, (p0, p1, p2, p3))


def first_volume_kernel(v_ref, t_ref, local_ref, mat_ref, vol_ref, part_ref):
    volume_kernel(v_ref, t_ref, local_ref, mat_ref, None, vol_ref, part_ref, None)


def volume_kernel(v_ref, t_ref, local_ref, mat_ref, acc_ref, vol_ref, part_ref, sum_ref):
    mat = materials(mat_ref)
    inv_density, lame, shear = mat

    def scaled(get, direction):
        out = []
        for k in range(3):
            if k == direction:
                out.append(
                    (k, [2.0 * shear * d + lame * (s0 + s1 + s2) for d, s0, s1, s2 in zip(get(3 + k), get(3), get(4), get(5))])
                )
            else:
                out.append((k, [shear * x for x in get(voigt_index[direction][k])]))
        for i in range(3):
            out.append((voigt_index[i][direction], [inv_density * x for x in get(i)]))
        return out

    def tiles(j, carry):
        for row, x in scaled(lambda i: [v_ref[i, j, along(b), :] for b in range(8)], 1):
            for b, y in enumerate(line_product(x)):
                vol_ref[row, j, along(b), :] = y
        for row, x in scaled(lambda i: [v_ref[i, j, pl.ds(8 * a, 8), :] for a in range(8)], 0):
            for a, y in enumerate(line_product(x)):
                if row not in (3, 7):
                    y = y + vol_ref[row, j, pl.ds(8 * a, 8), :]
                vol_ref[row, j, pl.ds(8 * a, 8), :] = y
        return carry

    lax.fori_loop(0, 4, tiles, 0)
    patterns = lane_patterns()

    def groups(a, carry):
        rows = pl.ds(pl.multiple_of(a * 8, 8), 8)
        for row, x in scaled(lambda i: [v_ref[i, j, rows, :] for j in range(4)], 2):
            for j, y in enumerate(lane_product(x, patterns)):
                if row != 5:
                    y = y + vol_ref[row, j, rows, :]
                vol_ref[row, j, rows, :] = y
        chunk = pl.ds(pl.multiple_of(a * 48, 16), 48)
        part_ref[chunk, :] = jnp.dot(t_ref[chunk, :], local_ref[...], preferred_element_type=F32)
        if sum_ref is not None:
            for i in range(9):
                for j in range(4):
                    sum_ref[i, j, rows, :] = acc_ref[i, j, rows, :] + v_ref[i, j, rows, :]
        return carry

    lax.fori_loop(0, 8, groups, 0, unroll=4)


def add_faces(vol_ref, part_ref, r_refs, remote_ref, factor, out_ref, face_ref):
    for i in range(9):
        out_ref[i] = vol_ref[i] * factor
    arrived = jnp.concatenate([r[...] for r in r_refs], axis=0).T
    both = jnp.concatenate(split(arrived), axis=1)
    face_ref[...] = (part_ref[...] + jnp.dot(both, remote_ref[...], preferred_element_type=F32)) * factor
    low = low_half()
    for direction in range(3):
        for value in range(6):
            row = target_row(value, direction)
            for j in range(4):
                x0 = face_ref[pl.ds(value * 64 + 16 * j, 8), pl.ds(direction * 128, 128)]
                x1 = face_ref[pl.ds(value * 64 + 16 * j + 8, 8), pl.ds(direction * 128, 128)]
                if direction < 2:
                    y0 = jnp.where(low, x0, swap_halves(x1))
                    y1 = jnp.where(low, swap_halves(x0), x1)
                    rows = (pl.ds(0, 8), pl.ds(56, 8)) if direction == 0 else (along(0), along(7))
                    out_ref[row, j, rows[0], :] += y0
                    out_ref[row, j, rows[1], :] += y1
                else:
                    for b, x in ((2 * j, x0), (2 * j + 1, x1)):
                        out_ref[row, 0, along(b), :] += jnp.where(low, x, 0.0)
                        out_ref[row, 3, along(b), :] += jnp.where(low, 0.0, x)


def finish_kernel(
    factor, vol_ref, part_ref, r3, r2, r1, r0, remote_ref, mat_ref, send_ref,
    v_ref, t_ref, p0, p1, p2, p3, face_ref,
):
    add_faces(vol_ref, part_ref, (r0, r1, r2, r3), remote_ref, factor, v_ref, face_ref)
    build_table(v_ref, materials(mat_ref), t_ref)
    send_values(send_ref, t_ref, (p0, p1, p2, p3))


def end_kernel(
    factor, keys_ref, vol_ref, part_ref, r3, r2, r1, r0, remote_ref, acc_ref, place_ref, wa_ref, wb_ref, lines_ref,
    total_ref, home_ref, away_ref, v_ref, face_ref, turn_ref, ranked_ref, rows_ref, plane_ref, parent_ref,
):
    add_faces(vol_ref, part_ref, (r0, r1, r2, r3), remote_ref, factor, v_ref, face_ref)
    place = jnp.where(
        lax.broadcasted_iota(jnp.int32, (64, 128), 0) == place_ref[...], 1.0, 0.0
    ).astype(BF)
    wide = lax.broadcasted_iota(jnp.int32, (64, 128), 1) < 64
    low = low_half()
    for i in range(9):
        for j in range(4):
            tile = acc_ref[i, j] + v_ref[i, j]
            total_ref[i, j] = tile
            high = tile.astype(BF).astype(F32)
            rest = tile - high
            turn_ref[i, pl.ds(2 * j, 64, stride=8), :] = jnp.where(wide, high, pltpu.roll(rest, 64, 1))
            turn_ref[i, pl.ds(2 * j + 1, 64, stride=8), :] = jnp.where(wide, pltpu.roll(high, 64, 1), rest)
        ranked_ref[i] = lax.dot_general(
            place, turn_ref[i].astype(BF), (((1,), (1,)), ((), ())), preferred_element_type=F32
        )
    for i in range(9):
        for upper in range(2):
            for t in range(4):
                x = [ranked_ref[i, pl.ds(8 * (4 * upper + k), 8), pl.ds(128 * t, 128)] for k in range(4)]
                for pair in range(2):
                    x0, x1 = x[2 * pair], x[2 * pair + 1]
                    lanes = pl.ds(128 * pair, 128)
                    rows_ref[i, pl.ds(64 * upper + 16 * t, 8), lanes] = jnp.where(low, x0, swap_halves(x1))
                    rows_ref[i, pl.ds(64 * upper + 16 * t + 8, 8), lanes] = jnp.where(low, swap_halves(x0), x1)
        high, rest = split(rows_ref[i])
        plane = jnp.dot(high, wa_ref[...], preferred_element_type=F32)
        plane_ref[i] = plane + pltpu.roll(plane, 64, 1) + jnp.dot(rest, wb_ref[...], preferred_element_type=F32)
    for t in range(4):
        sums = [None] * 9
        for k in range(16):
            line = lines_ref[4 * k + t]
            for i in range(9):
                term = plane_ref[i, pl.ds(8 * k, 8), :] * line
                sums[i] = term if k == 0 else sums[i] + term
        for i in range(9):
            parent_ref[i, t] = sums[i]
    home_ref[...] = jnp.zeros_like(home_ref)
    for g in range(P_DEV):
        key = keys_ref[g]

        @pl.when(key < P_DEV)
        def _():
            for i in range(9):
                for t in range(4):
                    home_ref[i, t, pl.ds(key, 1), :] = parent_ref[i, t, pl.ds(g, 1), :]

        @pl.when(key >= P_DEV)
        def _():
            owner = (key - P_DEV) // 2
            slot = (key - P_DEV) % 2
            for i in range(9):
                for t in range(4):
                    away_ref[owner, i, pl.ds(slot * 4 + t, 1), :] = parent_ref[i, t, pl.ds(g, 1), :]


def next_kernel(total_ref, next_ref, turn_ref):
    def body(i, carry):
        for j in range(4):
            tile = total_ref[i, j]
            turn_ref[pl.ds(2 * j, 64, stride=8), :] = tile
            turn_ref[pl.ds(2 * j + 1, 64, stride=8), :] = pltpu.roll(tile, 64, 1)
        next_ref[i] = turn_ref[...].T[:64]
        return carry

    lax.fori_loop(0, 9, body, 0)


def parent_kernel(table_ref, home_ref, arrived_ref, out_ref):
    for i in range(9):
        for t in range(4):
            out_ref[i, :, pl.ds(128 * t, 128)] = home_ref[i, t]
    for p in range(P_DEV):
        holder = table_ref[0, p]
        slot = table_ref[1, p]

        @pl.when(slot >= 0)
        def _():
            for i in range(9):
                for t in range(4):
                    out_ref[i, pl.ds(p, 1), pl.ds(128 * t, 128)] = arrived_ref[
                        holder, i, pl.ds(slot * 4 + t, 1), :
                    ]


def shape(*dims, dtype=F32):
    return jax.ShapeDtypeStruct(dims, dtype)


VMEM = pl.BlockSpec(memory_space=pltpu.VMEM)
SMEM = pl.BlockSpec(memory_space=pltpu.SMEM)


def call(kernel, outs, scratch=(), smem=(), count=0, flops=10**8, traffic=6 * 10**6):
    return pl.pallas_call(
        kernel,
        out_shape=outs,
        in_specs=[SMEM if k in smem else VMEM for k in range(count)],
        out_specs=jax.tree.map(lambda _: VMEM, outs),
        scratch_shapes=list(scratch),
        compiler_params=pltpu.CompilerParams(vmem_limit_bytes=32 * 2**20),
        cost_estimate=pl.CostEstimate(flops=flops, bytes_accessed=traffic, transcendentals=0),
    )


def exchange_pairs():
    along_x = [[(k, (k + 1) % N_CURVE) for k in range(start, N_CURVE, 2)] for start in (0, 1)]
    along_y = [[(k, (k + 1) % N_SEG) for k in range(start, N_SEG, 2)] for start in (0, 1)]
    both = lambda pairs: pairs + [(b, a) for a, b in pairs]
    return [("curve", both(p)) for p in along_x] + [("seg", both(p)) for p in along_y]


def shards(adjoint, material, face_partner, send_faces, migration, children):
    own_seg = lax.axis_index("seg")
    owner, slot, octant = migration[0], migration[1], migration[2]
    key = jnp.where(owner == own_seg, slot, P_DEV + 2 * owner + slot)
    first = octant == 0
    rank = jnp.sum((first[:, None] & (key[:, None] < key[None, :])).astype(jnp.int32), axis=0)
    place = octant * P_DEV + rank
    place = jnp.concatenate([place, place]).reshape(1, 128)
    keys = jnp.sum(
        jnp.where(first[:, None] & (rank[:, None] == jnp.arange(P_DEV)[None, :]), key[:, None], 0), axis=0
    )
    source = jnp.stack([children[0], jnp.where(children[0] == own_seg, -1, children[1])])

    state = shape(9, 4, 64, 128)
    table = shape(LOCAL, 2 * LOCAL, dtype=BF)
    face_part = shape(LOCAL, LOCAL)
    payload = [shape(CAP, LOCAL)] * 4
    face_scratch = pltpu.VMEM((LOCAL, LOCAL), F32)
    turn = pltpu.VMEM((NODES, 128), F32)

    twice = lambda x: jnp.concatenate([x, x], axis=1)
    pack = jnp.concatenate(
        [
            twice(material),
            twice(face_partner.T.astype(F32)),
            jnp.pad(send_faces[0].astype(F32), ((0, 3), (0, 128 - CAP))),
        ],
        axis=0,
    )
    mat, local_hot, remote_hot, send_hot = call(
        index_kernel,
        [shape(3, 8, 128)]
        + [shape(2 * LOCAL, LOCAL, dtype=BF), shape(128, LOCAL, dtype=BF), shape(64, 2 * LOCAL, dtype=BF)],
        [pltpu.VMEM((128, 128), F32)],
        count=1,
        traffic=4 * 10**7,
    )(pack)
    outs = call(begin_kernel, [state, table] + payload, [pltpu.VMEM((3, NODES, 128), F32)], count=3)(
        adjoint, mat, send_hot
    )
    v, t, out_going = outs[0], outs[1], outs[2:]
    pairs = exchange_pairs()
    for step in range(1, 5):
        arrived = [lax.ppermute(out_going[k], *pairs[k]) for k in (3, 2, 1, 0)]
        if step == 1:
            vol, part = call(first_volume_kernel, [state, face_part], count=4)(v, t, local_hot, mat)
            acc = v
        else:
            vol, part, acc = call(volume_kernel, [state, face_part, state], count=5)(v, t, local_hot, mat, acc)
        factor = time_step / step
        if step < 4:
            outs = call(
                functools.partial(finish_kernel, factor), [state, table] + payload, [face_scratch], count=9
            )(vol, part, *arrived, remote_hot, mat, send_hot)
            v, t, out_going = outs[0], outs[1], outs[2:]
    wa, wb, lines = (jnp.asarray(x) for x in refine_parts())
    total, home, away = call(
        functools.partial(end_kernel, factor),
        [state, shape(9, 4, P_DEV, 128), shape(N_SEG, 9, 8, 128)],
        [
            pltpu.VMEM((9, 4, 64, 128), F32),
            face_scratch,
            pltpu.VMEM((9, NODES, 128), F32),
            pltpu.VMEM((9, 64, NODES), F32),
            pltpu.VMEM((9, 128, 256), F32),
            pltpu.VMEM((9, 128, 128), F32),
            pltpu.VMEM((9, 4, 8, 128), F32),
        ],
        smem=(0,),
        count=13,
    )(keys, vol, part, *arrived, remote_hot, acc, place, wa, wb, lines)
    fetched = lax.all_to_all(away, "seg", split_axis=0, concat_axis=0, tiled=True)
    updated = call(next_kernel, [shape(9, E_DEV, NODES)], [turn], count=1)(total)[0]
    parents = call(parent_kernel, [shape(9, P_DEV, NODES)], smem=(0,), count=3)(source, home, fetched)[0]
    return (updated, parents)


def solution(mesh):
    in_specs = (
        P(None, ("curve", "seg"), None),
        P(None, ("curve", "seg")),
        P(("curve", "seg"), None),
        P(("curve", "seg"), None, None),
        P(None, ("curve", "seg")),
        P(None, ("curve", "seg")),
    )
    out_specs = (P(None, ("curve", "seg"), None), P(None, ("curve", "seg"), None))
    return jax.shard_map(shards, mesh=mesh, in_specs=in_specs, out_specs=out_specs, check_vma=False)
```

```python
import functools

import jax
import jax.numpy as jnp
import numpy as np
from jax import lax
from jax.experimental import pallas as pl
from jax.experimental.pallas import tpu as pltpu
from jax.sharding import PartitionSpec as P

NP = 8
NODES = 512
E_DEV = 64
CAP = 16
P_DEV = 8
N_CURVE = 8
N_SEG = 16
LOCAL = 6 * E_DEV

voigt_index = ((3, 8, 7), (8, 4, 6), (7, 6, 5))
time_step = 0.8 / (NP * NP)
lift_half = 0.25 * NP * (NP - 1)
BF = jnp.bfloat16
F32 = jnp.float32


def lobatto_nodes(edge_nodes):
    return -np.cos(np.pi * np.arange(edge_nodes) / (edge_nodes - 1))


def derivative_line(edge_nodes):
    points = lobatto_nodes(edge_nodes)
    node_ids = np.arange(edge_nodes)
    weight = np.where((node_ids == 0) | (node_ids == edge_nodes - 1), 2.0, 1.0)
    row_ids = node_ids[:, None]
    column_ids = node_ids[None, :]
    differ = points[:, None] - points[None, :]
    safe_gap = np.where(row_ids == column_ids, 1.0, differ)
    matrix = weight[:, None] / weight[None, :] * (-1.0) ** (row_ids + column_ids) / safe_gap
    matrix = np.where(row_ids == column_ids, 0.0, matrix)
    return matrix - np.eye(edge_nodes) * matrix.sum(axis=1)[:, None]


def refine_line(edge_nodes, upper):
    points = lobatto_nodes(edge_nodes)
    targets = (points + (2.0 * upper - 1.0)) / 2.0
    columns = []
    for column in range(edge_nodes):
        factor = np.ones(edge_nodes)
        for other_node in range(edge_nodes):
            if other_node != column:
                factor = (
                    factor * (targets - points[other_node]) / (points[column] - points[other_node])
                )
        columns.append(factor)
    return np.stack(columns, axis=1)


def refine_parts():
    lines = [refine_line(NP, upper) for upper in range(2)]
    plane = np.concatenate([np.kron(lines[k // 2], lines[k % 2]) for k in range(4)], axis=0).astype(np.float32)
    high = plane.astype(BF)
    low = (plane - high.astype(np.float32)).astype(BF)
    columns = [
        np.repeat(lines[upper][a, 2 * t : 2 * t + 2], 64) for upper in range(2) for a in range(8) for t in range(4)
    ]
    patterns = np.broadcast_to(np.stack(columns)[:, None, :], (64, 8, 128)).astype(np.float32)
    return np.concatenate([high, low], axis=1), np.concatenate([high, high], axis=1), patterns


_line = derivative_line(NP)
_line[0, 0] += lift_half
_line[7, 7] -= lift_half
ODD = 0.5 * (_line[:4, :4] - _line[:3:-1, :4])
EVEN = 0.5 * (_line[:4, :4] + _line[:3:-1, :4])


def line_product(x):
    odd = [x[a] - x[7 - a] for a in range(4)]
    even = [x[a] + x[7 - a] for a in range(4)]
    out = [None] * 8
    for m in range(4):
        p = sum(odd[a] * float(ODD[a, m]) for a in range(4))
        q = sum(even[a] * float(EVEN[a, m]) for a in range(4))
        out[m] = p + q
        out[7 - m] = p - q
    return out


def low_half():
    return lax.broadcasted_iota(jnp.int32, (8, 128), 1) < 64


def swap_halves(x):
    return pltpu.roll(x, 64, 1)


def lane_patterns():
    low = low_half()
    out = []
    for matrix in (ODD, EVEN):
        straight = [[None] * 2 for _ in range(2)]
        crossed = [[None] * 2 for _ in range(2)]
        for j in range(2):
            for m in range(2):
                straight[j][m] = jnp.where(low, float(matrix[2 * j, 2 * m]), float(matrix[2 * j + 1, 2 * m + 1]))
                crossed[j][m] = jnp.where(low, float(matrix[2 * j + 1, 2 * m]), float(matrix[2 * j, 2 * m + 1]))
        out.append((straight, crossed))
    return out


def lane_product(x, patterns):
    back = [swap_halves(x[3]), swap_halves(x[2])]
    sums = []
    for parts, (straight, crossed) in zip(
        ([x[0] - back[0], x[1] - back[1]], [x[0] + back[0], x[1] + back[1]]), patterns
    ):
        turned = [swap_halves(part) for part in parts]
        sums.append(
            [
                parts[0] * straight[0][m] + turned[0] * crossed[0][m] + parts[1] * straight[1][m] + turned[1] * crossed[1][m]
                for m in range(2)
            ]
        )
    p, q = sums
    return [p[0] + q[0], p[1] + q[1], swap_halves(p[1] - q[1]), swap_halves(p[0] - q[0])]


def split(x):
    high = x.astype(BF)
    return high, (x - high.astype(F32)).astype(BF)


def along(k, start=None):
    return pl.ds(k, 8, stride=8)


def image_rows(get, mat, direction):
    inv_density, lame, shear = mat
    trace = get(3) + get(4) + get(5)
    out = []
    for k in range(3):
        term = shear * get(voigt_index[direction][k])
        if k == direction:
            term = 2.0 * term + lame * trace
        out.append(term)
    return out + [inv_density * get(i) for i in range(3)]


def target_row(value, direction):
    return value if value < 3 else voigt_index[value - 3][direction]


def build_table(v_ref, mat, t_ref):
    low = low_half()

    def put(value, block, direction, x0, x1):
        pair = jnp.concatenate([x0, x1], axis=0)
        high, rest = split(pair)
        rows = pl.ds(value * 64 + block * 16, 16)
        t_ref[rows, pl.ds(direction * 128, 128)] = high
        t_ref[rows, pl.ds(LOCAL + direction * 128, 128)] = rest

    for direction in range(2):
        for j in range(4):
            if direction == 0:
                ends = [image_rows(lambda i, r=r: v_ref[i, j, pl.ds(r, 8), :], mat, 0) for r in (0, 56)]
            else:
                ends = [image_rows(lambda i, r=r: v_ref[i, j, along(r), :], mat, 1) for r in (0, 7)]
            for value in range(6):
                a0, a1 = ends[0][value], ends[1][value]
                put(
                    value,
                    j,
                    direction,
                    jnp.where(low, a0, swap_halves(a1)),
                    jnp.where(low, swap_halves(a0), a1),
                )
    for pair in range(4):
        blocks = []
        for b in (2 * pair, 2 * pair + 1):
            blocks.append(
                image_rows(
                    lambda i, b=b: jnp.where(
                        low, v_ref[i, 0, along(b), :], v_ref[i, 3, along(b), :]
                    ),
                    mat,
                    2,
                )
            )
        for value in range(6):
            put(value, pair, 2, blocks[0][value], blocks[1][value])


def materials(mat_ref):
    return mat_ref[0], mat_ref[1], mat_ref[2]


def send_values(send_ref, t_ref, out_refs):
    rows = lax.dot_general(
        send_ref[...], t_ref[...], (((1,), (1,)), ((), ())), preferred_element_type=F32
    )
    for k in range(4):
        out_refs[k][...] = rows[16 * k : 16 * k + 16]


def parities():
    return 1 - lax.axis_index("curve") % 2, 1 - lax.axis_index("seg") % 2


def table_lane(q):
    element = (q * 10923) >> 16
    return (q - 6 * element) * E_DEV + element


def partner_tables(faces_ref, local_ref, remote_ref):
    even_x, even_y = parities()
    low_row = lax.broadcasted_iota(jnp.int32, (1, 128), 1) < 64
    weight = jnp.where(low_row, lift_half, -lift_half)
    for direction in range(3):
        q = jnp.where(
            low_row,
            faces_ref[pl.ds(2 * direction, 1), :],
            pltpu.roll(faces_ref[pl.ds(2 * direction + 1, 1), :], 64, 1),
        ).astype(jnp.int32)
        remote = q - LOCAL
        side = remote >> 4
        block = side ^ jnp.where(side < 2, even_x, even_y)
        partner = jnp.where(remote < 0, table_lane(q), LOCAL + block * CAP + (remote & 15))
        lanes = pl.ds(direction * 128, 128)
        for start in range(0, LOCAL + 64, 64):
            source = lax.broadcasted_iota(jnp.int32, (64, 128), 0) + start
            hot = jnp.where(source == partner, weight, 0.0).astype(BF)
            for part in range(2):
                if start < LOCAL:
                    local_ref[pl.ds(part * LOCAL + start, 64), lanes] = hot
                else:
                    remote_ref[pl.ds(part * 64, 64), lanes] = hot


def send_table(pack_ref, send_ref, small_ref):
    even_x, even_y = parities()
    small_ref[pl.ds(0, 8), :] = pack_ref[0]
    small_ref[pl.ds(8, 120), :] = jnp.zeros((120, 128), F32)
    turned = small_ref[...].T
    columns = [table_lane(turned[0:CAP, 3 + r : 4 + r].astype(jnp.int32)) for r in range(4)]
    for axis, even in ((0, even_x), (1, even_y)):
        first, second = columns[2 * axis], columns[2 * axis + 1]
        for k, column in enumerate((first + even * (second - first), second + even * (first - second))):
            hot = jnp.where(
                lax.broadcasted_iota(jnp.int32, (CAP, LOCAL), 1) == column, 1.0, 0.0
            ).astype(BF)
            rows = pl.ds((2 * axis + k) * CAP, CAP)
            send_ref[rows, pl.ds(0, LOCAL)] = hot
            send_ref[rows, pl.ds(LOCAL, LOCAL)] = hot


def begin_kernel(
    pack_ref, adjoint_ref, v_ref, t_ref, mat_ref, send_ref, p0, p1, p2, p3, turn_ref, small_ref
):
    low_row = lax.broadcasted_iota(jnp.int32, (1, 128), 1) < 64
    for i in range(3):
        row = pack_ref[0, pl.ds(i, 1), :]
        row = jnp.where(low_row, row, pltpu.roll(row, 64, 1))
        if i == 0:
            row = 1.0 / row
        mat_ref[i] = jnp.broadcast_to(row, (8, 128))
    send_table(pack_ref, send_ref, small_ref)
    low = lax.broadcasted_iota(jnp.int32, (64, 128), 1) < 64
    for i in range(9):
        x = adjoint_ref[i]
        turn = turn_ref.at[i % 3]
        turn[...] = jnp.concatenate([x, x], axis=0).T
        for j in range(4):
            v_ref[i, j] = jnp.where(
                low, turn[pl.ds(2 * j, 64, stride=8), :], turn[pl.ds(2 * j + 1, 64, stride=8), :]
            )
    build_table(v_ref, materials(mat_ref), t_ref)
    send_values(send_ref, t_ref, (p0, p1, p2, p3))


def first_volume_kernel(factor, faces_ref, v_ref, t_ref, mat_ref, vol_ref, part_ref, local_ref, remote_ref):
    partner_tables(faces_ref, local_ref, remote_ref)
    volume_kernel(factor, v_ref, t_ref, local_ref, mat_ref, None, vol_ref, part_ref, None)


def volume_kernel(factor, v_ref, t_ref, local_ref, mat_ref, acc_ref, vol_ref, part_ref, sum_ref):
    inv_density, lame, shear = [m * factor for m in materials(mat_ref)]

    def scaled(get, direction):
        out = []
        for k in range(3):
            if k == direction:
                out.append(
                    (k, [2.0 * shear * d + lame * (s0 + s1 + s2) for d, s0, s1, s2 in zip(get(3 + k), get(3), get(4), get(5))])
                )
            else:
                out.append((k, [shear * x for x in get(voigt_index[direction][k])]))
        for i in range(3):
            out.append((voigt_index[i][direction], [inv_density * x for x in get(i)]))
        return out

    def tiles(j):
        for row, x in scaled(lambda i: [v_ref[i, j, along(b), :] for b in range(8)], 1):
            for b, y in enumerate(line_product(x)):
                vol_ref[row, j, along(b), :] = y
        chunk = pl.ds(j * 96, 96)
        part_ref[chunk, :] = jnp.dot(t_ref[chunk, :], local_ref[...], preferred_element_type=F32) * factor
        for row, x in scaled(lambda i: [v_ref[i, j, pl.ds(8 * a, 8), :] for a in range(8)], 0):
            for a, y in enumerate(line_product(x)):
                if row not in (3, 7):
                    y = y + vol_ref[row, j, pl.ds(8 * a, 8), :]
                vol_ref[row, j, pl.ds(8 * a, 8), :] = y

    for j in range(4):
        tiles(j)
    patterns = lane_patterns()

    def groups(a, carry):
        rows = pl.ds(pl.multiple_of(a * 8, 8), 8)
        for row, x in scaled(lambda i: [v_ref[i, j, rows, :] for j in range(4)], 2):
            for j, y in enumerate(lane_product(x, patterns)):
                if row != 5:
                    y = y + vol_ref[row, j, rows, :]
                vol_ref[row, j, rows, :] = y
        if sum_ref is not None:
            for i in range(9):
                for j in range(4):
                    sum_ref[i, j, rows, :] = acc_ref[i, j, rows, :] + v_ref[i, j, rows, :]
        return carry

    lax.fori_loop(0, 8, groups, 0, unroll=4)


def add_faces(part_ref, r_refs, remote_ref, factor, out_ref, face_ref):
    arrived = jnp.concatenate([r[...] for r in r_refs], axis=0).T * factor
    both = jnp.concatenate(split(arrived), axis=1)
    face_ref[...] = part_ref[...] + jnp.dot(both, remote_ref[...], preferred_element_type=F32)
    low = low_half()
    for direction in range(3):
        for value in range(6):
            row = target_row(value, direction)
            for j in range(4):
                x0 = face_ref[pl.ds(value * 64 + 16 * j, 8), pl.ds(direction * 128, 128)]
                x1 = face_ref[pl.ds(value * 64 + 16 * j + 8, 8), pl.ds(direction * 128, 128)]
                if direction < 2:
                    y0 = jnp.where(low, x0, swap_halves(x1))
                    y1 = jnp.where(low, swap_halves(x0), x1)
                    rows = (pl.ds(0, 8), pl.ds(56, 8)) if direction == 0 else (along(0), along(7))
                    out_ref[row, j, rows[0], :] += y0
                    out_ref[row, j, rows[1], :] += y1
                else:
                    for b, x in ((2 * j, x0), (2 * j + 1, x1)):
                        out_ref[row, 0, along(b), :] += jnp.where(low, x, 0.0)
                        out_ref[row, 3, along(b), :] += jnp.where(low, 0.0, x)


def finish_kernel(
    factor, order, vol_ref, part_ref, ra, rb, rc, rd, remote_ref, mat_ref, send_ref,
    v_ref, t_ref, p0, p1, p2, p3, face_ref,
):
    add_faces(part_ref, in_order(order, (ra, rb, rc, rd)), remote_ref, factor, v_ref, face_ref)
    build_table(v_ref, materials(mat_ref), t_ref)
    send_values(send_ref, t_ref, (p0, p1, p2, p3))


def in_order(order, refs):
    return [refs[order.index(k)] for k in range(4)]


def end_kernel(
    factor, order, keys_ref, vol_ref, part_ref, ra, rb, rc, rd, remote_ref, acc_ref, place_ref, wa_ref, wb_ref, lines_ref,
    total_ref, home_ref, away_ref, face_ref, turn_ref, ranked_ref, rows_ref, plane_ref, parent_ref,
):
    add_faces(part_ref, in_order(order, (ra, rb, rc, rd)), remote_ref, factor, total_ref, face_ref)
    place = jnp.where(
        lax.broadcasted_iota(jnp.int32, (64, 128), 0) == place_ref[...], 1.0, 0.0
    ).astype(BF)
    wide = lax.broadcasted_iota(jnp.int32, (64, 128), 1) < 64
    low = low_half()
    for i in range(9):
        for j in range(4):
            tile = acc_ref[i, j] + total_ref[i, j]
            total_ref[i, j] = tile
            high = tile.astype(BF).astype(F32)
            rest = tile - high
            turn_ref[i, pl.ds(2 * j, 64, stride=8), :] = jnp.where(wide, high, pltpu.roll(rest, 64, 1))
            turn_ref[i, pl.ds(2 * j + 1, 64, stride=8), :] = jnp.where(wide, pltpu.roll(high, 64, 1), rest)
        ranked_ref[i] = lax.dot_general(
            place, turn_ref[i].astype(BF), (((1,), (1,)), ((), ())), preferred_element_type=F32
        )
    for i in range(9):
        for upper in range(2):
            for t in range(4):
                x = [ranked_ref[i, pl.ds(8 * (4 * upper + k), 8), pl.ds(128 * t, 128)] for k in range(4)]
                for pair in range(2):
                    x0, x1 = x[2 * pair], x[2 * pair + 1]
                    lanes = pl.ds(128 * pair, 128)
                    rows_ref[i, pl.ds(64 * upper + 16 * t, 8), lanes] = jnp.where(low, x0, swap_halves(x1))
                    rows_ref[i, pl.ds(64 * upper + 16 * t + 8, 8), lanes] = jnp.where(low, swap_halves(x0), x1)
        high, rest = split(rows_ref[i])
        plane = jnp.dot(high, wa_ref[...], preferred_element_type=F32)
        plane_ref[i] = plane + pltpu.roll(plane, 64, 1) + jnp.dot(rest, wb_ref[...], preferred_element_type=F32)
    for t in range(4):
        sums = [None] * 9
        for k in range(16):
            line = lines_ref[4 * k + t]
            for i in range(9):
                term = plane_ref[i, pl.ds(8 * k, 8), :] * line
                sums[i] = term if k == 0 else sums[i] + term
        for i in range(9):
            parent_ref[i, t] = sums[i]
    home_ref[...] = jnp.zeros_like(home_ref)
    for g in range(P_DEV):
        key = keys_ref[g]

        @pl.when(key < P_DEV)
        def _():
            for i in range(9):
                for t in range(4):
                    home_ref[i, t, pl.ds(key, 1), :] = parent_ref[i, t, pl.ds(g, 1), :]

        @pl.when(key >= P_DEV)
        def _():
            owner = (key - P_DEV) // 2
            slot = (key - P_DEV) % 2
            for i in range(9):
                for t in range(4):
                    away_ref[owner, i, pl.ds(slot * 4 + t, 1), :] = parent_ref[i, t, pl.ds(g, 1), :]


def next_kernel(total_ref, next_ref, turn_ref):
    def body(i, carry):
        for j in range(4):
            tile = total_ref[i, j]
            turn_ref[pl.ds(2 * j, 64, stride=8), :] = tile
            turn_ref[pl.ds(2 * j + 1, 64, stride=8), :] = pltpu.roll(tile, 64, 1)
        next_ref[i] = turn_ref[...].T[:64]
        return carry

    lax.fori_loop(0, 9, body, 0)


def parent_kernel(table_ref, home_ref, arrived_ref, out_ref):
    for i in range(9):
        for t in range(4):
            out_ref[i, :, pl.ds(128 * t, 128)] = home_ref[i, t]
    for p in range(P_DEV):
        holder = table_ref[0, p]
        slot = table_ref[1, p]

        @pl.when(slot >= 0)
        def _():
            for i in range(9):
                for t in range(4):
                    out_ref[i, pl.ds(p, 1), pl.ds(128 * t, 128)] = arrived_ref[
                        holder, i, pl.ds(slot * 4 + t, 1), :
                    ]


def shape(*dims, dtype=F32):
    return jax.ShapeDtypeStruct(dims, dtype)


VMEM = pl.BlockSpec(memory_space=pltpu.VMEM)
SMEM = pl.BlockSpec(memory_space=pltpu.SMEM)


def call(kernel, outs, scratch=(), smem=(), aliases={}, count=0, flops=10**8, traffic=6 * 10**6):
    return pl.pallas_call(
        kernel,
        out_shape=outs,
        in_specs=[SMEM if k in smem else VMEM for k in range(count)],
        out_specs=jax.tree.map(lambda _: VMEM, outs),
        scratch_shapes=list(scratch),
        input_output_aliases=aliases,
        compiler_params=pltpu.CompilerParams(vmem_limit_bytes=32 * 2**20),
        cost_estimate=pl.CostEstimate(flops=flops, bytes_accessed=traffic, transcendentals=0),
    )


def exchange_pairs():
    along_x = [[(k, (k + 1) % N_CURVE) for k in range(start, N_CURVE, 2)] for start in (0, 1)]
    along_y = [[(k, (k + 1) % N_SEG) for k in range(start, N_SEG, 2)] for start in (0, 1)]
    both = lambda pairs: pairs + [(b, a) for a, b in pairs]
    return [("curve", both(p)) for p in along_x] + [("seg", both(p)) for p in along_y]


def shards(adjoint, material, face_partner, send_faces, migration, children):
    own_seg = lax.axis_index("seg")
    owner, slot, octant = migration[0], migration[1], migration[2]
    key = jnp.where(owner == own_seg, slot, P_DEV + 2 * owner + slot)
    first = octant == 0
    rank = jnp.sum((first[:, None] & (key[:, None] < key[None, :])).astype(jnp.int32), axis=0)
    place = octant * P_DEV + rank
    place = jnp.concatenate([place, place]).reshape(1, 128)
    keys = jnp.sum(
        jnp.where(first[:, None] & (rank[:, None] == jnp.arange(P_DEV)[None, :]), key[:, None], 0), axis=0
    )
    source = jnp.stack([children[0], jnp.where(children[0] == own_seg, -1, children[1])])

    state = shape(9, 4, 64, 128)
    table = shape(LOCAL, 2 * LOCAL, dtype=BF)
    face_part = shape(LOCAL, LOCAL)
    payload = [shape(CAP, LOCAL)] * 4
    face_scratch = pltpu.VMEM((LOCAL, LOCAL), F32)
    turn = pltpu.VMEM((NODES, 128), F32)

    pack = jnp.concatenate(
        [
            jnp.pad(material[None], ((0, 0), (0, 0), (0, 64))),
            jnp.pad(send_faces, ((0, 0), (0, 1), (0, 128 - CAP))).astype(F32),
        ],
        axis=1,
    )
    faces = jnp.pad(face_partner.T.astype(F32), ((0, 2), (0, 64)))
    outs = call(
        begin_kernel,
        [state, table, shape(3, 8, 128), shape(64, 2 * LOCAL, dtype=BF)] + payload,
        [pltpu.VMEM((3, NODES, 128), F32), pltpu.VMEM((128, 128), F32)],
        count=2,
    )(pack, adjoint)
    v, t, mat, send_hot = outs[:4]
    out_going = outs[4:]
    pairs = exchange_pairs()
    for step in range(1, 5):
        factor = time_step / step
        order = (1, 0, 3, 2) if step == 3 else (3, 2, 1, 0)
        arrived = [lax.ppermute(out_going[k], *pairs[k]) for k in order]
        if step == 1:
            vol, part, local_hot, remote_hot = call(
                functools.partial(first_volume_kernel, factor),
                [state, face_part, shape(2 * LOCAL, LOCAL, dtype=BF), shape(128, LOCAL, dtype=BF)],
                count=4,
            )(faces, v, t, mat)
            acc = v
        else:
            vol, part, acc = call(
                functools.partial(volume_kernel, factor), [state, face_part, state], count=5
            )(v, t, local_hot, mat, acc)
        if step < 4:
            outs = call(
                functools.partial(finish_kernel, factor, order),
                [state, table] + payload,
                [face_scratch],
                aliases={0: 0},
                count=9,
            )(vol, part, *arrived, remote_hot, mat, send_hot)
            v, t, out_going = outs[0], outs[1], outs[2:]
    wa, wb, lines = (jnp.asarray(x) for x in refine_parts())
    total, home, away = call(
        functools.partial(end_kernel, factor, order),
        [state, shape(9, 4, P_DEV, 128), shape(N_SEG, 9, 8, 128)],
        [
            face_scratch,
            pltpu.VMEM((9, NODES, 128), F32),
            pltpu.VMEM((9, 64, NODES), F32),
            pltpu.VMEM((9, 128, 256), F32),
            pltpu.VMEM((9, 128, 128), F32),
            pltpu.VMEM((9, 4, 8, 128), F32),
        ],
        smem=(0,),
        aliases={1: 0},
        count=13,
    )(keys, vol, part, *arrived, remote_hot, acc, place, wa, wb, lines)
    fetched = lax.all_to_all(away, "seg", split_axis=0, concat_axis=0, tiled=True)
    updated = call(next_kernel, [shape(9, E_DEV, NODES)], [turn], count=1)(total)[0]
    parents = call(parent_kernel, [shape(9, P_DEV, NODES)], smem=(0,), count=3)(source, home, fetched)[0]
    return (updated, parents)


def solution(mesh):
    in_specs = (
        P(None, ("curve", "seg"), None),
        P(None, ("curve", "seg")),
        P(("curve", "seg"), None),
        P(("curve", "seg"), None, None),
        P(None, ("curve", "seg")),
        P(None, ("curve", "seg")),
    )
    out_specs = (P(None, ("curve", "seg"), None), P(None, ("curve", "seg"), None))
    return jax.shard_map(shards, mesh=mesh, in_specs=in_specs, out_specs=out_specs, check_vma=False)
```

```python
import functools

import jax
import jax.numpy as jnp
import numpy as np
from jax import lax
from jax.experimental import pallas as pl
from jax.experimental.pallas import tpu as pltpu
from jax.sharding import PartitionSpec as P

NP = 8
NODES = 512
E_DEV = 64
CAP = 16
P_DEV = 8
N_CURVE = 8
N_SEG = 16
LOCAL = 6 * E_DEV

voigt_index = ((3, 8, 7), (8, 4, 6), (7, 6, 5))
time_step = 0.8 / (NP * NP)
lift_half = 0.25 * NP * (NP - 1)
BF = jnp.bfloat16
F32 = jnp.float32


def lobatto_nodes(edge_nodes):
    return -np.cos(np.pi * np.arange(edge_nodes) / (edge_nodes - 1))


def derivative_line(edge_nodes):
    points = lobatto_nodes(edge_nodes)
    node_ids = np.arange(edge_nodes)
    weight = np.where((node_ids == 0) | (node_ids == edge_nodes - 1), 2.0, 1.0)
    row_ids = node_ids[:, None]
    column_ids = node_ids[None, :]
    differ = points[:, None] - points[None, :]
    safe_gap = np.where(row_ids == column_ids, 1.0, differ)
    matrix = weight[:, None] / weight[None, :] * (-1.0) ** (row_ids + column_ids) / safe_gap
    matrix = np.where(row_ids == column_ids, 0.0, matrix)
    return matrix - np.eye(edge_nodes) * matrix.sum(axis=1)[:, None]


def refine_line(edge_nodes, upper):
    points = lobatto_nodes(edge_nodes)
    targets = (points + (2.0 * upper - 1.0)) / 2.0
    columns = []
    for column in range(edge_nodes):
        factor = np.ones(edge_nodes)
        for other_node in range(edge_nodes):
            if other_node != column:
                factor = (
                    factor * (targets - points[other_node]) / (points[column] - points[other_node])
                )
        columns.append(factor)
    return np.stack(columns, axis=1)


def refine_parts():
    lines = [refine_line(NP, upper) for upper in range(2)]
    plane = np.concatenate([np.kron(lines[k // 2], lines[k % 2]) for k in range(4)], axis=0).astype(np.float32)
    high = plane.astype(BF)
    low = (plane - high.astype(np.float32)).astype(BF)
    columns = [
        np.repeat(lines[upper][a, 2 * t : 2 * t + 2], 64) for upper in range(2) for a in range(8) for t in range(4)
    ]
    patterns = np.broadcast_to(np.stack(columns)[:, None, :], (64, 8, 128)).astype(np.float32)
    return np.concatenate([high, low], axis=1), np.concatenate([high, high], axis=1), patterns


_line = derivative_line(NP)
_line[0, 0] += lift_half
_line[7, 7] -= lift_half
ODD = 0.5 * (_line[:4, :4] - _line[:3:-1, :4])
EVEN = 0.5 * (_line[:4, :4] + _line[:3:-1, :4])


def line_product(x):
    odd = [x[a] - x[7 - a] for a in range(4)]
    even = [x[a] + x[7 - a] for a in range(4)]
    out = [None] * 8
    for m in range(4):
        p = sum(odd[a] * float(ODD[a, m]) for a in range(4))
        q = sum(even[a] * float(EVEN[a, m]) for a in range(4))
        out[m] = p + q
        out[7 - m] = p - q
    return out


def low_half():
    return lax.broadcasted_iota(jnp.int32, (8, 128), 1) < 64


def swap_halves(x):
    return pltpu.roll(x, 64, 1)


def lane_patterns():
    low = low_half()
    out = []
    for matrix in (ODD, EVEN):
        straight = [[None] * 2 for _ in range(2)]
        crossed = [[None] * 2 for _ in range(2)]
        for j in range(2):
            for m in range(2):
                straight[j][m] = jnp.where(low, float(matrix[2 * j, 2 * m]), float(matrix[2 * j + 1, 2 * m + 1]))
                crossed[j][m] = jnp.where(low, float(matrix[2 * j + 1, 2 * m]), float(matrix[2 * j, 2 * m + 1]))
        out.append((straight, crossed))
    return out


def lane_product(x, patterns):
    back = [swap_halves(x[3]), swap_halves(x[2])]
    sums = []
    for parts, (straight, crossed) in zip(
        ([x[0] - back[0], x[1] - back[1]], [x[0] + back[0], x[1] + back[1]]), patterns
    ):
        turned = [swap_halves(part) for part in parts]
        sums.append(
            [
                parts[0] * straight[0][m] + turned[0] * crossed[0][m] + parts[1] * straight[1][m] + turned[1] * crossed[1][m]
                for m in range(2)
            ]
        )
    p, q = sums
    return [p[0] + q[0], p[1] + q[1], swap_halves(p[1] - q[1]), swap_halves(p[0] - q[0])]


def split(x):
    high = x.astype(BF)
    return high, (x - high.astype(F32)).astype(BF)


def along(k, start=None):
    return pl.ds(k, 8, stride=8)


def image_rows(get, mat, direction):
    inv_density, lame, shear = mat
    trace = get(3) + get(4) + get(5)
    out = []
    for k in range(3):
        term = shear * get(voigt_index[direction][k])
        if k == direction:
            term = 2.0 * term + lame * trace
        out.append(term)
    return out + [inv_density * get(i) for i in range(3)]


def target_row(value, direction):
    return value if value < 3 else voigt_index[value - 3][direction]


def build_table(v_ref, mat, t_ref):
    low = low_half()

    def put(value, block, direction, x0, x1):
        pair = jnp.concatenate([x0, x1], axis=0)
        high, rest = split(pair)
        rows = pl.ds(value * 64 + block * 16, 16)
        t_ref[rows, pl.ds(direction * 128, 128)] = high
        t_ref[rows, pl.ds(LOCAL + direction * 128, 128)] = rest

    for direction in range(2):
        for j in range(4):
            if direction == 0:
                ends = [image_rows(lambda i, r=r: v_ref[i, j, pl.ds(r, 8), :], mat, 0) for r in (0, 56)]
            else:
                ends = [image_rows(lambda i, r=r: v_ref[i, j, along(r), :], mat, 1) for r in (0, 7)]
            for value in range(6):
                a0, a1 = ends[0][value], ends[1][value]
                put(
                    value,
                    j,
                    direction,
                    jnp.where(low, a0, swap_halves(a1)),
                    jnp.where(low, swap_halves(a0), a1),
                )
    for pair in range(4):
        blocks = []
        for b in (2 * pair, 2 * pair + 1):
            blocks.append(
                image_rows(
                    lambda i, b=b: jnp.where(
                        low, v_ref[i, 0, along(b), :], v_ref[i, 3, along(b), :]
                    ),
                    mat,
                    2,
                )
            )
        for value in range(6):
            put(value, pair, 2, blocks[0][value], blocks[1][value])


def materials(mat_ref):
    return mat_ref[0], mat_ref[1], mat_ref[2]


def send_values(send_ref, t_ref, out_refs):
    rows = lax.dot_general(
        send_ref[...], t_ref[...], (((1,), (1,)), ((), ())), preferred_element_type=F32
    )
    for k in range(4):
        out_refs[k][...] = rows[16 * k : 16 * k + 16]


def parities():
    return 1 - lax.axis_index("curve") % 2, 1 - lax.axis_index("seg") % 2


def table_lane(q):
    element = (q * 10923) >> 16
    return (q - 6 * element) * E_DEV + element


def partner_tables(faces_ref, local_ref, remote_ref):
    even_x, even_y = parities()
    low_row = lax.broadcasted_iota(jnp.int32, (1, 128), 1) < 64
    weight = jnp.where(low_row, lift_half, -lift_half)
    for direction in range(3):
        q = jnp.where(
            low_row,
            faces_ref[pl.ds(2 * direction, 1), :],
            pltpu.roll(faces_ref[pl.ds(2 * direction + 1, 1), :], 64, 1),
        ).astype(jnp.int32)
        remote = q - LOCAL
        side = remote >> 4
        block = side ^ jnp.where(side < 2, even_x, even_y)
        partner = jnp.where(remote < 0, table_lane(q), LOCAL + block * CAP + (remote & 15))
        lanes = pl.ds(direction * 128, 128)
        for start in range(0, LOCAL + 64, 64):
            source = lax.broadcasted_iota(jnp.int32, (64, 128), 0) + start
            hot = jnp.where(source == partner, weight, 0.0).astype(BF)
            for part in range(2):
                if start < LOCAL:
                    local_ref[pl.ds(part * LOCAL + start, 64), lanes] = hot
                else:
                    remote_ref[pl.ds(part * 64, 64), lanes] = hot


def send_table(pack_ref, send_ref, small_ref):
    even_x, even_y = parities()
    small_ref[pl.ds(0, 8), :] = pack_ref[0]
    small_ref[pl.ds(8, 120), :] = jnp.zeros((120, 128), F32)
    turned = small_ref[...].T
    columns = [table_lane(turned[0:CAP, 3 + r : 4 + r].astype(jnp.int32)) for r in range(4)]
    for axis, even in ((0, even_x), (1, even_y)):
        first, second = columns[2 * axis], columns[2 * axis + 1]
        for k, column in enumerate((first + even * (second - first), second + even * (first - second))):
            hot = jnp.where(
                lax.broadcasted_iota(jnp.int32, (CAP, LOCAL), 1) == column, 1.0, 0.0
            ).astype(BF)
            rows = pl.ds((2 * axis + k) * CAP, CAP)
            send_ref[rows, pl.ds(0, LOCAL)] = hot
            send_ref[rows, pl.ds(LOCAL, LOCAL)] = hot


def begin_kernel(
    pack_ref, adjoint_ref, v_ref, t_ref, mat_ref, send_ref, p0, p1, p2, p3, turn_ref, small_ref
):
    low_row = lax.broadcasted_iota(jnp.int32, (1, 128), 1) < 64
    for i in range(3):
        row = pack_ref[0, pl.ds(i, 1), :]
        row = jnp.where(low_row, row, pltpu.roll(row, 64, 1))
        if i == 0:
            row = 1.0 / row
        mat_ref[i] = jnp.broadcast_to(row, (8, 128))
    send_table(pack_ref, send_ref, small_ref)
    low = lax.broadcasted_iota(jnp.int32, (64, 128), 1) < 64
    for i in range(9):
        x = adjoint_ref[i]
        turn = turn_ref.at[i % 3]
        turn[...] = jnp.concatenate([x, x], axis=0).T
        for j in range(4):
            v_ref[i, j] = jnp.where(
                low, turn[pl.ds(2 * j, 64, stride=8), :], turn[pl.ds(2 * j + 1, 64, stride=8), :]
            )
    build_table(v_ref, materials(mat_ref), t_ref)
    send_values(send_ref, t_ref, (p0, p1, p2, p3))


def first_volume_kernel(factor, faces_ref, v_ref, t_ref, mat_ref, vol_ref, part_ref, local_ref, remote_ref):
    partner_tables(faces_ref, local_ref, remote_ref)
    volume_kernel(factor, v_ref, t_ref, local_ref, mat_ref, None, vol_ref, part_ref, None)


def volume_kernel(factor, v_ref, t_ref, local_ref, mat_ref, acc_ref, vol_ref, part_ref, sum_ref):
    inv_density, lame, shear = [m * factor for m in materials(mat_ref)]

    def scaled(get, direction):
        out = []
        for k in range(3):
            if k == direction:
                out.append(
                    (k, [2.0 * shear * d + lame * (s0 + s1 + s2) for d, s0, s1, s2 in zip(get(3 + k), get(3), get(4), get(5))])
                )
            else:
                out.append((k, [shear * x for x in get(voigt_index[direction][k])]))
        for i in range(3):
            out.append((voigt_index[i][direction], [inv_density * x for x in get(i)]))
        return out

    def tiles(j):
        for row, x in scaled(lambda i: [v_ref[i, j, along(b), :] for b in range(8)], 1):
            for b, y in enumerate(line_product(x)):
                vol_ref[row, j, along(b), :] = y
        chunk = pl.ds(j * 96, 96)
        part_ref[chunk, :] = jnp.dot(t_ref[chunk, :], local_ref[...], preferred_element_type=F32) * factor
        for row, x in scaled(lambda i: [v_ref[i, j, pl.ds(8 * a, 8), :] for a in range(8)], 0):
            for a, y in enumerate(line_product(x)):
                if row not in (3, 7):
                    y = y + vol_ref[row, j, pl.ds(8 * a, 8), :]
                vol_ref[row, j, pl.ds(8 * a, 8), :] = y

    for j in range(4):
        tiles(j)
    patterns = lane_patterns()

    def groups(a, carry):
        rows = pl.ds(pl.multiple_of(a * 8, 8), 8)
        for row, x in scaled(lambda i: [v_ref[i, j, rows, :] for j in range(4)], 2):
            for j, y in enumerate(lane_product(x, patterns)):
                if row != 5:
                    y = y + vol_ref[row, j, rows, :]
                vol_ref[row, j, rows, :] = y
        if sum_ref is not None:
            for i in range(9):
                for j in range(4):
                    sum_ref[i, j, rows, :] = acc_ref[i, j, rows, :] + v_ref[i, j, rows, :]
        return carry

    lax.fori_loop(0, 8, groups, 0, unroll=4)


def add_faces(part_ref, r_refs, remote_ref, factor, out_ref, face_ref):
    arrived = jnp.concatenate([r[...] for r in r_refs], axis=0) * factor
    both = jnp.concatenate(split(arrived), axis=0)
    face_ref[...] = part_ref[...] + lax.dot_general(
        both, remote_ref[...], (((0,), (0,)), ((), ())), preferred_element_type=F32
    )
    low = low_half()
    for direction in range(3):
        for value in range(6):
            row = target_row(value, direction)
            for j in range(4):
                x0 = face_ref[pl.ds(value * 64 + 16 * j, 8), pl.ds(direction * 128, 128)]
                x1 = face_ref[pl.ds(value * 64 + 16 * j + 8, 8), pl.ds(direction * 128, 128)]
                if direction < 2:
                    y0 = jnp.where(low, x0, swap_halves(x1))
                    y1 = jnp.where(low, swap_halves(x0), x1)
                    rows = (pl.ds(0, 8), pl.ds(56, 8)) if direction == 0 else (along(0), along(7))
                    out_ref[row, j, rows[0], :] += y0
                    out_ref[row, j, rows[1], :] += y1
                else:
                    for b, x in ((2 * j, x0), (2 * j + 1, x1)):
                        out_ref[row, 0, along(b), :] += jnp.where(low, x, 0.0)
                        out_ref[row, 3, along(b), :] += jnp.where(low, 0.0, x)


def finish_kernel(
    factor, order, vol_ref, part_ref, ra, rb, rc, rd, remote_ref, mat_ref, send_ref,
    v_ref, t_ref, p0, p1, p2, p3, face_ref,
):
    add_faces(part_ref, in_order(order, (ra, rb, rc, rd)), remote_ref, factor, v_ref, face_ref)
    build_table(v_ref, materials(mat_ref), t_ref)
    send_values(send_ref, t_ref, (p0, p1, p2, p3))


def in_order(order, refs):
    return [refs[order.index(k)] for k in range(4)]


def end_kernel(
    factor, order, keys_ref, vol_ref, part_ref, ra, rb, rc, rd, remote_ref, acc_ref, place_ref, wa_ref, wb_ref, lines_ref,
    total_ref, parent_ref, away_ref, face_ref, turn_ref, ranked_ref, rows_ref, plane_ref,
):
    add_faces(part_ref, in_order(order, (ra, rb, rc, rd)), remote_ref, factor, total_ref, face_ref)
    place = jnp.where(
        lax.broadcasted_iota(jnp.int32, (64, 128), 0) == place_ref[...], 1.0, 0.0
    ).astype(BF)
    wide = lax.broadcasted_iota(jnp.int32, (64, 128), 1) < 64
    low = low_half()
    for i in range(9):
        for j in range(4):
            tile = acc_ref[i, j] + total_ref[i, j]
            total_ref[i, j] = tile
            high = tile.astype(BF).astype(F32)
            rest = tile - high
            turn_ref[i, pl.ds(2 * j, 64, stride=8), :] = jnp.where(wide, high, pltpu.roll(rest, 64, 1))
            turn_ref[i, pl.ds(2 * j + 1, 64, stride=8), :] = jnp.where(wide, pltpu.roll(high, 64, 1), rest)
        ranked_ref[i] = lax.dot_general(
            place, turn_ref[i].astype(BF), (((1,), (1,)), ((), ())), preferred_element_type=F32
        )
    for i in range(9):
        for upper in range(2):
            for t in range(4):
                x = [ranked_ref[i, pl.ds(8 * (4 * upper + k), 8), pl.ds(128 * t, 128)] for k in range(4)]
                for pair in range(2):
                    x0, x1 = x[2 * pair], x[2 * pair + 1]
                    lanes = pl.ds(128 * pair, 128)
                    rows_ref[i, pl.ds(64 * upper + 16 * t, 8), lanes] = jnp.where(low, x0, swap_halves(x1))
                    rows_ref[i, pl.ds(64 * upper + 16 * t + 8, 8), lanes] = jnp.where(low, swap_halves(x0), x1)
        high, rest = split(rows_ref[i])
        plane = jnp.dot(high, wa_ref[...], preferred_element_type=F32)
        plane_ref[i] = plane + pltpu.roll(plane, 64, 1) + jnp.dot(rest, wb_ref[...], preferred_element_type=F32)
    for t in range(4):
        sums = [None] * 9
        for k in range(16):
            line = lines_ref[4 * k + t]
            for i in range(9):
                term = plane_ref[i, pl.ds(8 * k, 8), :] * line
                sums[i] = term if k == 0 else sums[i] + term
        for i in range(9):
            parent_ref[i, t] = sums[i]
    for g in range(P_DEV):
        key = keys_ref[g]

        @pl.when(key >= P_DEV)
        def _():
            owner = (key - P_DEV) // 2
            slot = (key - P_DEV) % 2
            for i in range(9):
                for t in range(4):
                    away_ref[owner, i, pl.ds(slot * 4 + t, 1), :] = parent_ref[i, t, pl.ds(g, 1), :]


def next_kernel(total_ref, next_ref, turn_ref):
    def body(i, carry):
        for j in range(4):
            tile = total_ref[i, j]
            turn_ref[pl.ds(2 * j, 64, stride=8), :] = tile
            turn_ref[pl.ds(2 * j + 1, 64, stride=8), :] = pltpu.roll(tile, 64, 1)
        next_ref[i] = turn_ref[...].T[:64]
        return carry

    lax.fori_loop(0, 9, body, 0)


def parent_kernel(table_ref, groups_ref, arrived_ref, out_ref):
    for p in range(P_DEV):
        holder = table_ref[0, p]
        slot = table_ref[1, p]

        @pl.when(slot < 0)
        def _():
            for i in range(9):
                for t in range(4):
                    out_ref[i, pl.ds(p, 1), pl.ds(128 * t, 128)] = groups_ref[i, t, pl.ds(holder, 1), :]

        @pl.when(slot >= 0)
        def _():
            for i in range(9):
                for t in range(4):
                    out_ref[i, pl.ds(p, 1), pl.ds(128 * t, 128)] = arrived_ref[
                        holder, i, pl.ds(slot * 4 + t, 1), :
                    ]


def shape(*dims, dtype=F32):
    return jax.ShapeDtypeStruct(dims, dtype)


VMEM = pl.BlockSpec(memory_space=pltpu.VMEM)
SMEM = pl.BlockSpec(memory_space=pltpu.SMEM)


def call(kernel, outs, scratch=(), smem=(), aliases={}, count=0, flops=10**8, traffic=6 * 10**6):
    return pl.pallas_call(
        kernel,
        out_shape=outs,
        in_specs=[SMEM if k in smem else VMEM for k in range(count)],
        out_specs=jax.tree.map(lambda _: VMEM, outs),
        scratch_shapes=list(scratch),
        input_output_aliases=aliases,
        compiler_params=pltpu.CompilerParams(vmem_limit_bytes=32 * 2**20),
        cost_estimate=pl.CostEstimate(flops=flops, bytes_accessed=traffic, transcendentals=0),
    )


def exchange_pairs():
    along_x = [[(k, (k + 1) % N_CURVE) for k in range(start, N_CURVE, 2)] for start in (0, 1)]
    along_y = [[(k, (k + 1) % N_SEG) for k in range(start, N_SEG, 2)] for start in (0, 1)]
    both = lambda pairs: pairs + [(b, a) for a, b in pairs]
    return [("curve", both(p)) for p in along_x] + [("seg", both(p)) for p in along_y]


def shards(adjoint, material, face_partner, send_faces, migration, children):
    own_seg = lax.axis_index("seg")
    owner, slot, octant = migration[0], migration[1], migration[2]
    key = jnp.where(owner == own_seg, slot, P_DEV + 2 * owner + slot)
    first = octant == 0
    rank = jnp.sum((first[:, None] & (key[:, None] < key[None, :])).astype(jnp.int32), axis=0)
    place = octant * P_DEV + rank
    place = jnp.concatenate([place, place]).reshape(1, 128)
    keys = jnp.sum(
        jnp.where(first[:, None] & (rank[:, None] == jnp.arange(P_DEV)[None, :]), key[:, None], 0), axis=0
    )
    stays = children[0] == own_seg
    group = jnp.sum((keys[:, None] < jnp.arange(P_DEV)[None, :]).astype(jnp.int32), axis=0)
    source = jnp.stack([jnp.where(stays, group, children[0]), jnp.where(stays, -1, children[1])])

    state = shape(9, 4, 64, 128)
    table = shape(LOCAL, 2 * LOCAL, dtype=BF)
    face_part = shape(LOCAL, LOCAL)
    payload = [shape(CAP, LOCAL)] * 4
    face_scratch = pltpu.VMEM((LOCAL, LOCAL), F32)
    turn = pltpu.VMEM((NODES, 128), F32)

    zero = jnp.float32(0)
    pack = lax.pad(material[None], zero, ((0, 0, 0), (0, 5, 0), (0, 64, 0))) + lax.pad(
        send_faces, jnp.int32(0), ((0, 0, 0), (3, 1, 0), (0, 128 - CAP, 0))
    ).astype(F32)
    faces = jnp.pad(face_partner.T.astype(F32), ((0, 2), (0, 64)))
    outs = call(
        begin_kernel,
        [state, table, shape(3, 8, 128), shape(64, 2 * LOCAL, dtype=BF)] + payload,
        [pltpu.VMEM((3, NODES, 128), F32), pltpu.VMEM((128, 128), F32)],
        count=2,
    )(pack, adjoint)
    v, t, mat, send_hot = outs[:4]
    out_going = outs[4:]
    pairs = exchange_pairs()
    for step in range(1, 5):
        factor = time_step / step
        order = (1, 0, 3, 2) if step == 3 else (3, 2, 1, 0)
        arrived = [lax.ppermute(out_going[k], *pairs[k]) for k in order]
        if step == 1:
            vol, part, local_hot, remote_hot = call(
                functools.partial(first_volume_kernel, factor),
                [state, face_part, shape(2 * LOCAL, LOCAL, dtype=BF), shape(128, LOCAL, dtype=BF)],
                count=4,
            )(faces, v, t, mat)
            acc = v
        else:
            vol, part, acc = call(
                functools.partial(volume_kernel, factor), [state, face_part, state], count=5
            )(v, t, local_hot, mat, acc)
        if step < 4:
            outs = call(
                functools.partial(finish_kernel, factor, order),
                [state, table] + payload,
                [face_scratch],
                aliases={0: 0},
                count=9,
            )(vol, part, *arrived, remote_hot, mat, send_hot)
            v, t, out_going = outs[0], outs[1], outs[2:]
    wa, wb, lines = (jnp.asarray(x) for x in refine_parts())
    total, groups, away = call(
        functools.partial(end_kernel, factor, order),
        [state, shape(9, 4, P_DEV, 128), shape(N_SEG, 9, 8, 128)],
        [
            face_scratch,
            pltpu.VMEM((9, NODES, 128), F32),
            pltpu.VMEM((9, 64, NODES), F32),
            pltpu.VMEM((9, 128, 256), F32),
            pltpu.VMEM((9, 128, 128), F32),
        ],
        smem=(0,),
        aliases={1: 0},
        count=13,
    )(keys, vol, part, *arrived, remote_hot, acc, place, wa, wb, lines)
    fetched = lax.all_to_all(away, "seg", split_axis=0, concat_axis=0, tiled=True)
    updated = call(next_kernel, [shape(9, E_DEV, NODES)], [turn], count=1)(total)[0]
    parents = call(parent_kernel, [shape(9, P_DEV, NODES)], smem=(0,), count=3)(source, groups, fetched)[0]
    return (updated, parents)


def solution(mesh):
    in_specs = (
        P(None, ("curve", "seg"), None),
        P(None, ("curve", "seg")),
        P(("curve", "seg"), None),
        P(("curve", "seg"), None, None),
        P(None, ("curve", "seg")),
        P(None, ("curve", "seg")),
    )
    out_specs = (P(None, ("curve", "seg"), None), P(None, ("curve", "seg"), None))
    return jax.shard_map(shards, mesh=mesh, in_specs=in_specs, out_specs=out_specs, check_vma=False)
```

```python
import functools

import jax
import jax.numpy as jnp
import numpy as np
from jax import lax
from jax.experimental import pallas as pl
from jax.experimental.pallas import tpu as pltpu
from jax.sharding import PartitionSpec as P

NP = 8
NODES = 512
E_DEV = 64
CAP = 16
P_DEV = 8
N_CURVE = 8
N_SEG = 16
LOCAL = 6 * E_DEV

voigt_index = ((3, 8, 7), (8, 4, 6), (7, 6, 5))
time_step = 0.8 / (NP * NP)
lift_half = 0.25 * NP * (NP - 1)
BF = jnp.bfloat16
F32 = jnp.float32


def lobatto_nodes(edge_nodes):
    return -np.cos(np.pi * np.arange(edge_nodes) / (edge_nodes - 1))


def derivative_line(edge_nodes):
    points = lobatto_nodes(edge_nodes)
    node_ids = np.arange(edge_nodes)
    weight = np.where((node_ids == 0) | (node_ids == edge_nodes - 1), 2.0, 1.0)
    row_ids = node_ids[:, None]
    column_ids = node_ids[None, :]
    differ = points[:, None] - points[None, :]
    safe_gap = np.where(row_ids == column_ids, 1.0, differ)
    matrix = weight[:, None] / weight[None, :] * (-1.0) ** (row_ids + column_ids) / safe_gap
    matrix = np.where(row_ids == column_ids, 0.0, matrix)
    return matrix - np.eye(edge_nodes) * matrix.sum(axis=1)[:, None]


def refine_line(edge_nodes, upper):
    points = lobatto_nodes(edge_nodes)
    targets = (points + (2.0 * upper - 1.0)) / 2.0
    columns = []
    for column in range(edge_nodes):
        factor = np.ones(edge_nodes)
        for other_node in range(edge_nodes):
            if other_node != column:
                factor = (
                    factor * (targets - points[other_node]) / (points[column] - points[other_node])
                )
        columns.append(factor)
    return np.stack(columns, axis=1)


def refine_parts():
    lines = [refine_line(NP, upper) for upper in range(2)]
    plane = np.concatenate([np.kron(lines[k // 2], lines[k % 2]) for k in range(4)], axis=0).astype(np.float32)
    high = plane.astype(BF)
    low = (plane - high.astype(np.float32)).astype(BF)
    columns = [
        np.repeat(lines[upper][a, 2 * t : 2 * t + 2], 64) for upper in range(2) for a in range(8) for t in range(4)
    ]
    patterns = np.broadcast_to(np.stack(columns)[:, None, :], (64, 8, 128)).astype(np.float32)
    return np.concatenate([high, low], axis=1), np.concatenate([high, high], axis=1), patterns


_line = derivative_line(NP)
_line[0, 0] += lift_half
_line[7, 7] -= lift_half
ODD = 0.5 * (_line[:4, :4] - _line[:3:-1, :4])
EVEN = 0.5 * (_line[:4, :4] + _line[:3:-1, :4])


def line_product(x):
    odd = [x[a] - x[7 - a] for a in range(4)]
    even = [x[a] + x[7 - a] for a in range(4)]
    out = [None] * 8
    for m in range(4):
        p = sum(odd[a] * float(ODD[a, m]) for a in range(4))
        q = sum(even[a] * float(EVEN[a, m]) for a in range(4))
        out[m] = p + q
        out[7 - m] = p - q
    return out


def low_half():
    return lax.broadcasted_iota(jnp.int32, (8, 128), 1) < 64


def swap_halves(x):
    return pltpu.roll(x, 64, 1)


def lane_patterns():
    low = low_half()
    out = []
    for matrix in (ODD, EVEN):
        straight = [[None] * 2 for _ in range(2)]
        crossed = [[None] * 2 for _ in range(2)]
        for j in range(2):
            for m in range(2):
                straight[j][m] = jnp.where(low, float(matrix[2 * j, 2 * m]), float(matrix[2 * j + 1, 2 * m + 1]))
                crossed[j][m] = jnp.where(low, float(matrix[2 * j + 1, 2 * m]), float(matrix[2 * j, 2 * m + 1]))
        out.append((straight, crossed))
    return out


def lane_product(x, patterns):
    back = [swap_halves(x[3]), swap_halves(x[2])]
    sums = []
    for parts, (straight, crossed) in zip(
        ([x[0] - back[0], x[1] - back[1]], [x[0] + back[0], x[1] + back[1]]), patterns
    ):
        turned = [swap_halves(part) for part in parts]
        sums.append(
            [
                parts[0] * straight[0][m] + turned[0] * crossed[0][m] + parts[1] * straight[1][m] + turned[1] * crossed[1][m]
                for m in range(2)
            ]
        )
    p, q = sums
    return [p[0] + q[0], p[1] + q[1], swap_halves(p[1] - q[1]), swap_halves(p[0] - q[0])]


def split(x):
    high = x.astype(BF)
    return high, (x - high.astype(F32)).astype(BF)


def along(k, start=None):
    return pl.ds(k, 8, stride=8)


def image_rows(get, mat, direction):
    inv_density, lame, shear = mat
    trace = get(3) + get(4) + get(5)
    out = []
    for k in range(3):
        term = shear * get(voigt_index[direction][k])
        if k == direction:
            term = 2.0 * term + lame * trace
        out.append(term)
    return out + [inv_density * get(i) for i in range(3)]


def target_row(value, direction):
    return value if value < 3 else voigt_index[value - 3][direction]


def build_table(v_ref, mat, t_ref, directions):
    low = low_half()

    def put(value, block, direction, x0, x1):
        pair = jnp.concatenate([x0, x1], axis=0)
        high, rest = split(pair)
        rows = pl.ds(value * 64 + block * 16, 16)
        column = 256 * directions.index(direction)
        t_ref[rows, pl.ds(column, 128)] = high
        t_ref[rows, pl.ds(column + 128, 128)] = rest

    for direction in directions:
        if direction == 2:
            continue
        for j in range(4):
            if direction == 0:
                ends = [image_rows(lambda i, r=r: v_ref[i, j, pl.ds(r, 8), :], mat, 0) for r in (0, 56)]
            else:
                ends = [image_rows(lambda i, r=r: v_ref[i, j, along(r), :], mat, 1) for r in (0, 7)]
            for value in range(6):
                a0, a1 = ends[0][value], ends[1][value]
                put(
                    value,
                    j,
                    direction,
                    jnp.where(low, a0, swap_halves(a1)),
                    jnp.where(low, swap_halves(a0), a1),
                )
    for pair in range(4 if 2 in directions else 0):
        blocks = []
        for b in (2 * pair, 2 * pair + 1):
            blocks.append(
                image_rows(
                    lambda i, b=b: jnp.where(
                        low, v_ref[i, 0, along(b), :], v_ref[i, 3, along(b), :]
                    ),
                    mat,
                    2,
                )
            )
        for value in range(6):
            put(value, pair, 2, blocks[0][value], blocks[1][value])


def materials(mat_ref):
    return mat_ref[0], mat_ref[1], mat_ref[2]


def send_values(send_ref, t_ref, out_refs):
    rows = lax.dot_general(
        send_ref[...], t_ref[:, pl.ds(0, 256)], (((1,), (1,)), ((), ())), preferred_element_type=F32
    )
    for k in range(2):
        out_refs[k][...] = rows[16 * k : 16 * k + 16]


def parities():
    return 1 - lax.axis_index("curve") % 2, 1 - lax.axis_index("seg") % 2


def table_lane(q):
    element = (q * 10923) >> 16
    return (q - 6 * element) * E_DEV + element


def partner_tables(faces_ref, local_y_ref, local_ref, remote_ref):
    even_x, even_y = parities()
    low_row = lax.broadcasted_iota(jnp.int32, (1, 128), 1) < 64
    weight = jnp.where(low_row, lift_half, -lift_half)
    for direction in range(3):
        q = jnp.where(
            low_row,
            faces_ref[pl.ds(2 * direction, 1), :],
            pltpu.roll(faces_ref[pl.ds(2 * direction + 1, 1), :], 64, 1),
        ).astype(jnp.int32)
        remote = q - LOCAL
        side = remote >> 4
        block = side ^ jnp.where(side < 2, even_x, even_y)
        partner = jnp.where(remote < 0, table_lane(q), LOCAL + block * CAP + (remote & 15))
        lanes = pl.ds(direction * 128, 128)
        for start in range(0, LOCAL + 64, 64):
            source = lax.broadcasted_iota(jnp.int32, (64, 128), 0) + start
            hot = jnp.where(source == partner, weight, 0.0).astype(BF)
            target = (local_ref, local_y_ref, local_ref, remote_ref)[start // 128]
            base = start % 128 + (256 if start // 128 == 2 else 0)
            gap = 64 if start == LOCAL else 128
            for part in range(2):
                target[pl.ds(base + part * gap, 64), lanes] = hot


def send_table(pack_ref, send_x_ref, send_y_ref, small_ref):
    even_x, even_y = parities()
    small_ref[pl.ds(0, 8), :] = pack_ref[0]
    small_ref[pl.ds(8, 120), :] = jnp.zeros((120, 128), F32)
    turned = small_ref[...].T
    columns = [table_lane(turned[0:CAP, 3 + r : 4 + r].astype(jnp.int32)) for r in range(4)]
    for axis, even in ((0, even_x), (1, even_y)):
        first, second = columns[2 * axis], columns[2 * axis + 1]
        for k, column in enumerate((first + even * (second - first), second + even * (first - second))):
            hot = jnp.where(
                lax.broadcasted_iota(jnp.int32, (CAP, 128), 1) + 128 * axis == column, 1.0, 0.0
            ).astype(BF)
            for part in range(2):
                (send_x_ref, send_y_ref)[axis][pl.ds(k * CAP, CAP), pl.ds(128 * part, 128)] = hot


def begin_kernel(
    pack_ref, adjoint_ref,
    v_ref, ty_ref, t_ref, mat_ref, send_x_ref, send_y_ref, p0, p1, p2, p3, turn_ref, small_ref,
):
    low_row = lax.broadcasted_iota(jnp.int32, (1, 128), 1) < 64
    for i in range(3):
        row = pack_ref[0, pl.ds(i, 1), :]
        row = jnp.where(low_row, row, pltpu.roll(row, 64, 1))
        if i == 0:
            row = 1.0 / row
        mat_ref[i] = jnp.broadcast_to(row, (8, 128))
    send_table(pack_ref, send_x_ref, send_y_ref, small_ref)
    low = lax.broadcasted_iota(jnp.int32, (64, 128), 1) < 64
    for i in range(9):
        x = adjoint_ref[i]
        turn = turn_ref.at[i % 3]
        turn[...] = jnp.concatenate([x, x], axis=0).T
        for j in range(4):
            v_ref[i, j] = jnp.where(
                low, turn[pl.ds(2 * j, 64, stride=8), :], turn[pl.ds(2 * j + 1, 64, stride=8), :]
            )
    build_table(v_ref, materials(mat_ref), ty_ref, (1,))
    send_values(send_y_ref, ty_ref, (p2, p3))
    build_table(v_ref, materials(mat_ref), t_ref, (0, 2))
    send_values(send_x_ref, t_ref, (p0, p1))


def first_volume_kernel(
    factor, faces_ref, v_ref, ty_ref, t_ref, mat_ref, vol_ref, part_ref, local_y_ref, local_ref, remote_ref
):
    partner_tables(faces_ref, local_y_ref, local_ref, remote_ref)
    volume_kernel(factor, v_ref, ty_ref, t_ref, local_y_ref, local_ref, mat_ref, None, vol_ref, part_ref, None)


def last_volume_kernel(factor, v_ref, ty_ref, t_ref, local_y_ref, local_ref, mat_ref, acc_ref, vol_ref, part_ref):
    volume_kernel(factor, v_ref, ty_ref, t_ref, local_y_ref, local_ref, mat_ref, acc_ref, vol_ref, part_ref, None)


def volume_kernel(
    factor, v_ref, ty_ref, t_ref, local_y_ref, local_ref, mat_ref, acc_ref, vol_ref, part_ref, sum_ref
):
    inv_density, lame, shear = [m * factor for m in materials(mat_ref)]

    def scaled(get, direction):
        out = []
        for k in range(3):
            if k == direction:
                out.append(
                    (k, [2.0 * shear * d + lame * (s0 + s1 + s2) for d, s0, s1, s2 in zip(get(3 + k), get(3), get(4), get(5))])
                )
            else:
                out.append((k, [shear * x for x in get(voigt_index[direction][k])]))
        for i in range(3):
            out.append((voigt_index[i][direction], [inv_density * x for x in get(i)]))
        return out

    def tiles(j):
        for row, x in scaled(lambda i: [v_ref[i, j, along(b), :] for b in range(8)], 1):
            for b, y in enumerate(line_product(x)):
                vol_ref[row, j, along(b), :] = y
        chunk = pl.ds(j * 96, 96)
        part_ref[chunk, :] = factor * (
            jnp.dot(ty_ref[chunk, :], local_y_ref[...], preferred_element_type=F32)
            + jnp.dot(t_ref[chunk, :], local_ref[...], preferred_element_type=F32)
        )
        for row, x in scaled(lambda i: [v_ref[i, j, pl.ds(8 * a, 8), :] for a in range(8)], 0):
            for a, y in enumerate(line_product(x)):
                if row not in (3, 7):
                    y = y + vol_ref[row, j, pl.ds(8 * a, 8), :]
                vol_ref[row, j, pl.ds(8 * a, 8), :] = y

    for j in range(4):
        tiles(j)
    patterns = lane_patterns()

    def groups(a, carry):
        rows = pl.ds(pl.multiple_of(a * 8, 8), 8)
        for row, x in scaled(lambda i: [v_ref[i, j, rows, :] for j in range(4)], 2):
            for j, y in enumerate(lane_product(x, patterns)):
                if row != 5:
                    y = y + vol_ref[row, j, rows, :]
                vol_ref[row, j, rows, :] = y
        if acc_ref is not None:
            for i in range(9):
                for j in range(4):
                    y = acc_ref[i, j, rows, :] + v_ref[i, j, rows, :]
                    if sum_ref is not None:
                        sum_ref[i, j, rows, :] = y
                    else:
                        vol_ref[i, j, rows, :] += y
        return carry

    lax.fori_loop(0, 8, groups, 0, unroll=4)


def add_faces(part_ref, r_refs, remote_ref, factor, out_ref, face_ref):
    arrived = jnp.concatenate([r[...] for r in r_refs], axis=0) * factor
    both = jnp.concatenate(split(arrived), axis=0)
    face_ref[...] = part_ref[...] + lax.dot_general(
        both, remote_ref[...], (((0,), (0,)), ((), ())), preferred_element_type=F32
    )
    low = low_half()
    for direction in range(3):
        for value in range(6):
            row = target_row(value, direction)
            for j in range(4):
                x0 = face_ref[pl.ds(value * 64 + 16 * j, 8), pl.ds(direction * 128, 128)]
                x1 = face_ref[pl.ds(value * 64 + 16 * j + 8, 8), pl.ds(direction * 128, 128)]
                if direction < 2:
                    y0 = jnp.where(low, x0, swap_halves(x1))
                    y1 = jnp.where(low, swap_halves(x0), x1)
                    rows = (pl.ds(0, 8), pl.ds(56, 8)) if direction == 0 else (along(0), along(7))
                    out_ref[row, j, rows[0], :] += y0
                    out_ref[row, j, rows[1], :] += y1
                else:
                    for b, x in ((2 * j, x0), (2 * j + 1, x1)):
                        out_ref[row, 0, along(b), :] += jnp.where(low, x, 0.0)
                        out_ref[row, 3, along(b), :] += jnp.where(low, 0.0, x)


def finish_kernel(
    factor, order, vol_ref, part_ref, ra, rb, rc, rd, remote_ref, mat_ref, send_x_ref, send_y_ref,
    v_ref, ty_ref, t_ref, p0, p1, p2, p3, face_ref,
):
    add_faces(part_ref, in_order(order, (ra, rb, rc, rd)), remote_ref, factor, v_ref, face_ref)
    build_table(v_ref, materials(mat_ref), ty_ref, (1,))
    send_values(send_y_ref, ty_ref, (p2, p3))
    build_table(v_ref, materials(mat_ref), t_ref, (0, 2))
    send_values(send_x_ref, t_ref, (p0, p1))


def in_order(order, refs):
    return [refs[order.index(k)] for k in range(4)]


def end_kernel(
    factor, order, keys_ref, vol_ref, part_ref, ra, rb, rc, rd, remote_ref, place_ref, wa_ref, wb_ref, lines_ref,
    total_ref, parent_ref, away_ref, face_ref, turn_ref, ranked_ref, rows_ref, plane_ref,
):
    add_faces(part_ref, in_order(order, (ra, rb, rc, rd)), remote_ref, factor, total_ref, face_ref)
    place = jnp.where(
        lax.broadcasted_iota(jnp.int32, (64, 128), 0) == place_ref[...], 1.0, 0.0
    ).astype(BF)
    wide = lax.broadcasted_iota(jnp.int32, (64, 128), 1) < 64
    low = low_half()
    for i in range(9):
        for j in range(4):
            tile = total_ref[i, j]
            high = tile.astype(BF).astype(F32)
            rest = tile - high
            turn_ref[i, pl.ds(2 * j, 64, stride=8), :] = jnp.where(wide, high, pltpu.roll(rest, 64, 1))
            turn_ref[i, pl.ds(2 * j + 1, 64, stride=8), :] = jnp.where(wide, pltpu.roll(high, 64, 1), rest)
        ranked_ref[i] = lax.dot_general(
            place, turn_ref[i].astype(BF), (((1,), (1,)), ((), ())), preferred_element_type=F32
        )
    for i in range(9):
        for upper in range(2):
            for t in range(4):
                x = [ranked_ref[i, pl.ds(8 * (4 * upper + k), 8), pl.ds(128 * t, 128)] for k in range(4)]
                for pair in range(2):
                    x0, x1 = x[2 * pair], x[2 * pair + 1]
                    lanes = pl.ds(128 * pair, 128)
                    rows_ref[i, pl.ds(64 * upper + 16 * t, 8), lanes] = jnp.where(low, x0, swap_halves(x1))
                    rows_ref[i, pl.ds(64 * upper + 16 * t + 8, 8), lanes] = jnp.where(low, swap_halves(x0), x1)
        high, rest = split(rows_ref[i])
        plane = jnp.dot(high, wa_ref[...], preferred_element_type=F32)
        plane_ref[i] = plane + pltpu.roll(plane, 64, 1) + jnp.dot(rest, wb_ref[...], preferred_element_type=F32)
    for t in range(4):
        sums = [None] * 9
        for k in range(16):
            line = lines_ref[4 * k + t]
            for i in range(9):
                term = plane_ref[i, pl.ds(8 * k, 8), :] * line
                sums[i] = term if k == 0 else sums[i] + term
        for i in range(9):
            parent_ref[i, t] = sums[i]
    for g in range(P_DEV):
        key = keys_ref[g]

        @pl.when(key >= P_DEV)
        def _():
            owner = (key - P_DEV) // 2
            slot = (key - P_DEV) % 2
            for i in range(9):
                for t in range(4):
                    away_ref[owner, i, pl.ds(slot * 4 + t, 1), :] = parent_ref[i, t, pl.ds(g, 1), :]


def next_kernel(total_ref, next_ref, turn_ref):
    def body(i, carry):
        for j in range(4):
            tile = total_ref[i, j]
            turn_ref[pl.ds(2 * j, 64, stride=8), :] = tile
            turn_ref[pl.ds(2 * j + 1, 64, stride=8), :] = pltpu.roll(tile, 64, 1)
        next_ref[i] = turn_ref[...].T[:64]
        return carry

    lax.fori_loop(0, 9, body, 0)


def parent_kernel(table_ref, groups_ref, arrived_ref, out_ref):
    for p in range(P_DEV):
        holder = table_ref[0, p]
        slot = table_ref[1, p]

        @pl.when(slot < 0)
        def _():
            for i in range(9):
                for t in range(4):
                    out_ref[i, pl.ds(p, 1), pl.ds(128 * t, 128)] = groups_ref[i, t, pl.ds(holder, 1), :]

        @pl.when(slot >= 0)
        def _():
            for i in range(9):
                for t in range(4):
                    out_ref[i, pl.ds(p, 1), pl.ds(128 * t, 128)] = arrived_ref[
                        holder, i, pl.ds(slot * 4 + t, 1), :
                    ]


def shape(*dims, dtype=F32):
    return jax.ShapeDtypeStruct(dims, dtype)


VMEM = pl.BlockSpec(memory_space=pltpu.VMEM)
SMEM = pl.BlockSpec(memory_space=pltpu.SMEM)


def call(kernel, outs, scratch=(), smem=(), aliases={}, count=0, flops=10**8, traffic=6 * 10**6):
    return pl.pallas_call(
        kernel,
        out_shape=outs,
        in_specs=[SMEM if k in smem else VMEM for k in range(count)],
        out_specs=jax.tree.map(lambda _: VMEM, outs),
        scratch_shapes=list(scratch),
        input_output_aliases=aliases,
        compiler_params=pltpu.CompilerParams(vmem_limit_bytes=32 * 2**20),
        cost_estimate=pl.CostEstimate(flops=flops, bytes_accessed=traffic, transcendentals=0),
    )


def exchange_pairs():
    along_x = [[(k, (k + 1) % N_CURVE) for k in range(start, N_CURVE, 2)] for start in (0, 1)]
    along_y = [[(k, (k + 1) % N_SEG) for k in range(start, N_SEG, 2)] for start in (0, 1)]
    both = lambda pairs: pairs + [(b, a) for a, b in pairs]
    return [("curve", both(p)) for p in along_x] + [("seg", both(p)) for p in along_y]


def shards(adjoint, material, face_partner, send_faces, migration, children):
    own_seg = lax.axis_index("seg")
    owner, slot, octant = migration[0], migration[1], migration[2]
    key = jnp.where(owner == own_seg, slot, P_DEV + 2 * owner + slot)
    first = octant == 0
    rank = jnp.sum((first[:, None] & (key[:, None] < key[None, :])).astype(jnp.int32), axis=0)
    place = octant * P_DEV + rank
    place = jnp.concatenate([place, place]).reshape(1, 128)
    keys = jnp.sum(
        jnp.where(first[:, None] & (rank[:, None] == jnp.arange(P_DEV)[None, :]), key[:, None], 0), axis=0
    )
    stays = children[0] == own_seg
    group = jnp.sum((keys[:, None] < jnp.arange(P_DEV)[None, :]).astype(jnp.int32), axis=0)
    source = jnp.stack([jnp.where(stays, group, children[0]), jnp.where(stays, -1, children[1])])

    state = shape(9, 4, 64, 128)
    table_y = shape(LOCAL, 256, dtype=BF)
    table = shape(LOCAL, 512, dtype=BF)
    sent = shape(32, 256, dtype=BF)
    face_part = shape(LOCAL, LOCAL)
    payload = [shape(CAP, LOCAL)] * 4
    face_scratch = pltpu.VMEM((LOCAL, LOCAL), F32)
    turn = pltpu.VMEM((NODES, 128), F32)

    zero = jnp.float32(0)
    pack = lax.pad(material[None], zero, ((0, 0, 0), (0, 5, 0), (0, 64, 0))) + lax.pad(
        send_faces, jnp.int32(0), ((0, 0, 0), (3, 1, 0), (0, 128 - CAP, 0))
    ).astype(F32)
    faces = jnp.pad(face_partner.T.astype(F32), ((0, 2), (0, 64)))
    outs = call(
        begin_kernel,
        [state, table_y, table, shape(3, 8, 128), sent, sent] + payload,
        [pltpu.VMEM((3, NODES, 128), F32), pltpu.VMEM((128, 128), F32)],
        count=2,
    )(pack, adjoint)
    v, ty, t, mat, send_x, send_y = outs[:6]
    out_going = outs[6:]
    pairs = exchange_pairs()
    for step in range(1, 5):
        factor = time_step / step
        order = (1, 0, 3, 2) if step == 3 else (3, 2, 1, 0)
        arrived = [lax.ppermute(out_going[k], *pairs[k]) for k in order]
        if step == 1:
            vol, part, local_y, local, remote_hot = call(
                functools.partial(first_volume_kernel, factor),
                [
                    state,
                    face_part,
                    shape(256, LOCAL, dtype=BF),
                    shape(512, LOCAL, dtype=BF),
                    shape(128, LOCAL, dtype=BF),
                ],
                count=5,
            )(faces, v, ty, t, mat)
            acc = v
        elif step < 4:
            vol, part, acc = call(
                functools.partial(volume_kernel, factor), [state, face_part, state], count=7
            )(v, ty, t, local_y, local, mat, acc)
        else:
            vol, part = call(functools.partial(last_volume_kernel, factor), [state, face_part], count=7)(
                v, ty, t, local_y, local, mat, acc
            )
        if step < 4:
            outs = call(
                functools.partial(finish_kernel, factor, order),
                [state, table_y, table] + payload,
                [face_scratch],
                aliases={0: 0},
                count=10,
            )(vol, part, *arrived, remote_hot, mat, send_x, send_y)
            v, ty, t, out_going = outs[0], outs[1], outs[2], outs[3:]
    wa, wb, lines = (jnp.asarray(x) for x in refine_parts())
    total, groups, away = call(
        functools.partial(end_kernel, factor, order),
        [state, shape(9, 4, P_DEV, 128), shape(N_SEG, 9, 8, 128)],
        [
            face_scratch,
            pltpu.VMEM((9, NODES, 128), F32),
            pltpu.VMEM((9, 64, NODES), F32),
            pltpu.VMEM((9, 128, 256), F32),
            pltpu.VMEM((9, 128, 128), F32),
        ],
        smem=(0,),
        aliases={1: 0},
        count=12,
    )(keys, vol, part, *arrived, remote_hot, place, wa, wb, lines)
    fetched = lax.all_to_all(away, "seg", split_axis=0, concat_axis=0, tiled=True)
    updated = call(next_kernel, [shape(9, E_DEV, NODES)], [turn], count=1)(total)[0]
    parents = call(parent_kernel, [shape(9, P_DEV, NODES)], smem=(0,), count=3)(source, groups, fetched)[0]
    return (updated, parents)


def solution(mesh):
    in_specs = (
        P(None, ("curve", "seg"), None),
        P(None, ("curve", "seg")),
        P(("curve", "seg"), None),
        P(("curve", "seg"), None, None),
        P(None, ("curve", "seg")),
        P(None, ("curve", "seg")),
    )
    out_specs = (P(None, ("curve", "seg"), None), P(None, ("curve", "seg"), None))
    return jax.shard_map(shards, mesh=mesh, in_specs=in_specs, out_specs=out_specs, check_vma=False)
```

```python
import functools

import jax
import jax.numpy as jnp
import numpy as np
from jax import lax
from jax.experimental import pallas as pl
from jax.experimental.pallas import tpu as pltpu
from jax.sharding import PartitionSpec as P

NP = 8
NODES = 512
E_DEV = 64
CAP = 16
P_DEV = 8
N_CURVE = 8
N_SEG = 16
LOCAL = 6 * E_DEV

voigt_index = ((3, 8, 7), (8, 4, 6), (7, 6, 5))
time_step = 0.8 / (NP * NP)
lift_half = 0.25 * NP * (NP - 1)
BF = jnp.bfloat16
F32 = jnp.float32


def lobatto_nodes(edge_nodes):
    return -np.cos(np.pi * np.arange(edge_nodes) / (edge_nodes - 1))


def derivative_line(edge_nodes):
    points = lobatto_nodes(edge_nodes)
    node_ids = np.arange(edge_nodes)
    weight = np.where((node_ids == 0) | (node_ids == edge_nodes - 1), 2.0, 1.0)
    row_ids = node_ids[:, None]
    column_ids = node_ids[None, :]
    differ = points[:, None] - points[None, :]
    safe_gap = np.where(row_ids == column_ids, 1.0, differ)
    matrix = weight[:, None] / weight[None, :] * (-1.0) ** (row_ids + column_ids) / safe_gap
    matrix = np.where(row_ids == column_ids, 0.0, matrix)
    return matrix - np.eye(edge_nodes) * matrix.sum(axis=1)[:, None]


def refine_line(edge_nodes, upper):
    points = lobatto_nodes(edge_nodes)
    targets = (points + (2.0 * upper - 1.0)) / 2.0
    columns = []
    for column in range(edge_nodes):
        factor = np.ones(edge_nodes)
        for other_node in range(edge_nodes):
            if other_node != column:
                factor = (
                    factor * (targets - points[other_node]) / (points[column] - points[other_node])
                )
        columns.append(factor)
    return np.stack(columns, axis=1)


def refine_parts():
    lines = [refine_line(NP, upper) for upper in range(2)]
    plane = np.concatenate([np.kron(lines[k // 2], lines[k % 2]) for k in range(4)], axis=0).astype(np.float32)
    high = plane.astype(BF)
    low = (plane - high.astype(np.float32)).astype(BF)
    columns = [
        np.repeat(lines[upper][a, 2 * t : 2 * t + 2], 64) for upper in range(2) for a in range(8) for t in range(4)
    ]
    patterns = np.broadcast_to(np.stack(columns)[:, None, :], (64, 8, 128)).astype(np.float32)
    return np.concatenate([high, low], axis=1), np.concatenate([high, high], axis=1), patterns


_line = derivative_line(NP)
_line[0, 0] += lift_half
_line[7, 7] -= lift_half
ODD = 0.5 * (_line[:4, :4] - _line[:3:-1, :4])
EVEN = 0.5 * (_line[:4, :4] + _line[:3:-1, :4])


def line_product(x):
    odd = [x[a] - x[7 - a] for a in range(4)]
    even = [x[a] + x[7 - a] for a in range(4)]
    out = [None] * 8
    for m in range(4):
        p = sum(odd[a] * float(ODD[a, m]) for a in range(4))
        q = sum(even[a] * float(EVEN[a, m]) for a in range(4))
        out[m] = p + q
        out[7 - m] = p - q
    return out


def low_half():
    return lax.broadcasted_iota(jnp.int32, (8, 128), 1) < 64


def swap_halves(x):
    return pltpu.roll(x, 64, 1)


def lane_patterns():
    low = low_half()
    out = []
    for matrix in (ODD, EVEN):
        straight = [[None] * 2 for _ in range(2)]
        crossed = [[None] * 2 for _ in range(2)]
        for j in range(2):
            for m in range(2):
                straight[j][m] = jnp.where(low, float(matrix[2 * j, 2 * m]), float(matrix[2 * j + 1, 2 * m + 1]))
                crossed[j][m] = jnp.where(low, float(matrix[2 * j + 1, 2 * m]), float(matrix[2 * j, 2 * m + 1]))
        out.append((straight, crossed))
    return out


def lane_product(x, patterns):
    back = [swap_halves(x[3]), swap_halves(x[2])]
    sums = []
    for parts, (straight, crossed) in zip(
        ([x[0] - back[0], x[1] - back[1]], [x[0] + back[0], x[1] + back[1]]), patterns
    ):
        turned = [swap_halves(part) for part in parts]
        sums.append(
            [
                parts[0] * straight[0][m] + turned[0] * crossed[0][m] + parts[1] * straight[1][m] + turned[1] * crossed[1][m]
                for m in range(2)
            ]
        )
    p, q = sums
    return [p[0] + q[0], p[1] + q[1], swap_halves(p[1] - q[1]), swap_halves(p[0] - q[0])]


def split(x):
    high = x.astype(BF)
    return high, (x - high.astype(F32)).astype(BF)


def along(k, start=None):
    return pl.ds(k, 8, stride=8)


def image_rows(get, mat, direction):
    inv_density, lame, shear = mat
    trace = get(3) + get(4) + get(5)
    out = []
    for k in range(3):
        term = shear * get(voigt_index[direction][k])
        if k == direction:
            term = 2.0 * term + lame * trace
        out.append(term)
    return out + [inv_density * get(i) for i in range(3)]


def target_row(value, direction):
    return value if value < 3 else voigt_index[value - 3][direction]


def build_table(v_ref, mat, t_ref, directions):
    low = low_half()

    def put(value, block, direction, x0, x1):
        pair = jnp.concatenate([x0, x1], axis=0)
        high, rest = split(pair)
        rows = pl.ds(value * 64 + block * 16, 16)
        column = 256 * directions.index(direction)
        t_ref[rows, pl.ds(column, 128)] = high
        t_ref[rows, pl.ds(column + 128, 128)] = rest

    for direction in directions:
        if direction == 2:
            continue
        for j in range(4):
            if direction == 0:
                ends = [image_rows(lambda i, r=r: v_ref[i, j, pl.ds(r, 8), :], mat, 0) for r in (0, 56)]
            else:
                ends = [image_rows(lambda i, r=r: v_ref[i, j, along(r), :], mat, 1) for r in (0, 7)]
            for value in range(6):
                a0, a1 = ends[0][value], ends[1][value]
                put(
                    value,
                    j,
                    direction,
                    jnp.where(low, a0, swap_halves(a1)),
                    jnp.where(low, swap_halves(a0), a1),
                )
    for pair in range(4 if 2 in directions else 0):
        blocks = []
        for b in (2 * pair, 2 * pair + 1):
            blocks.append(
                image_rows(
                    lambda i, b=b: jnp.where(
                        low, v_ref[i, 0, along(b), :], v_ref[i, 3, along(b), :]
                    ),
                    mat,
                    2,
                )
            )
        for value in range(6):
            put(value, pair, 2, blocks[0][value], blocks[1][value])


def materials(mat_ref):
    return mat_ref[0], mat_ref[1], mat_ref[2]


def send_values(send_ref, t_ref, out_refs):
    rows = lax.dot_general(
        send_ref[...], t_ref[:, pl.ds(0, 256)], (((1,), (1,)), ((), ())), preferred_element_type=F32
    )
    for k in range(2):
        out_refs[k][...] = rows[16 * k : 16 * k + 16]


def parities():
    return 1 - lax.axis_index("curve") % 2, 1 - lax.axis_index("seg") % 2


def table_lane(q):
    element = (q * 10923) >> 16
    return (q - 6 * element) * E_DEV + element


def partner_tables(faces_ref, local_y_ref, local_ref, remote_ref):
    even_x, even_y = parities()
    low_row = lax.broadcasted_iota(jnp.int32, (1, 128), 1) < 64
    weight = jnp.where(low_row, lift_half, -lift_half)
    for direction in range(3):
        q = jnp.where(
            low_row,
            faces_ref[pl.ds(2 * direction, 1), :],
            pltpu.roll(faces_ref[pl.ds(2 * direction + 1, 1), :], 64, 1),
        ).astype(jnp.int32)
        remote = q - LOCAL
        side = remote >> 4
        block = side ^ jnp.where(side < 2, even_x, even_y)
        partner = jnp.where(remote < 0, table_lane(q), LOCAL + block * CAP + (remote & 15))
        lanes = pl.ds(direction * 128, 128)
        for start in range(0, LOCAL + 64, 64):
            source = lax.broadcasted_iota(jnp.int32, (64, 128), 0) + start
            hot = jnp.where(source == partner, weight, 0.0).astype(BF)
            target = (local_ref, local_y_ref, local_ref, remote_ref)[start // 128]
            base = start % 128 + (256 if start // 128 == 2 else 0)
            gap = 64 if start == LOCAL else 128
            for part in range(2):
                target[pl.ds(base + part * gap, 64), lanes] = hot


def send_table(pack_ref, send_x_ref, send_y_ref, small_ref):
    even_x, even_y = parities()
    small_ref[pl.ds(0, 8), :] = pack_ref[0]
    small_ref[pl.ds(8, 120), :] = jnp.zeros((120, 128), F32)
    turned = small_ref[...].T
    columns = [table_lane(turned[0:CAP, 3 + r : 4 + r].astype(jnp.int32)) for r in range(4)]
    for axis, even in ((0, even_x), (1, even_y)):
        first, second = columns[2 * axis], columns[2 * axis + 1]
        for k, column in enumerate((first + even * (second - first), second + even * (first - second))):
            hot = jnp.where(
                lax.broadcasted_iota(jnp.int32, (CAP, 128), 1) + 128 * axis == column, 1.0, 0.0
            ).astype(BF)
            for part in range(2):
                (send_x_ref, send_y_ref)[axis][pl.ds(k * CAP, CAP), pl.ds(128 * part, 128)] = hot


def begin_kernel(
    pack_ref, adjoint_ref,
    v_ref, ty_ref, t_ref, mat_ref, send_x_ref, send_y_ref, p0, p1, p2, p3, turn_ref, small_ref,
):
    low_row = lax.broadcasted_iota(jnp.int32, (1, 128), 1) < 64
    for i in range(3):
        row = pack_ref[0, pl.ds(i, 1), :]
        row = jnp.where(low_row, row, pltpu.roll(row, 64, 1))
        if i == 0:
            row = 1.0 / row
        mat_ref[i] = jnp.broadcast_to(row, (8, 128))
    send_table(pack_ref, send_x_ref, send_y_ref, small_ref)
    low = lax.broadcasted_iota(jnp.int32, (64, 128), 1) < 64
    for i in range(9):
        x = adjoint_ref[i]
        turn = turn_ref.at[i % 3]
        turn[...] = jnp.concatenate([x, x], axis=0).T
        for j in range(4):
            v_ref[i, j] = jnp.where(
                low, turn[pl.ds(2 * j, 64, stride=8), :], turn[pl.ds(2 * j + 1, 64, stride=8), :]
            )
    build_table(v_ref, materials(mat_ref), ty_ref, (1,))
    send_values(send_y_ref, ty_ref, (p2, p3))
    build_table(v_ref, materials(mat_ref), t_ref, (0, 2))
    send_values(send_x_ref, t_ref, (p0, p1))


def first_volume_kernel(
    factor, faces_ref, v_ref, ty_ref, t_ref, mat_ref, vol_ref, part_ref, local_y_ref, local_ref, remote_ref
):
    partner_tables(faces_ref, local_y_ref, local_ref, remote_ref)
    volume_kernel(factor, v_ref, ty_ref, t_ref, local_y_ref, local_ref, mat_ref, None, vol_ref, part_ref, None)


def last_volume_kernel(factor, v_ref, ty_ref, t_ref, local_y_ref, local_ref, mat_ref, acc_ref, vol_ref, part_ref):
    volume_kernel(factor, v_ref, ty_ref, t_ref, local_y_ref, local_ref, mat_ref, acc_ref, vol_ref, part_ref, None)


def volume_kernel(
    factor, v_ref, ty_ref, t_ref, local_y_ref, local_ref, mat_ref, acc_ref, vol_ref, part_ref, sum_ref
):
    inv_density, lame, shear = [m * factor for m in materials(mat_ref)]

    def scaled(get, direction):
        out = []
        for k in range(3):
            if k == direction:
                out.append(
                    (k, [2.0 * shear * d + lame * (s0 + s1 + s2) for d, s0, s1, s2 in zip(get(3 + k), get(3), get(4), get(5))])
                )
            else:
                out.append((k, [shear * x for x in get(voigt_index[direction][k])]))
        for i in range(3):
            out.append((voigt_index[i][direction], [inv_density * x for x in get(i)]))
        return out

    def tiles(j):
        for row, x in scaled(lambda i: [v_ref[i, j, along(b), :] for b in range(8)], 1):
            for b, y in enumerate(line_product(x)):
                vol_ref[row, j, along(b), :] = y
        chunk = pl.ds(j * 96, 96)
        part_ref[chunk, :] = factor * (
            jnp.dot(ty_ref[chunk, :], local_y_ref[...], preferred_element_type=F32)
            + jnp.dot(t_ref[chunk, :], local_ref[...], preferred_element_type=F32)
        )
        for row, x in scaled(lambda i: [v_ref[i, j, pl.ds(8 * a, 8), :] for a in range(8)], 0):
            for a, y in enumerate(line_product(x)):
                if row not in (3, 7):
                    y = y + vol_ref[row, j, pl.ds(8 * a, 8), :]
                vol_ref[row, j, pl.ds(8 * a, 8), :] = y

    for j in range(4):
        tiles(j)
    patterns = lane_patterns()

    def groups(a, carry):
        rows = pl.ds(pl.multiple_of(a * 8, 8), 8)
        for row, x in scaled(lambda i: [v_ref[i, j, rows, :] for j in range(4)], 2):
            for j, y in enumerate(lane_product(x, patterns)):
                if row != 5:
                    y = y + vol_ref[row, j, rows, :]
                vol_ref[row, j, rows, :] = y
        if acc_ref is not None:
            for i in range(9):
                for j in range(4):
                    y = acc_ref[i, j, rows, :] + v_ref[i, j, rows, :]
                    if sum_ref is not None:
                        sum_ref[i, j, rows, :] = y
                    else:
                        vol_ref[i, j, rows, :] += y
        return carry

    lax.fori_loop(0, 8, groups, 0, unroll=4)


def add_faces(part_ref, r_refs, remote_ref, factor, out_ref, face_ref):
    arrived = jnp.concatenate([r[...] for r in r_refs], axis=0) * factor
    both = jnp.concatenate(split(arrived), axis=0)
    face_ref[...] = part_ref[...] + lax.dot_general(
        both, remote_ref[...], (((0,), (0,)), ((), ())), preferred_element_type=F32
    )
    low = low_half()
    for direction in range(3):
        for value in range(6):
            row = target_row(value, direction)
            for j in range(4):
                x0 = face_ref[pl.ds(value * 64 + 16 * j, 8), pl.ds(direction * 128, 128)]
                x1 = face_ref[pl.ds(value * 64 + 16 * j + 8, 8), pl.ds(direction * 128, 128)]
                if direction < 2:
                    y0 = jnp.where(low, x0, swap_halves(x1))
                    y1 = jnp.where(low, swap_halves(x0), x1)
                    rows = (pl.ds(0, 8), pl.ds(56, 8)) if direction == 0 else (along(0), along(7))
                    out_ref[row, j, rows[0], :] += y0
                    out_ref[row, j, rows[1], :] += y1
                else:
                    for b, x in ((2 * j, x0), (2 * j + 1, x1)):
                        out_ref[row, 0, along(b), :] += jnp.where(low, x, 0.0)
                        out_ref[row, 3, along(b), :] += jnp.where(low, 0.0, x)


def finish_kernel(
    factor, order, vol_ref, part_ref, ra, rb, rc, rd, remote_ref, mat_ref, send_x_ref, send_y_ref,
    v_ref, ty_ref, t_ref, p0, p1, p2, p3, face_ref,
):
    add_faces(part_ref, in_order(order, (ra, rb, rc, rd)), remote_ref, factor, v_ref, face_ref)
    build_table(v_ref, materials(mat_ref), ty_ref, (1,))
    send_values(send_y_ref, ty_ref, (p2, p3))
    build_table(v_ref, materials(mat_ref), t_ref, (0, 2))
    send_values(send_x_ref, t_ref, (p0, p1))


def in_order(order, refs):
    return [refs[order.index(k)] for k in range(4)]


def end_kernel(
    factor, order, keys_ref, vol_ref, part_ref, ra, rb, rc, rd, remote_ref, place_ref, wa_ref, wb_ref, lines_ref,
    total_ref, parent_ref, away_ref, face_ref, turn_ref, ranked_ref, rows_ref, plane_ref, block_ref, sem,
):
    add_faces(part_ref, in_order(order, (ra, rb, rc, rd)), remote_ref, factor, total_ref, face_ref)
    place = jnp.where(
        lax.broadcasted_iota(jnp.int32, (64, 128), 0) == place_ref[...], 1.0, 0.0
    ).astype(BF)
    wide = lax.broadcasted_iota(jnp.int32, (64, 128), 1) < 64
    low = low_half()
    for i in range(9):
        for j in range(4):
            tile = total_ref[i, j]
            high = tile.astype(BF).astype(F32)
            rest = tile - high
            turn_ref[i, pl.ds(2 * j, 64, stride=8), :] = jnp.where(wide, high, pltpu.roll(rest, 64, 1))
            turn_ref[i, pl.ds(2 * j + 1, 64, stride=8), :] = jnp.where(wide, pltpu.roll(high, 64, 1), rest)
        ranked_ref[i] = lax.dot_general(
            place, turn_ref[i].astype(BF), (((1,), (1,)), ((), ())), preferred_element_type=F32
        )
    for i in range(9):
        for upper in range(2):
            for t in range(4):
                x = [ranked_ref[i, pl.ds(8 * (4 * upper + k), 8), pl.ds(128 * t, 128)] for k in range(4)]
                for pair in range(2):
                    x0, x1 = x[2 * pair], x[2 * pair + 1]
                    lanes = pl.ds(128 * pair, 128)
                    rows_ref[i, pl.ds(64 * upper + 16 * t, 8), lanes] = jnp.where(low, x0, swap_halves(x1))
                    rows_ref[i, pl.ds(64 * upper + 16 * t + 8, 8), lanes] = jnp.where(low, swap_halves(x0), x1)
        high, rest = split(rows_ref[i])
        plane = jnp.dot(high, wa_ref[...], preferred_element_type=F32)
        plane_ref[i] = plane + pltpu.roll(plane, 64, 1) + jnp.dot(rest, wb_ref[...], preferred_element_type=F32)
    for t in range(4):
        sums = [None] * 9
        for k in range(16):
            line = lines_ref[4 * k + t]
            for i in range(9):
                term = plane_ref[i, pl.ds(8 * k, 8), :] * line
                sums[i] = term if k == 0 else sums[i] + term
        for i in range(9):
            parent_ref[i, t] = sums[i]
    def send(g):
        place = keys_ref[g] - P_DEV
        return pltpu.make_async_copy(block_ref.at[g], away_ref.at[place // 2, place % 2], sem.at[g])

    for g in range(P_DEV):

        @pl.when(keys_ref[g] >= P_DEV)
        def _():
            for i in range(9):
                for t in range(4):
                    block_ref[g, i, pl.ds(t, 1), :] = parent_ref[i, t, pl.ds(g, 1), :]
            send(g).start()

    for g in range(P_DEV):

        @pl.when(keys_ref[g] >= P_DEV)
        def _():
            send(g).wait()


def next_kernel(total_ref, next_ref, turn_ref):
    def body(i, carry):
        for j in range(4):
            tile = total_ref[i, j]
            turn_ref[pl.ds(2 * j, 64, stride=8), :] = tile
            turn_ref[pl.ds(2 * j + 1, 64, stride=8), :] = pltpu.roll(tile, 64, 1)
        next_ref[i] = turn_ref[...].T[:64]
        return carry

    lax.fori_loop(0, 9, body, 0)


def parent_kernel(table_ref, groups_ref, arrived_ref, out_ref):
    for p in range(P_DEV):
        holder = table_ref[0, p]
        slot = table_ref[1, p]

        @pl.when(slot < 0)
        def _():
            for i in range(9):
                for t in range(4):
                    out_ref[i, pl.ds(p, 1), pl.ds(128 * t, 128)] = groups_ref[i, t, pl.ds(holder, 1), :]

        @pl.when(slot >= 0)
        def _():
            for i in range(9):
                for t in range(4):
                    out_ref[i, pl.ds(p, 1), pl.ds(128 * t, 128)] = arrived_ref[
                        holder, slot, i, pl.ds(t, 1), :
                    ]


def shape(*dims, dtype=F32):
    return jax.ShapeDtypeStruct(dims, dtype)


VMEM = pl.BlockSpec(memory_space=pltpu.VMEM)
SMEM = pl.BlockSpec(memory_space=pltpu.SMEM)
ANYWHERE = pl.BlockSpec(memory_space=pl.ANY)


def call(kernel, outs, scratch=(), smem=(), anywhere=(), aliases={}, count=0, flops=10**8, traffic=6 * 10**6):
    return pl.pallas_call(
        kernel,
        out_shape=outs,
        in_specs=[SMEM if k in smem else VMEM for k in range(count)],
        out_specs=[ANYWHERE if k in anywhere else VMEM for k in range(len(outs))],
        scratch_shapes=list(scratch),
        input_output_aliases=aliases,
        compiler_params=pltpu.CompilerParams(vmem_limit_bytes=32 * 2**20),
        cost_estimate=pl.CostEstimate(flops=flops, bytes_accessed=traffic, transcendentals=0),
    )


def exchange_pairs():
    along_x = [[(k, (k + 1) % N_CURVE) for k in range(start, N_CURVE, 2)] for start in (0, 1)]
    along_y = [[(k, (k + 1) % N_SEG) for k in range(start, N_SEG, 2)] for start in (0, 1)]
    both = lambda pairs: pairs + [(b, a) for a, b in pairs]
    return [("curve", both(p)) for p in along_x] + [("seg", both(p)) for p in along_y]


def shards(adjoint, material, face_partner, send_faces, migration, children):
    own_seg = lax.axis_index("seg")
    owner, slot, octant = migration[0], migration[1], migration[2]
    key = jnp.where(owner == own_seg, slot, P_DEV + 2 * owner + slot)
    first = octant == 0
    rank = jnp.sum((first[:, None] & (key[:, None] < key[None, :])).astype(jnp.int32), axis=0)
    place = octant * P_DEV + rank
    place = jnp.concatenate([place, place]).reshape(1, 128)
    keys = jnp.sum(
        jnp.where(first[:, None] & (rank[:, None] == jnp.arange(P_DEV)[None, :]), key[:, None], 0), axis=0
    )
    stays = children[0] == own_seg
    group = jnp.sum((keys[:, None] < jnp.arange(P_DEV)[None, :]).astype(jnp.int32), axis=0)
    source = jnp.stack([jnp.where(stays, group, children[0]), jnp.where(stays, -1, children[1])])

    state = shape(9, 4, 64, 128)
    table_y = shape(LOCAL, 256, dtype=BF)
    table = shape(LOCAL, 512, dtype=BF)
    sent = shape(32, 256, dtype=BF)
    face_part = shape(LOCAL, LOCAL)
    payload = [shape(CAP, LOCAL)] * 4
    face_scratch = pltpu.VMEM((LOCAL, LOCAL), F32)
    turn = pltpu.VMEM((NODES, 128), F32)

    zero = jnp.float32(0)
    pack = lax.pad(material[None], zero, ((0, 0, 0), (0, 5, 0), (0, 64, 0))) + lax.pad(
        send_faces, jnp.int32(0), ((0, 0, 0), (3, 1, 0), (0, 128 - CAP, 0))
    ).astype(F32)
    faces = jnp.pad(face_partner.T.astype(F32), ((0, 2), (0, 64)))
    outs = call(
        begin_kernel,
        [state, table_y, table, shape(3, 8, 128), sent, sent] + payload,
        [pltpu.VMEM((3, NODES, 128), F32), pltpu.VMEM((128, 128), F32)],
        count=2,
    )(pack, adjoint)
    v, ty, t, mat, send_x, send_y = outs[:6]
    out_going = outs[6:]
    pairs = exchange_pairs()
    for step in range(1, 5):
        factor = time_step / step
        order = (1, 0, 3, 2) if step == 3 else (3, 2, 1, 0)
        arrived = [lax.ppermute(out_going[k], *pairs[k]) for k in order]
        if step == 1:
            vol, part, local_y, local, remote_hot = call(
                functools.partial(first_volume_kernel, factor),
                [
                    state,
                    face_part,
                    shape(256, LOCAL, dtype=BF),
                    shape(512, LOCAL, dtype=BF),
                    shape(128, LOCAL, dtype=BF),
                ],
                count=5,
            )(faces, v, ty, t, mat)
            acc = v
        elif step < 4:
            vol, part, acc = call(
                functools.partial(volume_kernel, factor), [state, face_part, state], count=7
            )(v, ty, t, local_y, local, mat, acc)
        else:
            vol, part = call(functools.partial(last_volume_kernel, factor), [state, face_part], count=7)(
                v, ty, t, local_y, local, mat, acc
            )
        if step < 4:
            outs = call(
                functools.partial(finish_kernel, factor, order),
                [state, table_y, table] + payload,
                [face_scratch],
                aliases={0: 0},
                count=10,
            )(vol, part, *arrived, remote_hot, mat, send_x, send_y)
            v, ty, t, out_going = outs[0], outs[1], outs[2], outs[3:]
    wa, wb, lines = (jnp.asarray(x) for x in refine_parts())
    total, groups, away = call(
        functools.partial(end_kernel, factor, order),
        [state, shape(9, 4, P_DEV, 128), shape(N_SEG, 2, 9, 4, 128)],
        [
            face_scratch,
            pltpu.VMEM((9, NODES, 128), F32),
            pltpu.VMEM((9, 64, NODES), F32),
            pltpu.VMEM((9, 128, 256), F32),
            pltpu.VMEM((9, 128, 128), F32),
            pltpu.VMEM((P_DEV, 9, 4, 128), F32),
            pltpu.SemaphoreType.DMA((P_DEV,)),
        ],
        anywhere=(2,),
        smem=(0,),
        aliases={1: 0},
        count=12,
    )(keys, vol, part, *arrived, remote_hot, place, wa, wb, lines)
    fetched = lax.all_to_all(away, "seg", split_axis=0, concat_axis=0, tiled=True)
    updated = call(next_kernel, [shape(9, E_DEV, NODES)], [turn], count=1)(total)[0]
    parents = call(parent_kernel, [shape(9, P_DEV, NODES)], smem=(0,), count=3)(source, groups, fetched)[0]
    return (updated, parents)


def solution(mesh):
    in_specs = (
        P(None, ("curve", "seg"), None),
        P(None, ("curve", "seg")),
        P(("curve", "seg"), None),
        P(("curve", "seg"), None, None),
        P(None, ("curve", "seg")),
        P(None, ("curve", "seg")),
    )
    out_specs = (P(None, ("curve", "seg"), None), P(None, ("curve", "seg"), None))
    return jax.shard_map(shards, mesh=mesh, in_specs=in_specs, out_specs=out_specs, check_vma=False)
```

```python
import functools

import jax
import jax.numpy as jnp
import numpy as np
from jax import lax
from jax.experimental import pallas as pl
from jax.experimental.pallas import tpu as pltpu
from jax.sharding import PartitionSpec as P

NP = 8
NODES = 512
E_DEV = 64
CAP = 16
P_DEV = 8
N_CURVE = 8
N_SEG = 16
LOCAL = 6 * E_DEV

voigt_index = ((3, 8, 7), (8, 4, 6), (7, 6, 5))
time_step = 0.8 / (NP * NP)
lift_half = 0.25 * NP * (NP - 1)
BF = jnp.bfloat16
F32 = jnp.float32


def lobatto_nodes(edge_nodes):
    return -np.cos(np.pi * np.arange(edge_nodes) / (edge_nodes - 1))


def derivative_line(edge_nodes):
    points = lobatto_nodes(edge_nodes)
    node_ids = np.arange(edge_nodes)
    weight = np.where((node_ids == 0) | (node_ids == edge_nodes - 1), 2.0, 1.0)
    row_ids = node_ids[:, None]
    column_ids = node_ids[None, :]
    differ = points[:, None] - points[None, :]
    safe_gap = np.where(row_ids == column_ids, 1.0, differ)
    matrix = weight[:, None] / weight[None, :] * (-1.0) ** (row_ids + column_ids) / safe_gap
    matrix = np.where(row_ids == column_ids, 0.0, matrix)
    return matrix - np.eye(edge_nodes) * matrix.sum(axis=1)[:, None]


def refine_line(edge_nodes, upper):
    points = lobatto_nodes(edge_nodes)
    targets = (points + (2.0 * upper - 1.0)) / 2.0
    columns = []
    for column in range(edge_nodes):
        factor = np.ones(edge_nodes)
        for other_node in range(edge_nodes):
            if other_node != column:
                factor = (
                    factor * (targets - points[other_node]) / (points[column] - points[other_node])
                )
        columns.append(factor)
    return np.stack(columns, axis=1)


def refine_parts():
    lines = [refine_line(NP, upper) for upper in range(2)]
    plane = np.concatenate([np.kron(lines[k // 2], lines[k % 2]) for k in range(4)], axis=0).astype(np.float32)
    high = plane.astype(BF)
    low = (plane - high.astype(np.float32)).astype(BF)
    columns = [
        np.repeat(lines[upper][a, 2 * t : 2 * t + 2], 64) for upper in range(2) for a in range(8) for t in range(4)
    ]
    patterns = np.broadcast_to(np.stack(columns)[:, None, :], (64, 8, 128)).astype(np.float32)
    return np.concatenate([high, low], axis=1), np.concatenate([high, high], axis=1), patterns


_line = derivative_line(NP)
_line[0, 0] += lift_half
_line[7, 7] -= lift_half
ODD = 0.5 * (_line[:4, :4] - _line[:3:-1, :4])
EVEN = 0.5 * (_line[:4, :4] + _line[:3:-1, :4])


def line_product(x):
    odd = [x[a] - x[7 - a] for a in range(4)]
    even = [x[a] + x[7 - a] for a in range(4)]
    out = [None] * 8
    for m in range(4):
        p = sum(odd[a] * float(ODD[a, m]) for a in range(4))
        q = sum(even[a] * float(EVEN[a, m]) for a in range(4))
        out[m] = p + q
        out[7 - m] = p - q
    return out


def low_half():
    return lax.broadcasted_iota(jnp.int32, (8, 128), 1) < 64


def swap_halves(x):
    return pltpu.roll(x, 64, 1)


def lane_patterns():
    low = low_half()
    out = []
    for matrix in (ODD, EVEN):
        straight = [[None] * 2 for _ in range(2)]
        crossed = [[None] * 2 for _ in range(2)]
        for j in range(2):
            for m in range(2):
                straight[j][m] = jnp.where(low, float(matrix[2 * j, 2 * m]), float(matrix[2 * j + 1, 2 * m + 1]))
                crossed[j][m] = jnp.where(low, float(matrix[2 * j + 1, 2 * m]), float(matrix[2 * j, 2 * m + 1]))
        out.append((straight, crossed))
    return out


def lane_product(x, patterns):
    back = [swap_halves(x[3]), swap_halves(x[2])]
    sums = []
    for parts, (straight, crossed) in zip(
        ([x[0] - back[0], x[1] - back[1]], [x[0] + back[0], x[1] + back[1]]), patterns
    ):
        turned = [swap_halves(part) for part in parts]
        sums.append(
            [
                parts[0] * straight[0][m] + turned[0] * crossed[0][m] + parts[1] * straight[1][m] + turned[1] * crossed[1][m]
                for m in range(2)
            ]
        )
    p, q = sums
    return [p[0] + q[0], p[1] + q[1], swap_halves(p[1] - q[1]), swap_halves(p[0] - q[0])]


def split(x):
    high = x.astype(BF)
    return high, (x - high.astype(F32)).astype(BF)


def along(k, start=None):
    return pl.ds(k, 8, stride=8)


def image_rows(get, mat, direction):
    inv_density, lame, shear = mat
    trace = get(3) + get(4) + get(5)
    out = []
    for k in range(3):
        term = shear * get(voigt_index[direction][k])
        if k == direction:
            term = 2.0 * term + lame * trace
        out.append(term)
    return out + [inv_density * get(i) for i in range(3)]


def target_row(value, direction):
    return value if value < 3 else voigt_index[value - 3][direction]


def build_table(v_ref, mat, t_ref, directions):
    low = low_half()

    def put(value, block, direction, x0, x1):
        pair = jnp.concatenate([x0, x1], axis=0)
        high, rest = split(pair)
        rows = pl.ds(value * 64 + block * 16, 16)
        column = 256 * directions.index(direction)
        t_ref[rows, pl.ds(column, 128)] = high
        t_ref[rows, pl.ds(column + 128, 128)] = rest

    for direction in directions:
        if direction == 2:
            continue
        for j in range(4):
            if direction == 0:
                ends = [image_rows(lambda i, r=r: v_ref[i, j, pl.ds(r, 8), :], mat, 0) for r in (0, 56)]
            else:
                ends = [image_rows(lambda i, r=r: v_ref[i, j, along(r), :], mat, 1) for r in (0, 7)]
            for value in range(6):
                a0, a1 = ends[0][value], ends[1][value]
                put(
                    value,
                    j,
                    direction,
                    jnp.where(low, a0, swap_halves(a1)),
                    jnp.where(low, swap_halves(a0), a1),
                )
    for pair in range(4 if 2 in directions else 0):
        blocks = []
        for b in (2 * pair, 2 * pair + 1):
            blocks.append(
                image_rows(
                    lambda i, b=b: jnp.where(
                        low, v_ref[i, 0, along(b), :], v_ref[i, 3, along(b), :]
                    ),
                    mat,
                    2,
                )
            )
        for value in range(6):
            put(value, pair, 2, blocks[0][value], blocks[1][value])


def materials(mat_ref):
    return mat_ref[0], mat_ref[1], mat_ref[2]


def send_values(send_ref, t_ref, out_refs):
    rows = lax.dot_general(
        send_ref[...], t_ref[:, pl.ds(0, 256)], (((1,), (1,)), ((), ())), preferred_element_type=F32
    )
    for k in range(2):
        out_refs[k][...] = rows[16 * k : 16 * k + 16]


def parities():
    return 1 - lax.axis_index("curve") % 2, 1 - lax.axis_index("seg") % 2


def table_lane(q):
    element = (q * 10923) >> 16
    return (q - 6 * element) * E_DEV + element


def partner_tables(faces_ref, local_y_ref, local_ref, remote_ref):
    even_x, even_y = parities()
    low_row = lax.broadcasted_iota(jnp.int32, (1, 128), 1) < 64
    weight = jnp.where(low_row, lift_half, -lift_half)
    for direction in range(3):
        q = jnp.where(
            low_row,
            faces_ref[pl.ds(2 * direction, 1), :],
            pltpu.roll(faces_ref[pl.ds(2 * direction + 1, 1), :], 64, 1),
        ).astype(jnp.int32)
        remote = q - LOCAL
        side = remote >> 4
        block = side ^ jnp.where(side < 2, even_x, even_y)
        partner = jnp.where(remote < 0, table_lane(q), LOCAL + block * CAP + (remote & 15))
        lanes = pl.ds(direction * 128, 128)
        for start in range(0, LOCAL + 64, 64):
            source = lax.broadcasted_iota(jnp.int32, (64, 128), 0) + start
            hot = jnp.where(source == partner, weight, 0.0).astype(BF)
            target = (local_ref, local_y_ref, local_ref, remote_ref)[start // 128]
            base = start % 128 + (256 if start // 128 == 2 else 0)
            gap = 64 if start == LOCAL else 128
            for part in range(2):
                target[pl.ds(base + part * gap, 64), lanes] = hot


def send_table(pack_ref, send_x_ref, send_y_ref, small_ref):
    even_x, even_y = parities()
    small_ref[pl.ds(0, 8), :] = pack_ref[0]
    small_ref[pl.ds(8, 120), :] = jnp.zeros((120, 128), F32)
    turned = small_ref[...].T
    columns = [table_lane(turned[0:CAP, 3 + r : 4 + r].astype(jnp.int32)) for r in range(4)]
    for axis, even in ((0, even_x), (1, even_y)):
        first, second = columns[2 * axis], columns[2 * axis + 1]
        for k, column in enumerate((first + even * (second - first), second + even * (first - second))):
            hot = jnp.where(
                lax.broadcasted_iota(jnp.int32, (CAP, 128), 1) + 128 * axis == column, 1.0, 0.0
            ).astype(BF)
            for part in range(2):
                (send_x_ref, send_y_ref)[axis][pl.ds(k * CAP, CAP), pl.ds(128 * part, 128)] = hot


def begin_kernel(
    pack_ref, part0, part1, part2,
    v_ref, ty_ref, t_ref, mat_ref, send_x_ref, send_y_ref, p0, p1, p2, p3, turn_ref, small_ref,
):
    low_row = lax.broadcasted_iota(jnp.int32, (1, 128), 1) < 64
    for i in range(3):
        row = pack_ref[0, pl.ds(i, 1), :]
        row = jnp.where(low_row, row, pltpu.roll(row, 64, 1))
        if i == 0:
            row = 1.0 / row
        mat_ref[i] = jnp.broadcast_to(row, (8, 128))
    send_table(pack_ref, send_x_ref, send_y_ref, small_ref)
    low = lax.broadcasted_iota(jnp.int32, (64, 128), 1) < 64
    for i in range(9):
        x = (part0, part1, part2)[i // 3][i % 3]
        turn = turn_ref.at[i % 3]
        turn[...] = jnp.concatenate([x, x], axis=0).T
        for j in range(4):
            v_ref[i, j] = jnp.where(
                low, turn[pl.ds(2 * j, 64, stride=8), :], turn[pl.ds(2 * j + 1, 64, stride=8), :]
            )
    build_table(v_ref, materials(mat_ref), ty_ref, (1,))
    send_values(send_y_ref, ty_ref, (p2, p3))
    build_table(v_ref, materials(mat_ref), t_ref, (0, 2))
    send_values(send_x_ref, t_ref, (p0, p1))


def first_volume_kernel(
    factor, faces_ref, v_ref, ty_ref, t_ref, mat_ref, vol_ref, part_ref, local_y_ref, local_ref, remote_ref
):
    partner_tables(faces_ref, local_y_ref, local_ref, remote_ref)
    volume_kernel(factor, v_ref, ty_ref, t_ref, local_y_ref, local_ref, mat_ref, None, vol_ref, part_ref, None)


def last_volume_kernel(factor, v_ref, ty_ref, t_ref, local_y_ref, local_ref, mat_ref, acc_ref, vol_ref, part_ref):
    volume_kernel(factor, v_ref, ty_ref, t_ref, local_y_ref, local_ref, mat_ref, acc_ref, vol_ref, part_ref, None)


def volume_kernel(
    factor, v_ref, ty_ref, t_ref, local_y_ref, local_ref, mat_ref, acc_ref, vol_ref, part_ref, sum_ref
):
    inv_density, lame, shear = [m * factor for m in materials(mat_ref)]

    def scaled(get, direction):
        out = []
        for k in range(3):
            if k == direction:
                out.append(
                    (k, [2.0 * shear * d + lame * (s0 + s1 + s2) for d, s0, s1, s2 in zip(get(3 + k), get(3), get(4), get(5))])
                )
            else:
                out.append((k, [shear * x for x in get(voigt_index[direction][k])]))
        for i in range(3):
            out.append((voigt_index[i][direction], [inv_density * x for x in get(i)]))
        return out

    def tiles(j):
        for row, x in scaled(lambda i: [v_ref[i, j, along(b), :] for b in range(8)], 1):
            for b, y in enumerate(line_product(x)):
                vol_ref[row, j, along(b), :] = y
        chunk = pl.ds(j * 96, 96)
        part_ref[chunk, :] = factor * (
            jnp.dot(ty_ref[chunk, :], local_y_ref[...], preferred_element_type=F32)
            + jnp.dot(t_ref[chunk, :], local_ref[...], preferred_element_type=F32)
        )
        for row, x in scaled(lambda i: [v_ref[i, j, pl.ds(8 * a, 8), :] for a in range(8)], 0):
            for a, y in enumerate(line_product(x)):
                if row not in (3, 7):
                    y = y + vol_ref[row, j, pl.ds(8 * a, 8), :]
                vol_ref[row, j, pl.ds(8 * a, 8), :] = y

    for j in range(4):
        tiles(j)
    patterns = lane_patterns()

    def groups(a, carry):
        rows = pl.ds(pl.multiple_of(a * 8, 8), 8)
        for row, x in scaled(lambda i: [v_ref[i, j, rows, :] for j in range(4)], 2):
            for j, y in enumerate(lane_product(x, patterns)):
                if row != 5:
                    y = y + vol_ref[row, j, rows, :]
                vol_ref[row, j, rows, :] = y
        if acc_ref is not None:
            for i in range(9):
                for j in range(4):
                    y = acc_ref[i, j, rows, :] + v_ref[i, j, rows, :]
                    if sum_ref is not None:
                        sum_ref[i, j, rows, :] = y
                    else:
                        vol_ref[i, j, rows, :] += y
        return carry

    lax.fori_loop(0, 8, groups, 0, unroll=4)


def add_faces(part_ref, r_refs, remote_ref, factor, out_ref, face_ref):
    arrived = jnp.concatenate([r[...] for r in r_refs], axis=0) * factor
    both = jnp.concatenate(split(arrived), axis=0)
    face_ref[...] = part_ref[...] + lax.dot_general(
        both, remote_ref[...], (((0,), (0,)), ((), ())), preferred_element_type=F32
    )
    low = low_half()
    for direction in range(3):
        for value in range(6):
            row = target_row(value, direction)
            for j in range(4):
                x0 = face_ref[pl.ds(value * 64 + 16 * j, 8), pl.ds(direction * 128, 128)]
                x1 = face_ref[pl.ds(value * 64 + 16 * j + 8, 8), pl.ds(direction * 128, 128)]
                if direction < 2:
                    y0 = jnp.where(low, x0, swap_halves(x1))
                    y1 = jnp.where(low, swap_halves(x0), x1)
                    rows = (pl.ds(0, 8), pl.ds(56, 8)) if direction == 0 else (along(0), along(7))
                    out_ref[row, j, rows[0], :] += y0
                    out_ref[row, j, rows[1], :] += y1
                else:
                    for b, x in ((2 * j, x0), (2 * j + 1, x1)):
                        out_ref[row, 0, along(b), :] += jnp.where(low, x, 0.0)
                        out_ref[row, 3, along(b), :] += jnp.where(low, 0.0, x)


def finish_kernel(
    factor, order, vol_ref, part_ref, ra, rb, rc, rd, remote_ref, mat_ref, send_x_ref, send_y_ref,
    v_ref, ty_ref, t_ref, p0, p1, p2, p3, face_ref,
):
    add_faces(part_ref, in_order(order, (ra, rb, rc, rd)), remote_ref, factor, v_ref, face_ref)
    build_table(v_ref, materials(mat_ref), ty_ref, (1,))
    send_values(send_y_ref, ty_ref, (p2, p3))
    build_table(v_ref, materials(mat_ref), t_ref, (0, 2))
    send_values(send_x_ref, t_ref, (p0, p1))


def in_order(order, refs):
    return [refs[order.index(k)] for k in range(4)]


def end_kernel(
    factor, order, keys_ref, vol_ref, part_ref, ra, rb, rc, rd, remote_ref, place_ref, wa_ref, wb_ref, lines_ref,
    total_ref, parent_ref, away_ref, face_ref, turn_ref, ranked_ref, rows_ref, plane_ref, block_ref, sem,
):
    add_faces(part_ref, in_order(order, (ra, rb, rc, rd)), remote_ref, factor, total_ref, face_ref)
    place = jnp.where(
        lax.broadcasted_iota(jnp.int32, (64, 128), 0) == place_ref[...], 1.0, 0.0
    ).astype(BF)
    wide = lax.broadcasted_iota(jnp.int32, (64, 128), 1) < 64
    low = low_half()
    for i in range(9):
        for j in range(4):
            tile = total_ref[i, j]
            high = tile.astype(BF).astype(F32)
            rest = tile - high
            turn_ref[i, pl.ds(2 * j, 64, stride=8), :] = jnp.where(wide, high, pltpu.roll(rest, 64, 1))
            turn_ref[i, pl.ds(2 * j + 1, 64, stride=8), :] = jnp.where(wide, pltpu.roll(high, 64, 1), rest)
        ranked_ref[i] = lax.dot_general(
            place, turn_ref[i].astype(BF), (((1,), (1,)), ((), ())), preferred_element_type=F32
        )
    for i in range(9):
        for upper in range(2):
            for t in range(4):
                x = [ranked_ref[i, pl.ds(8 * (4 * upper + k), 8), pl.ds(128 * t, 128)] for k in range(4)]
                for pair in range(2):
                    x0, x1 = x[2 * pair], x[2 * pair + 1]
                    lanes = pl.ds(128 * pair, 128)
                    rows_ref[i, pl.ds(64 * upper + 16 * t, 8), lanes] = jnp.where(low, x0, swap_halves(x1))
                    rows_ref[i, pl.ds(64 * upper + 16 * t + 8, 8), lanes] = jnp.where(low, swap_halves(x0), x1)
        high, rest = split(rows_ref[i])
        plane = jnp.dot(high, wa_ref[...], preferred_element_type=F32)
        plane_ref[i] = plane + pltpu.roll(plane, 64, 1) + jnp.dot(rest, wb_ref[...], preferred_element_type=F32)
    for t in range(4):
        sums = [None] * 9
        for k in range(16):
            line = lines_ref[4 * k + t]
            for i in range(9):
                term = plane_ref[i, pl.ds(8 * k, 8), :] * line
                sums[i] = term if k == 0 else sums[i] + term
        for i in range(9):
            parent_ref[i, t] = sums[i]
    def send(g):
        place = keys_ref[g] - P_DEV
        return pltpu.make_async_copy(block_ref.at[g], away_ref.at[place // 2, place % 2], sem.at[g])

    for g in range(P_DEV):

        @pl.when(keys_ref[g] >= P_DEV)
        def _():
            for i in range(9):
                for t in range(4):
                    block_ref[g, i, pl.ds(t, 1), :] = parent_ref[i, t, pl.ds(g, 1), :]
            send(g).start()

    for g in range(P_DEV):

        @pl.when(keys_ref[g] >= P_DEV)
        def _():
            send(g).wait()


def next_kernel(total_ref, next_ref, turn_ref):
    def body(i, carry):
        for j in range(4):
            tile = total_ref[i, j]
            turn_ref[pl.ds(2 * j, 64, stride=8), :] = tile
            turn_ref[pl.ds(2 * j + 1, 64, stride=8), :] = pltpu.roll(tile, 64, 1)
        next_ref[i] = turn_ref[...].T[:64]
        return carry

    lax.fori_loop(0, 9, body, 0)


def parent_kernel(table_ref, groups_ref, arrived_ref, out_ref):
    for p in range(P_DEV):
        holder = table_ref[0, p]
        slot = table_ref[1, p]

        @pl.when(slot < 0)
        def _():
            for i in range(9):
                for t in range(4):
                    out_ref[i, pl.ds(p, 1), pl.ds(128 * t, 128)] = groups_ref[i, t, pl.ds(holder, 1), :]

        @pl.when(slot >= 0)
        def _():
            for i in range(9):
                for t in range(4):
                    out_ref[i, pl.ds(p, 1), pl.ds(128 * t, 128)] = arrived_ref[
                        holder, slot, i, pl.ds(t, 1), :
                    ]


def shape(*dims, dtype=F32):
    return jax.ShapeDtypeStruct(dims, dtype)


VMEM = pl.BlockSpec(memory_space=pltpu.VMEM)
SMEM = pl.BlockSpec(memory_space=pltpu.SMEM)
ANYWHERE = pl.BlockSpec(memory_space=pl.ANY)


def call(kernel, outs, scratch=(), smem=(), anywhere=(), aliases={}, count=0, flops=10**8, traffic=6 * 10**6):
    return pl.pallas_call(
        kernel,
        out_shape=outs,
        in_specs=[SMEM if k in smem else VMEM for k in range(count)],
        out_specs=[ANYWHERE if k in anywhere else VMEM for k in range(len(outs))],
        scratch_shapes=list(scratch),
        input_output_aliases=aliases,
        compiler_params=pltpu.CompilerParams(vmem_limit_bytes=32 * 2**20),
        cost_estimate=pl.CostEstimate(flops=flops, bytes_accessed=traffic, transcendentals=0),
    )


def exchange_pairs():
    along_x = [[(k, (k + 1) % N_CURVE) for k in range(start, N_CURVE, 2)] for start in (0, 1)]
    along_y = [[(k, (k + 1) % N_SEG) for k in range(start, N_SEG, 2)] for start in (0, 1)]
    both = lambda pairs: pairs + [(b, a) for a, b in pairs]
    return [("curve", both(p)) for p in along_x] + [("seg", both(p)) for p in along_y]


def shards(adjoint, material, face_partner, send_faces, migration, children):
    own_seg = lax.axis_index("seg")
    owner, slot, octant = migration[0], migration[1], migration[2]
    key = jnp.where(owner == own_seg, slot, P_DEV + 2 * owner + slot)
    first = octant == 0
    rank = jnp.sum((first[:, None] & (key[:, None] < key[None, :])).astype(jnp.int32), axis=0)
    place = octant * P_DEV + rank
    place = jnp.concatenate([place, place]).reshape(1, 128)
    keys = jnp.sum(
        jnp.where(first[:, None] & (rank[:, None] == jnp.arange(P_DEV)[None, :]), key[:, None], 0), axis=0
    )
    stays = children[0] == own_seg
    group = jnp.sum((keys[:, None] < jnp.arange(P_DEV)[None, :]).astype(jnp.int32), axis=0)
    source = jnp.stack([jnp.where(stays, group, children[0]), jnp.where(stays, -1, children[1])])

    state = shape(9, 4, 64, 128)
    table_y = shape(LOCAL, 256, dtype=BF)
    table = shape(LOCAL, 512, dtype=BF)
    sent = shape(32, 256, dtype=BF)
    face_part = shape(LOCAL, LOCAL)
    payload = [shape(CAP, LOCAL)] * 4
    face_scratch = pltpu.VMEM((LOCAL, LOCAL), F32)
    turn = pltpu.VMEM((NODES, 128), F32)

    zero = jnp.float32(0)
    pack = lax.pad(material[None], zero, ((0, 0, 0), (0, 5, 0), (0, 64, 0))) + lax.pad(
        send_faces, jnp.int32(0), ((0, 0, 0), (3, 1, 0), (0, 128 - CAP, 0))
    ).astype(F32)
    faces = jnp.pad(face_partner.T.astype(F32), ((0, 2), (0, 64)))
    outs = call(
        begin_kernel,
        [state, table_y, table, shape(3, 8, 128), sent, sent] + payload,
        [pltpu.VMEM((3, NODES, 128), F32), pltpu.VMEM((128, 128), F32)],
        count=4,
    )(pack, adjoint[0:3], adjoint[3:6], adjoint[6:9])
    v, ty, t, mat, send_x, send_y = outs[:6]
    out_going = outs[6:]
    pairs = exchange_pairs()
    for step in range(1, 5):
        factor = time_step / step
        order = (1, 0, 3, 2) if step == 3 else (3, 2, 1, 0)
        arrived = [lax.ppermute(out_going[k], *pairs[k]) for k in order]
        if step == 1:
            vol, part, local_y, local, remote_hot = call(
                functools.partial(first_volume_kernel, factor),
                [
                    state,
                    face_part,
                    shape(256, LOCAL, dtype=BF),
                    shape(512, LOCAL, dtype=BF),
                    shape(128, LOCAL, dtype=BF),
                ],
                count=5,
            )(faces, v, ty, t, mat)
            acc = v
        elif step < 4:
            vol, part, acc = call(
                functools.partial(volume_kernel, factor), [state, face_part, state], count=7
            )(v, ty, t, local_y, local, mat, acc)
        else:
            vol, part = call(functools.partial(last_volume_kernel, factor), [state, face_part], count=7)(
                v, ty, t, local_y, local, mat, acc
            )
        if step < 4:
            outs = call(
                functools.partial(finish_kernel, factor, order),
                [state, table_y, table] + payload,
                [face_scratch],
                aliases={0: 0},
                count=10,
            )(vol, part, *arrived, remote_hot, mat, send_x, send_y)
            v, ty, t, out_going = outs[0], outs[1], outs[2], outs[3:]
    wa, wb, lines = (jnp.asarray(x) for x in refine_parts())
    total, groups, away = call(
        functools.partial(end_kernel, factor, order),
        [state, shape(9, 4, P_DEV, 128), shape(N_SEG, 2, 9, 4, 128)],
        [
            face_scratch,
            pltpu.VMEM((9, NODES, 128), F32),
            pltpu.VMEM((9, 64, NODES), F32),
            pltpu.VMEM((9, 128, 256), F32),
            pltpu.VMEM((9, 128, 128), F32),
            pltpu.VMEM((P_DEV, 9, 4, 128), F32),
            pltpu.SemaphoreType.DMA((P_DEV,)),
        ],
        anywhere=(2,),
        smem=(0,),
        aliases={1: 0},
        count=12,
    )(keys, vol, part, *arrived, remote_hot, place, wa, wb, lines)
    fetched = lax.all_to_all(away, "seg", split_axis=0, concat_axis=0, tiled=True)
    updated = call(next_kernel, [shape(9, E_DEV, NODES)], [turn], count=1)(total)[0]
    parents = call(parent_kernel, [shape(9, P_DEV, NODES)], smem=(0,), count=3)(source, groups, fetched)[0]
    return (updated, parents)


def solution(mesh):
    in_specs = (
        P(None, ("curve", "seg"), None),
        P(None, ("curve", "seg")),
        P(("curve", "seg"), None),
        P(("curve", "seg"), None, None),
        P(None, ("curve", "seg")),
        P(None, ("curve", "seg")),
    )
    out_specs = (P(None, ("curve", "seg"), None), P(None, ("curve", "seg"), None))
    return jax.shard_map(shards, mesh=mesh, in_specs=in_specs, out_specs=out_specs, check_vma=False)
```

```python
import functools

import jax
import jax.numpy as jnp
import numpy as np
from jax import lax
from jax.experimental import pallas as pl
from jax.experimental.pallas import tpu as pltpu
from jax.sharding import PartitionSpec as P

NP = 8
NODES = 512
E_DEV = 64
CAP = 16
P_DEV = 8
N_CURVE = 8
N_SEG = 16
LOCAL = 6 * E_DEV

voigt_index = ((3, 8, 7), (8, 4, 6), (7, 6, 5))
time_step = 0.8 / (NP * NP)
lift_half = 0.25 * NP * (NP - 1)
BF = jnp.bfloat16
F32 = jnp.float32


def lobatto_nodes(edge_nodes):
    return -np.cos(np.pi * np.arange(edge_nodes) / (edge_nodes - 1))


def derivative_line(edge_nodes):
    points = lobatto_nodes(edge_nodes)
    node_ids = np.arange(edge_nodes)
    weight = np.where((node_ids == 0) | (node_ids == edge_nodes - 1), 2.0, 1.0)
    row_ids = node_ids[:, None]
    column_ids = node_ids[None, :]
    differ = points[:, None] - points[None, :]
    safe_gap = np.where(row_ids == column_ids, 1.0, differ)
    matrix = weight[:, None] / weight[None, :] * (-1.0) ** (row_ids + column_ids) / safe_gap
    matrix = np.where(row_ids == column_ids, 0.0, matrix)
    return matrix - np.eye(edge_nodes) * matrix.sum(axis=1)[:, None]


def refine_line(edge_nodes, upper):
    points = lobatto_nodes(edge_nodes)
    targets = (points + (2.0 * upper - 1.0)) / 2.0
    columns = []
    for column in range(edge_nodes):
        factor = np.ones(edge_nodes)
        for other_node in range(edge_nodes):
            if other_node != column:
                factor = (
                    factor * (targets - points[other_node]) / (points[column] - points[other_node])
                )
        columns.append(factor)
    return np.stack(columns, axis=1)


def refine_parts():
    lines = [refine_line(NP, upper) for upper in range(2)]
    plane = np.concatenate([np.kron(lines[k // 2], lines[k % 2]) for k in range(4)], axis=0).astype(np.float32)
    high = plane.astype(BF)
    low = (plane - high.astype(np.float32)).astype(BF)
    columns = [
        np.repeat(lines[upper][a, 2 * t : 2 * t + 2], 64) for upper in range(2) for a in range(8) for t in range(4)
    ]
    patterns = np.broadcast_to(np.stack(columns)[:, None, :], (64, 8, 128)).astype(np.float32)
    return np.concatenate([high, low], axis=1), np.concatenate([high, high], axis=1), patterns


_line = derivative_line(NP)
_line[0, 0] += lift_half
_line[7, 7] -= lift_half
ODD = 0.5 * (_line[:4, :4] - _line[:3:-1, :4])
EVEN = 0.5 * (_line[:4, :4] + _line[:3:-1, :4])


def line_product(x):
    odd = [x[a] - x[7 - a] for a in range(4)]
    even = [x[a] + x[7 - a] for a in range(4)]
    out = [None] * 8
    for m in range(4):
        p = sum(odd[a] * float(ODD[a, m]) for a in range(4))
        q = sum(even[a] * float(EVEN[a, m]) for a in range(4))
        out[m] = p + q
        out[7 - m] = p - q
    return out


def low_half():
    return lax.broadcasted_iota(jnp.int32, (8, 128), 1) < 64


def swap_halves(x):
    return pltpu.roll(x, 64, 1)


def lane_patterns():
    low = low_half()
    out = []
    for matrix in (ODD, EVEN):
        straight = [[None] * 2 for _ in range(2)]
        crossed = [[None] * 2 for _ in range(2)]
        for j in range(2):
            for m in range(2):
                straight[j][m] = jnp.where(low, float(matrix[2 * j, 2 * m]), float(matrix[2 * j + 1, 2 * m + 1]))
                crossed[j][m] = jnp.where(low, float(matrix[2 * j + 1, 2 * m]), float(matrix[2 * j, 2 * m + 1]))
        out.append((straight, crossed))
    return out


def lane_product(x, patterns):
    back = [swap_halves(x[3]), swap_halves(x[2])]
    sums = []
    for parts, (straight, crossed) in zip(
        ([x[0] - back[0], x[1] - back[1]], [x[0] + back[0], x[1] + back[1]]), patterns
    ):
        turned = [swap_halves(part) for part in parts]
        sums.append(
            [
                parts[0] * straight[0][m] + turned[0] * crossed[0][m] + parts[1] * straight[1][m] + turned[1] * crossed[1][m]
                for m in range(2)
            ]
        )
    p, q = sums
    return [p[0] + q[0], p[1] + q[1], swap_halves(p[1] - q[1]), swap_halves(p[0] - q[0])]


def split(x):
    high = x.astype(BF)
    return high, (x - high.astype(F32)).astype(BF)


def along(k, start=None):
    return pl.ds(k, 8, stride=8)


def image_rows(get, mat, direction):
    inv_density, lame, shear = mat
    trace = get(3) + get(4) + get(5)
    out = []
    for k in range(3):
        term = shear * get(voigt_index[direction][k])
        if k == direction:
            term = 2.0 * term + lame * trace
        out.append(term)
    return out + [inv_density * get(i) for i in range(3)]


def target_row(value, direction):
    return value if value < 3 else voigt_index[value - 3][direction]


def build_table(v_ref, mat, t_ref, directions):
    low = low_half()

    def put(value, block, direction, x0, x1):
        pair = jnp.concatenate([x0, x1], axis=0)
        high, rest = split(pair)
        rows = pl.ds(value * 64 + block * 16, 16)
        column = 256 * directions.index(direction)
        t_ref[rows, pl.ds(column, 128)] = high
        t_ref[rows, pl.ds(column + 128, 128)] = rest

    for direction in directions:
        if direction == 2:
            continue
        for j in range(4):
            if direction == 0:
                ends = [image_rows(lambda i, r=r: v_ref[i, j, pl.ds(r, 8), :], mat, 0) for r in (0, 56)]
            else:
                ends = [image_rows(lambda i, r=r: v_ref[i, j, along(r), :], mat, 1) for r in (0, 7)]
            for value in range(6):
                a0, a1 = ends[0][value], ends[1][value]
                put(
                    value,
                    j,
                    direction,
                    jnp.where(low, a0, swap_halves(a1)),
                    jnp.where(low, swap_halves(a0), a1),
                )
    for pair in range(4 if 2 in directions else 0):
        blocks = []
        for b in (2 * pair, 2 * pair + 1):
            blocks.append(
                image_rows(
                    lambda i, b=b: jnp.where(
                        low, v_ref[i, 0, along(b), :], v_ref[i, 3, along(b), :]
                    ),
                    mat,
                    2,
                )
            )
        for value in range(6):
            put(value, pair, 2, blocks[0][value], blocks[1][value])


def materials(mat_ref):
    return mat_ref[0], mat_ref[1], mat_ref[2]


def send_values(send_ref, t_ref, out_refs):
    rows = lax.dot_general(
        send_ref[...], t_ref[:, pl.ds(0, 256)], (((1,), (1,)), ((), ())), preferred_element_type=F32
    )
    for k in range(2):
        out_refs[k][...] = rows[16 * k : 16 * k + 16]


def parities():
    return 1 - lax.axis_index("curve") % 2, 1 - lax.axis_index("seg") % 2


def table_lane(q):
    element = (q * 10923) >> 16
    return (q - 6 * element) * E_DEV + element


def partner_tables(faces_ref, local_y_ref, local_ref, remote_ref):
    even_x, even_y = parities()
    low_row = lax.broadcasted_iota(jnp.int32, (1, 128), 1) < 64
    weight = jnp.where(low_row, lift_half, -lift_half)
    for direction in range(3):
        q = jnp.where(
            low_row,
            faces_ref[pl.ds(2 * direction, 1), :],
            pltpu.roll(faces_ref[pl.ds(2 * direction + 1, 1), :], 64, 1),
        ).astype(jnp.int32)
        remote = q - LOCAL
        side = remote >> 4
        block = side ^ jnp.where(side < 2, even_x, even_y)
        partner = jnp.where(remote < 0, table_lane(q), LOCAL + block * CAP + (remote & 15))
        lanes = pl.ds(direction * 128, 128)
        for start in range(0, LOCAL + 64, 64):
            source = lax.broadcasted_iota(jnp.int32, (64, 128), 0) + start
            hot = jnp.where(source == partner, weight, 0.0).astype(BF)
            target = (local_ref, local_y_ref, local_ref, remote_ref)[start // 128]
            base = start % 128 + (256 if start // 128 == 2 else 0)
            gap = 64 if start == LOCAL else 128
            for part in range(2):
                target[pl.ds(base + part * gap, 64), lanes] = hot


def send_table(pack_ref, send_x_ref, send_y_ref, small_ref):
    even_x, even_y = parities()
    small_ref[pl.ds(0, 8), :] = pack_ref[0]
    small_ref[pl.ds(8, 120), :] = jnp.zeros((120, 128), F32)
    turned = small_ref[...].T
    columns = [table_lane(turned[0:CAP, 3 + r : 4 + r].astype(jnp.int32)) for r in range(4)]
    for axis, even in ((0, even_x), (1, even_y)):
        first, second = columns[2 * axis], columns[2 * axis + 1]
        for k, column in enumerate((first + even * (second - first), second + even * (first - second))):
            hot = jnp.where(
                lax.broadcasted_iota(jnp.int32, (CAP, 128), 1) + 128 * axis == column, 1.0, 0.0
            ).astype(BF)
            for part in range(2):
                (send_x_ref, send_y_ref)[axis][pl.ds(k * CAP, CAP), pl.ds(128 * part, 128)] = hot


def begin_kernel(
    pack_ref, part0, part1, part2,
    v_ref, ty_ref, t_ref, mat_ref, send_x_ref, send_y_ref, p0, p1, p2, p3, turn_ref, small_ref,
):
    low_row = lax.broadcasted_iota(jnp.int32, (1, 128), 1) < 64
    for i in range(3):
        row = pack_ref[0, pl.ds(i, 1), :]
        row = jnp.where(low_row, row, pltpu.roll(row, 64, 1))
        if i == 0:
            row = 1.0 / row
        mat_ref[i] = jnp.broadcast_to(row, (8, 128))
    send_table(pack_ref, send_x_ref, send_y_ref, small_ref)
    low = lax.broadcasted_iota(jnp.int32, (64, 128), 1) < 64
    for i in range(9):
        x = (part0, part1, part2)[i // 3][i % 3]
        turn = turn_ref.at[i % 3]
        turn[...] = jnp.concatenate([x, x], axis=0).T
        for j in range(4):
            v_ref[i, j] = jnp.where(
                low, turn[pl.ds(2 * j, 64, stride=8), :], turn[pl.ds(2 * j + 1, 64, stride=8), :]
            )
    build_table(v_ref, materials(mat_ref), ty_ref, (1,))
    send_values(send_y_ref, ty_ref, (p2, p3))
    build_table(v_ref, materials(mat_ref), t_ref, (0, 2))
    send_values(send_x_ref, t_ref, (p0, p1))


def first_volume_kernel(
    factor, faces_ref, v_ref, ty_ref, t_ref, mat_ref, vol_ref, part_ref, local_y_ref, local_ref, remote_ref
):
    partner_tables(faces_ref, local_y_ref, local_ref, remote_ref)
    volume_kernel(factor, v_ref, ty_ref, t_ref, local_y_ref, local_ref, mat_ref, None, vol_ref, part_ref, None)


def last_volume_kernel(factor, v_ref, ty_ref, t_ref, local_y_ref, local_ref, mat_ref, acc_ref, vol_ref, part_ref):
    volume_kernel(factor, v_ref, ty_ref, t_ref, local_y_ref, local_ref, mat_ref, acc_ref, vol_ref, part_ref, None)


def volume_kernel(
    factor, v_ref, ty_ref, t_ref, local_y_ref, local_ref, mat_ref, acc_ref, vol_ref, part_ref, sum_ref
):
    inv_density, lame, shear = [m * factor for m in materials(mat_ref)]

    def scaled(get, direction):
        out = []
        for k in range(3):
            if k == direction:
                out.append(
                    (k, [2.0 * shear * d + lame * (s0 + s1 + s2) for d, s0, s1, s2 in zip(get(3 + k), get(3), get(4), get(5))])
                )
            else:
                out.append((k, [shear * x for x in get(voigt_index[direction][k])]))
        for i in range(3):
            out.append((voigt_index[i][direction], [inv_density * x for x in get(i)]))
        return out

    def tiles(j):
        for row, x in scaled(lambda i: [v_ref[i, j, along(b), :] for b in range(8)], 1):
            for b, y in enumerate(line_product(x)):
                vol_ref[row, j, along(b), :] = y
        chunk = pl.ds(j * 96, 96)
        part_ref[chunk, :] = factor * (
            jnp.dot(ty_ref[chunk, :], local_y_ref[...], preferred_element_type=F32)
            + jnp.dot(t_ref[chunk, :], local_ref[...], preferred_element_type=F32)
        )
        for row, x in scaled(lambda i: [v_ref[i, j, pl.ds(8 * a, 8), :] for a in range(8)], 0):
            for a, y in enumerate(line_product(x)):
                if row not in (3, 7):
                    y = y + vol_ref[row, j, pl.ds(8 * a, 8), :]
                vol_ref[row, j, pl.ds(8 * a, 8), :] = y

    for j in range(4):
        tiles(j)
    patterns = lane_patterns()

    def groups(a, carry):
        rows = pl.ds(pl.multiple_of(a * 8, 8), 8)
        for row, x in scaled(lambda i: [v_ref[i, j, rows, :] for j in range(4)], 2):
            for j, y in enumerate(lane_product(x, patterns)):
                if row != 5:
                    y = y + vol_ref[row, j, rows, :]
                vol_ref[row, j, rows, :] = y
        if acc_ref is not None:
            for i in range(9):
                for j in range(4):
                    y = acc_ref[i, j, rows, :] + v_ref[i, j, rows, :]
                    if sum_ref is not None:
                        sum_ref[i, j, rows, :] = y
                    else:
                        vol_ref[i, j, rows, :] += y
        return carry

    lax.fori_loop(0, 8, groups, 0, unroll=4)


def add_faces(part_ref, r_refs, remote_ref, factor, out_ref, face_ref):
    arrived = jnp.concatenate([r[...] for r in r_refs], axis=0) * factor
    both = jnp.concatenate(split(arrived), axis=0)
    face_ref[...] = part_ref[...] + lax.dot_general(
        both, remote_ref[...], (((0,), (0,)), ((), ())), preferred_element_type=F32
    )
    low = low_half()
    for direction in range(3):
        for value in range(6):
            row = target_row(value, direction)
            for j in range(4):
                x0 = face_ref[pl.ds(value * 64 + 16 * j, 8), pl.ds(direction * 128, 128)]
                x1 = face_ref[pl.ds(value * 64 + 16 * j + 8, 8), pl.ds(direction * 128, 128)]
                if direction < 2:
                    y0 = jnp.where(low, x0, swap_halves(x1))
                    y1 = jnp.where(low, swap_halves(x0), x1)
                    rows = (pl.ds(0, 8), pl.ds(56, 8)) if direction == 0 else (along(0), along(7))
                    out_ref[row, j, rows[0], :] += y0
                    out_ref[row, j, rows[1], :] += y1
                else:
                    for b, x in ((2 * j, x0), (2 * j + 1, x1)):
                        out_ref[row, 0, along(b), :] += jnp.where(low, x, 0.0)
                        out_ref[row, 3, along(b), :] += jnp.where(low, 0.0, x)


def finish_kernel(
    factor, order, vol_ref, part_ref, ra, rb, rc, rd, remote_ref, mat_ref, send_x_ref, send_y_ref,
    v_ref, ty_ref, t_ref, p0, p1, p2, p3, face_ref,
):
    add_faces(part_ref, in_order(order, (ra, rb, rc, rd)), remote_ref, factor, v_ref, face_ref)
    build_table(v_ref, materials(mat_ref), ty_ref, (1,))
    send_values(send_y_ref, ty_ref, (p2, p3))
    build_table(v_ref, materials(mat_ref), t_ref, (0, 2))
    send_values(send_x_ref, t_ref, (p0, p1))


def in_order(order, refs):
    return [refs[order.index(k)] for k in range(4)]


def end_kernel(
    factor, order, keys_ref, vol_ref, part_ref, ra, rb, rc, rd, remote_ref, place_ref, wa_ref, wb_ref, lines_ref,
    total_ref, parent_ref, away_ref, face_ref, turn_ref, ranked_ref, rows_ref, plane_ref, block_ref, sem,
):
    add_faces(part_ref, in_order(order, (ra, rb, rc, rd)), remote_ref, factor, total_ref, face_ref)
    place = jnp.where(
        lax.broadcasted_iota(jnp.int32, (64, 128), 0) == place_ref[...], 1.0, 0.0
    ).astype(BF)
    wide = lax.broadcasted_iota(jnp.int32, (64, 128), 1) < 64
    low = low_half()
    for i in range(9):
        for j in range(4):
            tile = total_ref[i, j]
            high = tile.astype(BF).astype(F32)
            rest = tile - high
            turn_ref[i, pl.ds(2 * j, 64, stride=8), :] = jnp.where(wide, high, pltpu.roll(rest, 64, 1))
            turn_ref[i, pl.ds(2 * j + 1, 64, stride=8), :] = jnp.where(wide, pltpu.roll(high, 64, 1), rest)
        ranked_ref[i] = lax.dot_general(
            place, turn_ref[i].astype(BF), (((1,), (1,)), ((), ())), preferred_element_type=F32
        )
    for i in range(9):
        for upper in range(2):
            for t in range(4):
                x = [ranked_ref[i, pl.ds(8 * (4 * upper + k), 8), pl.ds(128 * t, 128)] for k in range(4)]
                for pair in range(2):
                    x0, x1 = x[2 * pair], x[2 * pair + 1]
                    lanes = pl.ds(128 * pair, 128)
                    rows_ref[i, pl.ds(64 * upper + 16 * t, 8), lanes] = jnp.where(low, x0, swap_halves(x1))
                    rows_ref[i, pl.ds(64 * upper + 16 * t + 8, 8), lanes] = jnp.where(low, swap_halves(x0), x1)
        high, rest = split(rows_ref[i])
        plane = jnp.dot(high, wa_ref[...], preferred_element_type=F32)
        plane_ref[i] = plane + pltpu.roll(plane, 64, 1) + jnp.dot(rest, wb_ref[...], preferred_element_type=F32)
    for t in range(4):
        sums = [None] * 9
        for k in range(16):
            line = lines_ref[4 * k + t]
            for i in range(9):
                term = plane_ref[i, pl.ds(8 * k, 8), :] * line
                sums[i] = term if k == 0 else sums[i] + term
        for i in range(9):
            parent_ref[i, t] = sums[i]
    def send(g):
        place = keys_ref[g] - P_DEV
        return pltpu.make_async_copy(block_ref.at[g], away_ref.at[place // 2, place % 2], sem.at[g])

    for g in range(P_DEV):

        @pl.when(keys_ref[g] >= P_DEV)
        def _():
            for i in range(9):
                for t in range(4):
                    block_ref[g, i, pl.ds(t, 1), :] = parent_ref[i, t, pl.ds(g, 1), :]
            send(g).start()

    for g in range(P_DEV):

        @pl.when(keys_ref[g] >= P_DEV)
        def _():
            send(g).wait()


def next_kernel(table_ref, total_ref, groups_ref, next_ref, home_ref, turn_ref):
    home_ref[...] = jnp.zeros_like(home_ref)
    for p in range(P_DEV):

        @pl.when(table_ref[1, p] < 0)
        def _():
            for i in range(9):
                for t in range(4):
                    home_ref[i, pl.ds(p, 1), pl.ds(128 * t, 128)] = groups_ref[i, t, pl.ds(table_ref[0, p], 1), :]

    def body(i, carry):
        for j in range(4):
            tile = total_ref[i, j]
            turn_ref[pl.ds(2 * j, 64, stride=8), :] = tile
            turn_ref[pl.ds(2 * j + 1, 64, stride=8), :] = pltpu.roll(tile, 64, 1)
        next_ref[i] = turn_ref[...].T[:64]
        return carry

    lax.fori_loop(0, 9, body, 0)


def parent_kernel(table_ref, home_ref, arrived_ref, out_ref):
    out_ref[...] = home_ref[...]
    for p in range(P_DEV):
        holder = table_ref[0, p]
        slot = table_ref[1, p]

        @pl.when(slot >= 0)
        def _():
            for i in range(9):
                for t in range(4):
                    out_ref[i, pl.ds(p, 1), pl.ds(128 * t, 128)] = arrived_ref[
                        holder, slot, i, pl.ds(t, 1), :
                    ]


def shape(*dims, dtype=F32):
    return jax.ShapeDtypeStruct(dims, dtype)


VMEM = pl.BlockSpec(memory_space=pltpu.VMEM)
SMEM = pl.BlockSpec(memory_space=pltpu.SMEM)
ANYWHERE = pl.BlockSpec(memory_space=pl.ANY)


def call(kernel, outs, scratch=(), smem=(), anywhere=(), aliases={}, count=0, flops=10**8, traffic=6 * 10**6):
    return pl.pallas_call(
        kernel,
        out_shape=outs,
        in_specs=[SMEM if k in smem else VMEM for k in range(count)],
        out_specs=[ANYWHERE if k in anywhere else VMEM for k in range(len(outs))],
        scratch_shapes=list(scratch),
        input_output_aliases=aliases,
        compiler_params=pltpu.CompilerParams(vmem_limit_bytes=32 * 2**20),
        cost_estimate=pl.CostEstimate(flops=flops, bytes_accessed=traffic, transcendentals=0),
    )


def exchange_pairs():
    along_x = [[(k, (k + 1) % N_CURVE) for k in range(start, N_CURVE, 2)] for start in (0, 1)]
    along_y = [[(k, (k + 1) % N_SEG) for k in range(start, N_SEG, 2)] for start in (0, 1)]
    both = lambda pairs: pairs + [(b, a) for a, b in pairs]
    return [("curve", both(p)) for p in along_x] + [("seg", both(p)) for p in along_y]


def shards(adjoint, material, face_partner, send_faces, migration, children):
    own_seg = lax.axis_index("seg")
    owner, slot, octant = migration[0], migration[1], migration[2]
    key = jnp.where(owner == own_seg, slot, P_DEV + 2 * owner + slot)
    first = octant == 0
    rank = jnp.sum((first[:, None] & (key[:, None] < key[None, :])).astype(jnp.int32), axis=0)
    place = octant * P_DEV + rank
    place = jnp.concatenate([place, place]).reshape(1, 128)
    keys = jnp.sum(
        jnp.where(first[:, None] & (rank[:, None] == jnp.arange(P_DEV)[None, :]), key[:, None], 0), axis=0
    )
    stays = children[0] == own_seg
    group = jnp.sum((keys[:, None] < jnp.arange(P_DEV)[None, :]).astype(jnp.int32), axis=0)
    source = jnp.stack([jnp.where(stays, group, children[0]), jnp.where(stays, -1, children[1])])

    state = shape(9, 4, 64, 128)
    table_y = shape(LOCAL, 256, dtype=BF)
    table = shape(LOCAL, 512, dtype=BF)
    sent = shape(32, 256, dtype=BF)
    face_part = shape(LOCAL, LOCAL)
    payload = [shape(CAP, LOCAL)] * 4
    face_scratch = pltpu.VMEM((LOCAL, LOCAL), F32)
    turn = pltpu.VMEM((NODES, 128), F32)

    zero = jnp.float32(0)
    pack = lax.pad(material[None], zero, ((0, 0, 0), (0, 5, 0), (0, 64, 0))) + lax.pad(
        send_faces, jnp.int32(0), ((0, 0, 0), (3, 1, 0), (0, 128 - CAP, 0))
    ).astype(F32)
    faces = jnp.pad(face_partner.T.astype(F32), ((0, 2), (0, 64)))
    outs = call(
        begin_kernel,
        [state, table_y, table, shape(3, 8, 128), sent, sent] + payload,
        [pltpu.VMEM((3, NODES, 128), F32), pltpu.VMEM((128, 128), F32)],
        count=4,
    )(pack, adjoint[0:3], adjoint[3:6], adjoint[6:9])
    v, ty, t, mat, send_x, send_y = outs[:6]
    out_going = outs[6:]
    pairs = exchange_pairs()
    for step in range(1, 5):
        factor = time_step / step
        order = (1, 0, 3, 2) if step == 3 else (3, 2, 1, 0)
        arrived = [lax.ppermute(out_going[k], *pairs[k]) for k in order]
        if step == 1:
            vol, part, local_y, local, remote_hot = call(
                functools.partial(first_volume_kernel, factor),
                [
                    state,
                    face_part,
                    shape(256, LOCAL, dtype=BF),
                    shape(512, LOCAL, dtype=BF),
                    shape(128, LOCAL, dtype=BF),
                ],
                count=5,
            )(faces, v, ty, t, mat)
            acc = v
        elif step < 4:
            vol, part, acc = call(
                functools.partial(volume_kernel, factor), [state, face_part, state], count=7
            )(v, ty, t, local_y, local, mat, acc)
        else:
            vol, part = call(functools.partial(last_volume_kernel, factor), [state, face_part], count=7)(
                v, ty, t, local_y, local, mat, acc
            )
        if step < 4:
            outs = call(
                functools.partial(finish_kernel, factor, order),
                [state, table_y, table] + payload,
                [face_scratch],
                aliases={0: 0},
                count=10,
            )(vol, part, *arrived, remote_hot, mat, send_x, send_y)
            v, ty, t, out_going = outs[0], outs[1], outs[2], outs[3:]
    wa, wb, lines = (jnp.asarray(x) for x in refine_parts())
    total, groups, away = call(
        functools.partial(end_kernel, factor, order),
        [state, shape(9, 4, P_DEV, 128), shape(N_SEG, 2, 9, 4, 128)],
        [
            face_scratch,
            pltpu.VMEM((9, NODES, 128), F32),
            pltpu.VMEM((9, 64, NODES), F32),
            pltpu.VMEM((9, 128, 256), F32),
            pltpu.VMEM((9, 128, 128), F32),
            pltpu.VMEM((P_DEV, 9, 4, 128), F32),
            pltpu.SemaphoreType.DMA((P_DEV,)),
        ],
        anywhere=(2,),
        smem=(0,),
        aliases={1: 0},
        count=12,
    )(keys, vol, part, *arrived, remote_hot, place, wa, wb, lines)
    fetched = lax.all_to_all(away, "seg", split_axis=0, concat_axis=0, tiled=True)
    updated, home = call(
        next_kernel, [shape(9, E_DEV, NODES), shape(9, P_DEV, NODES)], [turn], smem=(0,), count=3
    )(source, total, groups)
    parents = call(parent_kernel, [shape(9, P_DEV, NODES)], smem=(0,), count=3)(source, home, fetched)[0]
    return (updated, parents)


def solution(mesh):
    in_specs = (
        P(None, ("curve", "seg"), None),
        P(None, ("curve", "seg")),
        P(("curve", "seg"), None),
        P(("curve", "seg"), None, None),
        P(None, ("curve", "seg")),
        P(None, ("curve", "seg")),
    )
    out_specs = (P(None, ("curve", "seg"), None), P(None, ("curve", "seg"), None))
    return jax.shard_map(shards, mesh=mesh, in_specs=in_specs, out_specs=out_specs, check_vma=False)
```

```python
import functools

import jax
import jax.numpy as jnp
import numpy as np
from jax import lax
from jax.experimental import pallas as pl
from jax.experimental.pallas import tpu as pltpu
from jax.sharding import PartitionSpec as P

NP = 8
NODES = 512
E_DEV = 64
CAP = 16
P_DEV = 8
N_CURVE = 8
N_SEG = 16
LOCAL = 6 * E_DEV

voigt_index = ((3, 8, 7), (8, 4, 6), (7, 6, 5))
time_step = 0.8 / (NP * NP)
lift_half = 0.25 * NP * (NP - 1)
BF = jnp.bfloat16
F32 = jnp.float32


def lobatto_nodes(edge_nodes):
    return -np.cos(np.pi * np.arange(edge_nodes) / (edge_nodes - 1))


def derivative_line(edge_nodes):
    points = lobatto_nodes(edge_nodes)
    node_ids = np.arange(edge_nodes)
    weight = np.where((node_ids == 0) | (node_ids == edge_nodes - 1), 2.0, 1.0)
    row_ids = node_ids[:, None]
    column_ids = node_ids[None, :]
    differ = points[:, None] - points[None, :]
    safe_gap = np.where(row_ids == column_ids, 1.0, differ)
    matrix = weight[:, None] / weight[None, :] * (-1.0) ** (row_ids + column_ids) / safe_gap
    matrix = np.where(row_ids == column_ids, 0.0, matrix)
    return matrix - np.eye(edge_nodes) * matrix.sum(axis=1)[:, None]


def refine_line(edge_nodes, upper):
    points = lobatto_nodes(edge_nodes)
    targets = (points + (2.0 * upper - 1.0)) / 2.0
    columns = []
    for column in range(edge_nodes):
        factor = np.ones(edge_nodes)
        for other_node in range(edge_nodes):
            if other_node != column:
                factor = (
                    factor * (targets - points[other_node]) / (points[column] - points[other_node])
                )
        columns.append(factor)
    return np.stack(columns, axis=1)


def refine_parts():
    lines = [refine_line(NP, upper) for upper in range(2)]
    plane = np.concatenate([np.kron(lines[k // 2], lines[k % 2]) for k in range(4)], axis=0).astype(np.float32)
    high = plane.astype(BF)
    low = (plane - high.astype(np.float32)).astype(BF)
    columns = [
        np.repeat(lines[upper][a, 2 * t : 2 * t + 2], 64) for upper in range(2) for a in range(8) for t in range(4)
    ]
    patterns = np.broadcast_to(np.stack(columns)[:, None, :], (64, 8, 128)).astype(np.float32)
    return np.concatenate([high, low], axis=1), np.concatenate([high, high], axis=1), patterns


_line = derivative_line(NP)
_line[0, 0] += lift_half
_line[7, 7] -= lift_half
ODD = 0.5 * (_line[:4, :4] - _line[:3:-1, :4])
EVEN = 0.5 * (_line[:4, :4] + _line[:3:-1, :4])


def line_product(x):
    odd = [x[a] - x[7 - a] for a in range(4)]
    even = [x[a] + x[7 - a] for a in range(4)]
    out = [None] * 8
    for m in range(4):
        p = sum(odd[a] * float(ODD[a, m]) for a in range(4))
        q = sum(even[a] * float(EVEN[a, m]) for a in range(4))
        out[m] = p + q
        out[7 - m] = p - q
    return out


def low_half():
    return lax.broadcasted_iota(jnp.int32, (8, 128), 1) < 64


def swap_halves(x):
    return pltpu.roll(x, 64, 1)


def lane_patterns():
    low = low_half()
    out = []
    for matrix in (ODD, EVEN):
        straight = [[None] * 2 for _ in range(2)]
        crossed = [[None] * 2 for _ in range(2)]
        for j in range(2):
            for m in range(2):
                straight[j][m] = jnp.where(low, float(matrix[2 * j, 2 * m]), float(matrix[2 * j + 1, 2 * m + 1]))
                crossed[j][m] = jnp.where(low, float(matrix[2 * j + 1, 2 * m]), float(matrix[2 * j, 2 * m + 1]))
        out.append((straight, crossed))
    return out


def lane_product(x, patterns):
    back = [swap_halves(x[3]), swap_halves(x[2])]
    sums = []
    for parts, (straight, crossed) in zip(
        ([x[0] - back[0], x[1] - back[1]], [x[0] + back[0], x[1] + back[1]]), patterns
    ):
        turned = [swap_halves(part) for part in parts]
        sums.append(
            [
                parts[0] * straight[0][m] + turned[0] * crossed[0][m] + parts[1] * straight[1][m] + turned[1] * crossed[1][m]
                for m in range(2)
            ]
        )
    p, q = sums
    return [p[0] + q[0], p[1] + q[1], swap_halves(p[1] - q[1]), swap_halves(p[0] - q[0])]


def split(x):
    high = x.astype(BF)
    return high, (x - high.astype(F32)).astype(BF)


def along(k, start=None):
    return pl.ds(k, 8, stride=8)


def image_rows(get, mat, direction):
    inv_density, lame, shear = mat
    trace = get(3) + get(4) + get(5)
    out = []
    for k in range(3):
        term = shear * get(voigt_index[direction][k])
        if k == direction:
            term = 2.0 * term + lame * trace
        out.append(term)
    return out + [inv_density * get(i) for i in range(3)]


def target_row(value, direction):
    return value if value < 3 else voigt_index[value - 3][direction]


def build_table(v_ref, mat, t_ref, directions):
    low = low_half()

    def put(value, block, direction, x0, x1):
        pair = jnp.concatenate([x0, x1], axis=0)
        high, rest = split(pair)
        rows = pl.ds(value * 64 + block * 16, 16)
        column = 256 * directions.index(direction)
        t_ref[rows, pl.ds(column, 128)] = high
        t_ref[rows, pl.ds(column + 128, 128)] = rest

    for direction in directions:
        if direction == 2:
            continue
        for j in range(4):
            if direction == 0:
                ends = [image_rows(lambda i, r=r: v_ref[i, j, pl.ds(r, 8), :], mat, 0) for r in (0, 56)]
            else:
                ends = [image_rows(lambda i, r=r: v_ref[i, j, along(r), :], mat, 1) for r in (0, 7)]
            for value in range(6):
                a0, a1 = ends[0][value], ends[1][value]
                put(
                    value,
                    j,
                    direction,
                    jnp.where(low, a0, swap_halves(a1)),
                    jnp.where(low, swap_halves(a0), a1),
                )
    for pair in range(4 if 2 in directions else 0):
        blocks = []
        for b in (2 * pair, 2 * pair + 1):
            blocks.append(
                image_rows(
                    lambda i, b=b: jnp.where(
                        low, v_ref[i, 0, along(b), :], v_ref[i, 3, along(b), :]
                    ),
                    mat,
                    2,
                )
            )
        for value in range(6):
            put(value, pair, 2, blocks[0][value], blocks[1][value])


def materials(mat_ref):
    return mat_ref[0], mat_ref[1], mat_ref[2]


def send_values(send_ref, t_ref, out_refs):
    rows = lax.dot_general(
        send_ref[...], t_ref[:, pl.ds(0, 256)], (((1,), (1,)), ((), ())), preferred_element_type=F32
    )
    for k in range(2):
        out_refs[k][...] = rows[16 * k : 16 * k + 16]


def parities():
    return 1 - lax.axis_index("curve") % 2, 1 - lax.axis_index("seg") % 2


def table_lane(q):
    element = (q * 10923) >> 16
    return (q - 6 * element) * E_DEV + element


def partner_tables(faces_ref, local_y_ref, local_ref, remote_ref):
    even_x, even_y = parities()
    low_row = lax.broadcasted_iota(jnp.int32, (1, 128), 1) < 64
    weight = jnp.where(low_row, lift_half, -lift_half)
    for direction in range(3):
        q = jnp.where(
            low_row,
            faces_ref[pl.ds(2 * direction, 1), :],
            pltpu.roll(faces_ref[pl.ds(2 * direction + 1, 1), :], 64, 1),
        ).astype(jnp.int32)
        remote = q - LOCAL
        side = remote >> 4
        block = side ^ jnp.where(side < 2, even_x, even_y)
        partner = jnp.where(remote < 0, table_lane(q), LOCAL + block * CAP + (remote & 15))
        lanes = pl.ds(direction * 128, 128)
        for start in range(0, LOCAL + 64, 64):
            source = lax.broadcasted_iota(jnp.int32, (64, 128), 0) + start
            hot = jnp.where(source == partner, weight, 0.0).astype(BF)
            target = (local_ref, local_y_ref, local_ref, remote_ref)[start // 128]
            base = start % 128 + (256 if start // 128 == 2 else 0)
            gap = 64 if start == LOCAL else 128
            for part in range(2):
                target[pl.ds(base + part * gap, 64), lanes] = hot


def send_table(pack_ref, send_x_ref, send_y_ref, small_ref):
    even_x, even_y = parities()
    small_ref[pl.ds(0, 8), :] = pack_ref[0]
    small_ref[pl.ds(8, 120), :] = jnp.zeros((120, 128), F32)
    turned = small_ref[...].T
    columns = [table_lane(turned[0:CAP, 3 + r : 4 + r].astype(jnp.int32)) for r in range(4)]
    for axis, even in ((0, even_x), (1, even_y)):
        first, second = columns[2 * axis], columns[2 * axis + 1]
        for k, column in enumerate((first + even * (second - first), second + even * (first - second))):
            hot = jnp.where(
                lax.broadcasted_iota(jnp.int32, (CAP, 128), 1) + 128 * axis == column, 1.0, 0.0
            ).astype(BF)
            for part in range(2):
                (send_x_ref, send_y_ref)[axis][pl.ds(k * CAP, CAP), pl.ds(128 * part, 128)] = hot


def begin_kernel(
    pack_ref, part0, part1, part2,
    v_ref, ty_ref, t_ref, mat_ref, send_x_ref, send_y_ref, p0, p1, p2, p3, turn_ref, small_ref,
):
    low_row = lax.broadcasted_iota(jnp.int32, (1, 128), 1) < 64
    for i in range(3):
        row = pack_ref[0, pl.ds(i, 1), :]
        row = jnp.where(low_row, row, pltpu.roll(row, 64, 1))
        if i == 0:
            row = 1.0 / row
        mat_ref[i] = jnp.broadcast_to(row, (8, 128))
    send_table(pack_ref, send_x_ref, send_y_ref, small_ref)
    low = lax.broadcasted_iota(jnp.int32, (64, 128), 1) < 64
    for i in range(9):
        x = (part0, part1, part2)[i // 3][i % 3]
        turn = turn_ref.at[i % 3]
        turn[...] = jnp.concatenate([x, x], axis=0).T
        for j in range(4):
            v_ref[i, j] = jnp.where(
                low, turn[pl.ds(2 * j, 64, stride=8), :], turn[pl.ds(2 * j + 1, 64, stride=8), :]
            )
    build_table(v_ref, materials(mat_ref), ty_ref, (1,))
    send_values(send_y_ref, ty_ref, (p2, p3))
    build_table(v_ref, materials(mat_ref), t_ref, (0, 2))
    send_values(send_x_ref, t_ref, (p0, p1))


def first_volume_kernel(
    factor, faces_ref, v_ref, ty_ref, t_ref, mat_ref, vol_ref, part_ref, local_y_ref, local_ref, remote_ref
):
    partner_tables(faces_ref, local_y_ref, local_ref, remote_ref)
    volume_kernel(factor, v_ref, ty_ref, t_ref, local_y_ref, local_ref, mat_ref, None, vol_ref, part_ref, None)


def last_volume_kernel(factor, v_ref, ty_ref, t_ref, local_y_ref, local_ref, mat_ref, acc_ref, vol_ref, part_ref):
    volume_kernel(factor, v_ref, ty_ref, t_ref, local_y_ref, local_ref, mat_ref, acc_ref, vol_ref, part_ref, None)


def volume_kernel(
    factor, v_ref, ty_ref, t_ref, local_y_ref, local_ref, mat_ref, acc_ref, vol_ref, part_ref, sum_ref
):
    inv_density, lame, shear = [m * factor for m in materials(mat_ref)]

    def scaled(get, direction):
        out = []
        for k in range(3):
            if k == direction:
                out.append(
                    (k, [2.0 * shear * d + lame * (s0 + s1 + s2) for d, s0, s1, s2 in zip(get(3 + k), get(3), get(4), get(5))])
                )
            else:
                out.append((k, [shear * x for x in get(voigt_index[direction][k])]))
        for i in range(3):
            out.append((voigt_index[i][direction], [inv_density * x for x in get(i)]))
        return out

    def tiles(j):
        for row, x in scaled(lambda i: [v_ref[i, j, along(b), :] for b in range(8)], 1):
            for b, y in enumerate(line_product(x)):
                vol_ref[row, j, along(b), :] = y
        chunk = pl.ds(j * 96, 96)
        part_ref[chunk, :] = factor * (
            jnp.dot(ty_ref[chunk, :], local_y_ref[...], preferred_element_type=F32)
            + jnp.dot(t_ref[chunk, :], local_ref[...], preferred_element_type=F32)
        )
        for row, x in scaled(lambda i: [v_ref[i, j, pl.ds(8 * a, 8), :] for a in range(8)], 0):
            for a, y in enumerate(line_product(x)):
                if row not in (3, 7):
                    y = y + vol_ref[row, j, pl.ds(8 * a, 8), :]
                vol_ref[row, j, pl.ds(8 * a, 8), :] = y

    for j in range(4):
        tiles(j)
    patterns = lane_patterns()

    def groups(a, carry):
        rows = pl.ds(pl.multiple_of(a * 8, 8), 8)
        for row, x in scaled(lambda i: [v_ref[i, j, rows, :] for j in range(4)], 2):
            for j, y in enumerate(lane_product(x, patterns)):
                if row != 5:
                    y = y + vol_ref[row, j, rows, :]
                vol_ref[row, j, rows, :] = y
        if acc_ref is not None:
            for i in range(9):
                for j in range(4):
                    y = acc_ref[i, j, rows, :] + v_ref[i, j, rows, :]
                    if sum_ref is not None:
                        sum_ref[i, j, rows, :] = y
                    else:
                        vol_ref[i, j, rows, :] += y
        return carry

    lax.fori_loop(0, 8, groups, 0, unroll=4)


def add_faces(part_ref, r_refs, remote_ref, factor, out_ref, face_ref):
    arrived = jnp.concatenate([r[...] for r in r_refs], axis=0) * factor
    both = jnp.concatenate(split(arrived), axis=0)
    face_ref[...] = part_ref[...] + lax.dot_general(
        both, remote_ref[...], (((0,), (0,)), ((), ())), preferred_element_type=F32
    )
    low = low_half()
    for direction in range(3):
        for value in range(6):
            row = target_row(value, direction)
            for j in range(4):
                x0 = face_ref[pl.ds(value * 64 + 16 * j, 8), pl.ds(direction * 128, 128)]
                x1 = face_ref[pl.ds(value * 64 + 16 * j + 8, 8), pl.ds(direction * 128, 128)]
                if direction < 2:
                    y0 = jnp.where(low, x0, swap_halves(x1))
                    y1 = jnp.where(low, swap_halves(x0), x1)
                    rows = (pl.ds(0, 8), pl.ds(56, 8)) if direction == 0 else (along(0), along(7))
                    out_ref[row, j, rows[0], :] += y0
                    out_ref[row, j, rows[1], :] += y1
                else:
                    for b, x in ((2 * j, x0), (2 * j + 1, x1)):
                        out_ref[row, 0, along(b), :] += jnp.where(low, x, 0.0)
                        out_ref[row, 3, along(b), :] += jnp.where(low, 0.0, x)


def finish_kernel(
    factor, order, vol_ref, part_ref, ra, rb, rc, rd, remote_ref, mat_ref, send_x_ref, send_y_ref,
    v_ref, ty_ref, t_ref, p0, p1, p2, p3, face_ref,
):
    add_faces(part_ref, in_order(order, (ra, rb, rc, rd)), remote_ref, factor, v_ref, face_ref)
    build_table(v_ref, materials(mat_ref), ty_ref, (1,))
    build_table(v_ref, materials(mat_ref), t_ref, (0, 2))
    send_values(send_y_ref, ty_ref, (p2, p3))
    send_values(send_x_ref, t_ref, (p0, p1))


def in_order(order, refs):
    return [refs[order.index(k)] for k in range(4)]


def end_kernel(
    factor, order, keys_ref, vol_ref, part_ref, ra, rb, rc, rd, remote_ref, place_ref, wa_ref, wb_ref, lines_ref,
    total_ref, parent_ref, away_ref, face_ref, turn_ref, ranked_ref, rows_ref, plane_ref, block_ref, sem,
):
    add_faces(part_ref, in_order(order, (ra, rb, rc, rd)), remote_ref, factor, total_ref, face_ref)
    place = jnp.where(
        lax.broadcasted_iota(jnp.int32, (64, 128), 0) == place_ref[...], 1.0, 0.0
    ).astype(BF)
    wide = lax.broadcasted_iota(jnp.int32, (64, 128), 1) < 64
    low = low_half()
    for i in range(9):
        for j in range(4):
            tile = total_ref[i, j]
            high = tile.astype(BF).astype(F32)
            rest = tile - high
            turn_ref[i, pl.ds(2 * j, 64, stride=8), :] = jnp.where(wide, high, pltpu.roll(rest, 64, 1))
            turn_ref[i, pl.ds(2 * j + 1, 64, stride=8), :] = jnp.where(wide, pltpu.roll(high, 64, 1), rest)
        ranked_ref[i] = lax.dot_general(
            place, turn_ref[i].astype(BF), (((1,), (1,)), ((), ())), preferred_element_type=F32
        )
    for i in range(9):
        for upper in range(2):
            for t in range(4):
                x = [ranked_ref[i, pl.ds(8 * (4 * upper + k), 8), pl.ds(128 * t, 128)] for k in range(4)]
                for pair in range(2):
                    x0, x1 = x[2 * pair], x[2 * pair + 1]
                    lanes = pl.ds(128 * pair, 128)
                    rows_ref[i, pl.ds(64 * upper + 16 * t, 8), lanes] = jnp.where(low, x0, swap_halves(x1))
                    rows_ref[i, pl.ds(64 * upper + 16 * t + 8, 8), lanes] = jnp.where(low, swap_halves(x0), x1)
        high, rest = split(rows_ref[i])
        plane = jnp.dot(high, wa_ref[...], preferred_element_type=F32)
        plane_ref[i] = plane + pltpu.roll(plane, 64, 1) + jnp.dot(rest, wb_ref[...], preferred_element_type=F32)
    for t in range(4):
        sums = [None] * 9
        for k in range(16):
            line = lines_ref[4 * k + t]
            for i in range(9):
                term = plane_ref[i, pl.ds(8 * k, 8), :] * line
                sums[i] = term if k == 0 else sums[i] + term
        for i in range(9):
            parent_ref[i, t] = sums[i]
    def send(g):
        place = keys_ref[g] - P_DEV
        return pltpu.make_async_copy(block_ref.at[g], away_ref.at[place // 2, place % 2], sem.at[g])

    for g in range(P_DEV):

        @pl.when(keys_ref[g] >= P_DEV)
        def _():
            for i in range(9):
                for t in range(4):
                    block_ref[g, i, pl.ds(t, 1), :] = parent_ref[i, t, pl.ds(g, 1), :]
            send(g).start()

    for g in range(P_DEV):

        @pl.when(keys_ref[g] >= P_DEV)
        def _():
            send(g).wait()


def next_kernel(total_ref, next_ref, turn_ref):
    def body(i, carry):
        for j in range(4):
            tile = total_ref[i, j]
            turn_ref[pl.ds(2 * j, 64, stride=8), :] = tile
            turn_ref[pl.ds(2 * j + 1, 64, stride=8), :] = pltpu.roll(tile, 64, 1)
        next_ref[i] = turn_ref[...].T[:64]
        return carry

    lax.fori_loop(0, 9, body, 0)


def parent_kernel(table_ref, groups_ref, arrived_ref, out_ref):
    for p in range(P_DEV):
        holder = table_ref[0, p]
        slot = table_ref[1, p]

        @pl.when(slot < 0)
        def _():
            for i in range(9):
                for t in range(4):
                    out_ref[i, pl.ds(p, 1), pl.ds(128 * t, 128)] = groups_ref[i, t, pl.ds(holder, 1), :]

        @pl.when(slot >= 0)
        def _():
            for i in range(9):
                for t in range(4):
                    out_ref[i, pl.ds(p, 1), pl.ds(128 * t, 128)] = arrived_ref[
                        holder, slot, i, pl.ds(t, 1), :
                    ]


def shape(*dims, dtype=F32):
    return jax.ShapeDtypeStruct(dims, dtype)


VMEM = pl.BlockSpec(memory_space=pltpu.VMEM)
SMEM = pl.BlockSpec(memory_space=pltpu.SMEM)
ANYWHERE = pl.BlockSpec(memory_space=pl.ANY)


def call(kernel, outs, scratch=(), smem=(), anywhere=(), aliases={}, count=0, flops=10**8, traffic=6 * 10**6):
    return pl.pallas_call(
        kernel,
        out_shape=outs,
        in_specs=[SMEM if k in smem else VMEM for k in range(count)],
        out_specs=[ANYWHERE if k in anywhere else VMEM for k in range(len(outs))],
        scratch_shapes=list(scratch),
        input_output_aliases=aliases,
        compiler_params=pltpu.CompilerParams(vmem_limit_bytes=32 * 2**20),
        cost_estimate=pl.CostEstimate(flops=flops, bytes_accessed=traffic, transcendentals=0),
    )


def exchange_pairs():
    along_x = [[(k, (k + 1) % N_CURVE) for k in range(start, N_CURVE, 2)] for start in (0, 1)]
    along_y = [[(k, (k + 1) % N_SEG) for k in range(start, N_SEG, 2)] for start in (0, 1)]
    both = lambda pairs: pairs + [(b, a) for a, b in pairs]
    return [("curve", both(p)) for p in along_x] + [("seg", both(p)) for p in along_y]


def shards(adjoint, material, face_partner, send_faces, migration, children):
    own_seg = lax.axis_index("seg")
    owner, slot, octant = migration[0], migration[1], migration[2]
    key = jnp.where(owner == own_seg, slot, P_DEV + 2 * owner + slot)
    first = octant == 0
    rank = jnp.sum((first[:, None] & (key[:, None] < key[None, :])).astype(jnp.int32), axis=0)
    place = octant * P_DEV + rank
    place = jnp.concatenate([place, place]).reshape(1, 128)
    keys = jnp.sum(
        jnp.where(first[:, None] & (rank[:, None] == jnp.arange(P_DEV)[None, :]), key[:, None], 0), axis=0
    )
    stays = children[0] == own_seg
    group = jnp.sum((keys[:, None] < jnp.arange(P_DEV)[None, :]).astype(jnp.int32), axis=0)
    source = jnp.stack([jnp.where(stays, group, children[0]), jnp.where(stays, -1, children[1])])

    state = shape(9, 4, 64, 128)
    table_y = shape(LOCAL, 256, dtype=BF)
    table = shape(LOCAL, 512, dtype=BF)
    sent = shape(32, 256, dtype=BF)
    face_part = shape(LOCAL, LOCAL)
    payload = [shape(CAP, LOCAL)] * 4
    face_scratch = pltpu.VMEM((LOCAL, LOCAL), F32)
    turn = pltpu.VMEM((NODES, 128), F32)

    zero = jnp.float32(0)
    pack = lax.pad(material[None], zero, ((0, 0, 0), (0, 5, 0), (0, 64, 0))) + lax.pad(
        send_faces, jnp.int32(0), ((0, 0, 0), (3, 1, 0), (0, 128 - CAP, 0))
    ).astype(F32)
    faces = jnp.pad(face_partner.T.astype(F32), ((0, 2), (0, 64)))
    outs = call(
        begin_kernel,
        [state, table_y, table, shape(3, 8, 128), sent, sent] + payload,
        [pltpu.VMEM((3, NODES, 128), F32), pltpu.VMEM((128, 128), F32)],
        count=4,
    )(pack, adjoint[0:3], adjoint[3:6], adjoint[6:9])
    v, ty, t, mat, send_x, send_y = outs[:6]
    out_going = outs[6:]
    pairs = exchange_pairs()
    for step in range(1, 5):
        factor = time_step / step
        order = (1, 0, 3, 2) if step == 3 else (3, 2, 1, 0)
        arrived = [lax.ppermute(out_going[k], *pairs[k]) for k in order]
        if step == 1:
            vol, part, local_y, local, remote_hot = call(
                functools.partial(first_volume_kernel, factor),
                [
                    state,
                    face_part,
                    shape(256, LOCAL, dtype=BF),
                    shape(512, LOCAL, dtype=BF),
                    shape(128, LOCAL, dtype=BF),
                ],
                count=5,
            )(faces, v, ty, t, mat)
            acc = v
        elif step < 4:
            vol, part, acc = call(
                functools.partial(volume_kernel, factor), [state, face_part, state], count=7
            )(v, ty, t, local_y, local, mat, acc)
        else:
            vol, part = call(functools.partial(last_volume_kernel, factor), [state, face_part], count=7)(
                v, ty, t, local_y, local, mat, acc
            )
        if step < 4:
            outs = call(
                functools.partial(finish_kernel, factor, order),
                [state, table_y, table] + payload,
                [face_scratch],
                aliases={0: 0},
                count=10,
            )(vol, part, *arrived, remote_hot, mat, send_x, send_y)
            v, ty, t, out_going = outs[0], outs[1], outs[2], outs[3:]
    wa, wb, lines = (jnp.asarray(x) for x in refine_parts())
    total, groups, away = call(
        functools.partial(end_kernel, factor, order),
        [state, shape(9, 4, P_DEV, 128), shape(N_SEG, 2, 9, 4, 128)],
        [
            face_scratch,
            pltpu.VMEM((9, NODES, 128), F32),
            pltpu.VMEM((9, 64, NODES), F32),
            pltpu.VMEM((9, 128, 256), F32),
            pltpu.VMEM((9, 128, 128), F32),
            pltpu.VMEM((P_DEV, 9, 4, 128), F32),
            pltpu.SemaphoreType.DMA((P_DEV,)),
        ],
        anywhere=(2,),
        smem=(0,),
        aliases={1: 0},
        count=12,
    )(keys, vol, part, *arrived, remote_hot, place, wa, wb, lines)
    fetched = lax.all_to_all(away, "seg", split_axis=0, concat_axis=0, tiled=True)
    updated = call(next_kernel, [shape(9, E_DEV, NODES)], [turn], count=1)(total)[0]
    parents = call(parent_kernel, [shape(9, P_DEV, NODES)], smem=(0,), count=3)(source, groups, fetched)[0]
    return (updated, parents)


def solution(mesh):
    in_specs = (
        P(None, ("curve", "seg"), None),
        P(None, ("curve", "seg")),
        P(("curve", "seg"), None),
        P(("curve", "seg"), None, None),
        P(None, ("curve", "seg")),
        P(None, ("curve", "seg")),
    )
    out_specs = (P(None, ("curve", "seg"), None), P(None, ("curve", "seg"), None))
    return jax.shard_map(shards, mesh=mesh, in_specs=in_specs, out_specs=out_specs, check_vma=False)
```
